32 devices in a mesh: grp: 2 (over x), seq: 4 (over z), mlp: 4 (over y, core).
Axes of the slice: x: 2, y: 2, z: 4, core: 2. Of those that a mesh axis runs over, the one named last changes fastest.
Arguments:
- tokens: bfloat16 [8, 4096, 768], P(('grp', 'mlp'), 'seq'), may hold values from -6 to 6
- step_index: int32 [8, 4], P(('grp', 'mlp')), may hold values from 0 to 1023, as said below
- time_table: bfloat16 [1024, 128], replicated, may hold values from -5 to 5
- ada_weight: bfloat16 [128, 4608], replicated, may hold values from -0.5 to 0.5
- ada_bias: bfloat16 [4608], replicated, may hold values from -3 to 3
- first_gain: bfloat16 [768], replicated, may hold values from 0.099609375 to 1.8984375
- qkv_weight: bfloat16 [768, 2304], replicated, may hold values from -0.21875 to 0.21875
- out_weight: bfloat16 [768, 768], replicated, may hold values from -1.75 to 1.75
- second_gain: bfloat16 [768], replicated, may hold values from 0.099609375 to 1.8984375
- up_weight: bfloat16 [768, 3072], P(None, 'mlp'), may hold values from -0.21875 to 0.21875
- up_bias: bfloat16 [3072], P('mlp'), may hold values from -3 to 3
- down_weight: bfloat16 [3072, 768], P('mlp'), may hold values from -0.109375 to 0.109375
- down_bias: bfloat16 [768], replicated, may hold values from -3 to 3
- cotangent: bfloat16 [8, 4096, 768], P(('grp', 'mlp'), 'seq'), may hold values from -6 to 6
Outputs:
- output: bfloat16 [8, 4096, 768], P(('grp', 'mlp'), 'seq')
- input_grad: float32 [8, 4096, 768], P(('grp', 'mlp'), 'seq')
- table_grad: float32 [1024, 128], P(('seq', 'mlp'))
- ada_weight_grad: float32 [128, 4608], P(None, ('seq', 'mlp'))
- ada_bias_grad: float32 [4608], P(('seq', 'mlp'))
- first_gain_grad: float32 [768], P(('seq', 'mlp'))
- qkv_weight_grad: float32 [768, 2304], P(('seq', 'mlp'))
- out_weight_grad: float32 [768, 768], P(('seq', 'mlp'))
- second_gain_grad: float32 [768], P(('seq', 'mlp'))
- up_weight_grad: float32 [768, 3072], P('seq', 'mlp')
- up_bias_grad: float32 [3072], P(('seq', 'mlp'))
- down_weight_grad: float32 [3072, 768], P('mlp', 'seq')
- down_bias_grad: float32 [768], P(('seq', 'mlp'))
The draws below stay inside these ranges and needn't reach their ends.
Inputs may be any that keep to these rules, and one draw needn't show every extreme that they name: `step_index`: in each line of the second group (the last 4 rows) the four entries are equal.
All inputs are finite; a program needn't handle non-finite values.
Results may differ from the reference program's by a relative error of at most 0.014.
The reference program's roundings to bfloat16 on the way count: a program that leaves them out, or rounds other values in their place, can miss the bound.
Values may be sent and summed in bfloat16 or wider, within the bound.
A program may use at most 384 MiB of HBM per device.

```python
import functools
import math
import jax
import jax.numpy as jnp
from jax import lax

D = 768
H = 12
HD = 64
FF = 3072
COND = 128
STEPS = 1024
LONG = 4096
LINES = 8


def draw_step_index(key, part):
    key_draw, key_high, key_low = jax.random.split(key, 3)
    drawn_steps = jax.random.randint(key_draw, (LINES, 4), 0, STEPS, dtype=jnp.int32)
    row_index = jnp.arange(LINES, dtype=jnp.int32)[:, None]
    col_index = jnp.arange(4, dtype=jnp.int32)[None, :]
    shared = jnp.where(row_index >= LINES // 2, drawn_steps[:, :1], drawn_steps)
    column_high = jax.random.randint(key_high, (), 0, 4, dtype=jnp.int32)
    column_low = jax.random.randint(key_low, (), 0, 4, dtype=jnp.int32)
    shared = jnp.where((row_index == 0) & (col_index == column_high), STEPS - 1, shared)
    shared = jnp.where((row_index == LINES // 2 - 1) & (col_index == column_low), 0, shared)
    return shared.astype(jnp.int32)


def block_scale(stream_key, extent, shards, low, high):
    def one(dim, blocks):
        draws = jax.random.uniform(jax.random.fold_in(jax.random.fold_in(stream_key, 6), dim), (blocks,), jnp.float32, low / len(shards), high / len(shards))
        return jnp.repeat(jnp.exp(draws), extent[dim] // blocks).reshape((-1,) + (1,) * (len(extent) - dim - 1))

    gain = one(*shards[0])
    for cut in shards[1:]:
        gain = gain * one(*cut)
    return gain


def bell_draw(key, dims, scale, limit, cuts=(), kind=jnp.bfloat16):
    values = jax.random.normal(key, dims, jnp.float32) * scale
    if len(cuts) > 0:
        values = block_scale(key, dims, cuts, -0.22, 0.18) * values
    return jnp.clip(values, min=-limit, max=limit).astype(kind)


def setup_inputs(seed: int = 0) -> dict:
    key_list = jax.random.split(jax.random.key(seed), 15)
    return {
        "tokens": bell_draw(key_list[0], (LINES, LONG, D), 1.0, 6.0, ((0, 8), (1, 4))),
        "step_index": draw_step_index(jax.random.fold_in(key_list[14], 71), 0),
        "time_table": bell_draw(key_list[2], (STEPS, COND), 1.0, 5.0),
        "ada_weight": bell_draw(key_list[3], (COND, 6 * D), COND ** -0.5, 0.5),
        "ada_bias": bell_draw(key_list[4], (6 * D,), 0.5, 3.0),
        "first_gain": jnp.clip(1.0 + 0.18 * jax.random.normal(key_list[5], (D,), jnp.float32), 0.099609375, 1.8984375).astype(jnp.bfloat16),
        "qkv_weight": bell_draw(key_list[6], (D, 3 * D), D ** -0.5, 0.21875),
        "out_weight": bell_draw(key_list[7], (D, D), (max(D // 64, 1)) ** -0.5, 1.75),
        "second_gain": jnp.clip(1.0 + 0.18 * jax.random.normal(key_list[8], (D,), jnp.float32), 0.099609375, 1.8984375).astype(jnp.bfloat16),
        "up_weight": bell_draw(key_list[9], (D, FF), D ** -0.5, 0.21875, ((1, 4),)),
        "up_bias": bell_draw(key_list[10], (FF,), 0.5, 3.0, ((0, 4),)),
        "down_weight": bell_draw(key_list[11], (FF, D), FF ** -0.5, 0.109375, ((0, 4),)),
        "down_bias": bell_draw(key_list[12], (D,), 0.5, 3.0),
        "cotangent": bell_draw(key_list[13], (LINES, LONG, D), 1.0, 6.0, ((0, 8), (1, 4))),
    }


@jax.custom_vjp
def low(v):
    return lax.optimization_barrier(v.astype(jnp.bfloat16)).astype(jnp.float32)

@jax.custom_vjp
def low_back(v):
    return v

def low_keep(v):
    return (low(v), None)

def low_pass(kept, grad):
    return (grad,)

def back_keep(v):
    return (v, None)

def back_low(kept, grad):
    return (low(grad),)
low.defvjp(low_keep, low_pass)
low_back.defvjp(back_keep, back_low)
highest = lax.Precision.HIGHEST

def product(left, right):
    return jnp.dot(left, right, precision=highest)

def layer_norm(values, norm_gain):
    centred = values - lax.optimization_barrier(jnp.mean(values, axis=-1, keepdims=True))
    spread = lax.optimization_barrier(jnp.mean(centred * centred, axis=-1, keepdims=True))
    return centred * lax.rsqrt(spread + 1e-05) * norm_gain

def rotate_pairs(values, positions):
    half_dim = HD // 2
    frequency = jnp.exp(jnp.arange(half_dim, dtype=jnp.float32) * (-2.0 * math.log(10000.0) / HD))
    angles = positions.astype(jnp.float32)[:, None] * frequency[None, :]
    cosine = jnp.cos(angles)[:, None, :]
    sine_part = jnp.sin(angles)[:, None, :]
    leading = values[..., :half_dim]
    trailing = values[..., half_dim:]
    return jnp.concatenate([leading * cosine - trailing * sine_part, trailing * cosine + leading * sine_part], axis=-1)

def attend(triple):
    queries, key_rows, value_rows = triple
    length = queries.shape[0]
    block_rows = min(length, 512)
    blocks = queries.reshape(length // block_rows, block_rows, H, HD)

    def one_block(query_block):
        scores = jnp.einsum('qhd,khd->hqk', query_block, key_rows, precision=highest) * (1.0 / math.sqrt(HD))
        scores = low_back(scores)
        weights = jax.nn.softmax(scores, axis=-1)
        return jnp.einsum('hqk,khd->qhd', low(weights), value_rows, precision=highest)
    return lax.map(jax.checkpoint(one_block), blocks).reshape(length, H * HD)

def line_forward(seq_length, params, line_tokens, line_steps):
    time_table, ada_weight, ada_bias, first_gain, qkv_weight, out_weight, second_gain, up_weight, up_bias, down_weight, down_bias = params
    condition = jax.nn.silu(time_table[line_steps])
    modulation = product(low(condition), ada_weight) + ada_bias
    per_token = jnp.repeat(modulation, LONG // 4, axis=0)
    shift_one, scale_one, gate_one, shift_two, scale_two, gate_two = jnp.split(per_token, 6, axis=1)
    positions = jnp.arange(LONG, dtype=jnp.int32) % seq_length
    normed = low(layer_norm(line_tokens, first_gain) * (1.0 + scale_one) + shift_one)
    mixed_rows = low_back(product(normed, qkv_weight))
    queries = low(rotate_pairs(mixed_rows[:, :D].reshape(LONG, H, HD), positions))
    key_rows = low(rotate_pairs(mixed_rows[:, D:2 * D].reshape(LONG, H, HD), positions))
    value_rows = low(mixed_rows[:, 2 * D:].reshape(LONG, H, HD))
    seq_total = LONG // seq_length
    shaped = (queries.reshape(seq_total, seq_length, H, HD), key_rows.reshape(seq_total, seq_length, H, HD), value_rows.reshape(seq_total, seq_length, H, HD))
    attended = lax.map(attend, shaped).reshape(LONG, D)
    attended = low(low_back(attended))
    branch = low_back(product(attended, out_weight))
    middle = line_tokens + gate_one * branch
    hidden = low(layer_norm(middle, second_gain) * (1.0 + scale_two) + shift_two)
    pre_act = low_back(product(hidden, up_weight) + up_bias)
    activated = low(jax.nn.gelu(pre_act, approximate=True))
    feed_out = low_back(product(activated, down_weight) + down_bias)
    return middle + gate_two * feed_out

def reference(tokens, step_index, time_table, ada_weight, ada_bias, first_gain, qkv_weight, out_weight, second_gain, up_weight, up_bias, down_weight, down_bias, cotangent):
    params = tuple((argument.astype(jnp.float32) for argument in (time_table, ada_weight, ada_bias, first_gain, qkv_weight, out_weight, second_gain, up_weight, up_bias, down_weight, down_bias)))
    inputs = tokens.astype(jnp.float32)

    def forward(weights, line_inputs):
        outputs = []
        for line_number in range(LINES):
            seq_length = LONG // 4 if line_number < LINES // 2 else LONG
            line_fn = jax.checkpoint(functools.partial(line_forward, seq_length))
            outputs.append(line_fn(weights, line_inputs[line_number], step_index[line_number]))
        return jnp.stack(outputs)
    result, pullback = jax.vjp(forward, params, inputs)
    weight_grads, input_grad = pullback(cotangent.astype(jnp.float32))
    return (result.astype(jnp.bfloat16), input_grad, weight_grads[0], weight_grads[1], weight_grads[2], weight_grads[3], weight_grads[4], weight_grads[5], weight_grads[6], weight_grads[7], weight_grads[8], weight_grads[9], weight_grads[10])
```

```python
import math

import jax
import jax.numpy as jnp
from jax import lax
from jax.experimental import pallas as pl
from jax.experimental.pallas import tpu as pltpu
from jax.sharding import PartitionSpec as P

HD = 64


highest = lax.Precision.HIGHEST


def shifted(value, axis, steps):
    count = lax.axis_size(axis)
    pairs = [(source, (source + steps) % count) for source in range(count)]
    return lax.ppermute(value, axis, pairs)


def layer_norm(values, norm_gain):
    centred = values - jnp.mean(values, axis=-1, keepdims=True)
    spread = jnp.mean(centred * centred, axis=-1, keepdims=True)
    return centred * lax.rsqrt(spread + 1e-05) * norm_gain


def modulate(values, norm_gain, shift_part, scale_part):
    return layer_norm(values, norm_gain) * (1.0 + scale_part) + shift_part


def gelu_tanh(values):
    return jax.nn.gelu(values, approximate=True)


def rotate_pairs(values, positions):
    half_dim = HD // 2
    frequency = jnp.exp(jnp.arange(half_dim, dtype=jnp.float32) * (-2.0 * math.log(10000.0) / HD))
    angles = positions.astype(jnp.float32)[:, None] * frequency[None, :]
    cosine = jnp.cos(angles)[:, None, :]
    sine_part = jnp.sin(angles)[:, None, :]
    leading = values[..., :half_dim]
    trailing = values[..., half_dim:]
    return jnp.concatenate(
        [leading * cosine - trailing * sine_part, trailing * cosine + leading * sine_part], axis=-1
    )


def shards(
    tokens,
    step_index,
    time_table,
    ada_weight,
    ada_bias,
    first_gain,
    qkv_weight,
    out_weight,
    second_gain,
    up_weight,
    up_bias,
    down_weight,
    down_bias,
    cotangent,
):
    seq_count = lax.axis_size("seq")
    seq_place = lax.axis_index("seq")
    group_index = lax.axis_index("grp")
    mlp_place = lax.axis_index("mlp")
    tok_rows = tokens.shape[1]
    model_width = tokens.shape[2]
    head_count = model_width // HD
    score_scale = 1.0 / math.sqrt(HD)
    line_len = tok_rows * seq_count
    seq_length = jnp.where(group_index == 0, line_len // 4, line_len).astype(jnp.int32)
    row_ids = jnp.arange(tok_rows, dtype=jnp.int32)
    own_pos = seq_place * tok_rows + row_ids
    positions = own_pos % seq_length
    quarter = seq_place // (seq_count // 4)
    step_value = jnp.sum(jnp.where(jnp.arange(4, dtype=jnp.int32) == quarter, step_index[0], 0))
    table_pick = jnp.arange(time_table.shape[0], dtype=jnp.int32) == step_value
    embedded = jnp.dot(
        table_pick.astype(jnp.bfloat16)[None, :], time_table, preferred_element_type=jnp.float32
    )[0]
    condition, silu_back = jax.vjp(jax.nn.silu, embedded)
    cond_low = condition.astype(jnp.bfloat16)
    modulation = jnp.dot(cond_low[None, :], ada_weight, preferred_element_type=jnp.float32)[
        0
    ] + ada_bias.astype(jnp.float32)
    shift_one, scale_one, gate_one, shift_two, scale_two, gate_two = jnp.split(modulation, 6)
    inputs = tokens[0].astype(jnp.float32)
    normed, first_back = jax.vjp(
        modulate, inputs, first_gain.astype(jnp.float32), shift_one, scale_one
    )
    normed_low = normed.astype(jnp.bfloat16)
    mixed_rows = jnp.dot(normed_low, qkv_weight, preferred_element_type=jnp.float32)

    def rotate_all(mixed_in):
        query_part = rotate_pairs(
            mixed_in[:, :model_width].reshape(tok_rows, head_count, HD), positions
        )
        key_part = rotate_pairs(
            mixed_in[:, model_width : 2 * model_width].reshape(tok_rows, head_count, HD), positions
        )
        return (
            query_part,
            key_part,
            mixed_in[:, 2 * model_width :].reshape(tok_rows, head_count, HD),
        )

    rotated, rotate_back = jax.vjp(rotate_all, mixed_rows)
    queries = rotated[0].astype(jnp.bfloat16)
    key_rows = rotated[1].astype(jnp.bfloat16)
    value_rows = rotated[2].astype(jnp.bfloat16)
    start_state = (
        jnp.full((head_count, tok_rows), -1e30, jnp.float32),
        jnp.zeros((head_count, tok_rows), jnp.float32),
        jnp.zeros((head_count, tok_rows, HD), jnp.float32),
    )
    key_piece = lax.all_gather(key_rows.reshape(tok_rows, model_width), "seq", axis=0, tiled=True)
    value_piece = lax.all_gather(
        value_rows.reshape(tok_rows, model_width), "seq", axis=0, tiled=True
    )
    piece_rows = key_piece.shape[0]
    sub_rows = math.gcd(piece_rows, 512)

    def one_block(block_index, block_state):
        run_max, run_total, run_acc = block_state
        offset = block_index * sub_rows
        key_block = lax.dynamic_slice_in_dim(key_piece, offset, sub_rows, 0).reshape(
            sub_rows, head_count, HD
        )
        value_block = lax.dynamic_slice_in_dim(value_piece, offset, sub_rows, 0).reshape(
            sub_rows, head_count, HD
        )
        key_pos = offset + jnp.arange(sub_rows, dtype=jnp.int32)
        same_seq = (own_pos // seq_length)[:, None] == (key_pos // seq_length)[None, :]
        scores = (
            jnp.einsum("qhd,khd->hqk", queries, key_block, preferred_element_type=jnp.float32)
            * score_scale
        )
        masked = jnp.where(same_seq[None], scores, -1e30)
        new_max = jnp.maximum(run_max, jnp.max(masked, axis=-1))
        shrink = jnp.exp(run_max - new_max)
        weights = jnp.where(same_seq[None], jnp.exp(masked - new_max[..., None]), 0.0)
        run_total = run_total * shrink + jnp.sum(weights, axis=-1)
        run_acc = run_acc * shrink[..., None] + jnp.einsum(
            "hqk,khd->hqd",
            weights.astype(jnp.bfloat16),
            value_block,
            preferred_element_type=jnp.float32,
        )
        return (new_max, run_total, run_acc)

    run_max, run_total, run_acc = lax.fori_loop(0, piece_rows // sub_rows, one_block, start_state)
    log_total = run_max + jnp.log(run_total)
    attended3 = jnp.transpose(run_acc / run_total[..., None], (1, 0, 2))
    attended_low = attended3.reshape(tok_rows, model_width).astype(jnp.bfloat16)
    branch = jnp.dot(attended_low, out_weight, preferred_element_type=jnp.float32)
    middle = inputs + gate_one * branch
    hidden, second_back = jax.vjp(
        modulate, middle, second_gain.astype(jnp.float32), shift_two, scale_two
    )
    hidden_low = hidden.astype(jnp.bfloat16)
    gathered = lax.all_gather(hidden_low, "mlp", axis=0, tiled=True)
    pre_act = jnp.dot(gathered, up_weight, preferred_element_type=jnp.float32) + up_bias.astype(
        jnp.float32
    )
    activated, gelu_back = jax.vjp(gelu_tanh, pre_act)
    act_low = activated.astype(jnp.bfloat16)
    feed_terms = jnp.dot(act_low, down_weight, preferred_element_type=jnp.float32)
    feed_out = lax.psum_scatter(
        feed_terms, "mlp", scatter_dimension=0, tiled=True
    ) + down_bias.astype(jnp.float32)
    output = (middle + gate_two * feed_out).astype(jnp.bfloat16)[None]
    grad_out = cotangent[0].astype(jnp.float32)
    gate_two_grad = jnp.sum(grad_out * feed_out, axis=0)
    grad_feed = (gate_two * grad_out).astype(jnp.bfloat16)
    down_bias_grad = jnp.sum(grad_feed, axis=0, dtype=jnp.float32)
    grad_rows = lax.all_gather(grad_feed, "mlp", axis=0, tiled=True)
    down_grad = jnp.einsum("tf,td->fd", act_low, grad_rows, preferred_element_type=jnp.float32)
    grad_act = jnp.einsum("td,fd->tf", grad_rows, down_weight, preferred_element_type=jnp.float32)
    grad_pre = gelu_back(grad_act)[0].astype(jnp.bfloat16)
    up_grad = jnp.einsum("td,tf->df", gathered, grad_pre, preferred_element_type=jnp.float32)
    local_units = up_weight.shape[1]
    bias_slot = lax.dynamic_update_slice_in_dim(
        jnp.zeros((local_units * lax.axis_size("mlp"),), jnp.float32),
        jnp.sum(grad_pre, axis=0, dtype=jnp.float32),
        mlp_place * local_units,
        0,
    )
    hidden_terms = jnp.einsum("tf,df->td", grad_pre, up_weight, preferred_element_type=jnp.float32)
    grad_hidden = lax.psum_scatter(hidden_terms, "mlp", scatter_dimension=0, tiled=True)
    middle_part, second_gain_grad, shift_two_grad, scale_two_grad = second_back(grad_hidden)
    middle_grad = grad_out + middle_part
    gate_one_grad = jnp.sum(middle_grad * branch, axis=0)
    grad_branch = (gate_one * middle_grad).astype(jnp.bfloat16)
    out_grad = jnp.einsum(
        "td,te->de", attended_low, grad_branch, preferred_element_type=jnp.float32
    )
    grad_attended = jnp.einsum(
        "te,de->td", grad_branch, out_weight, preferred_element_type=jnp.float32
    ).astype(jnp.bfloat16)
    grad_heads = grad_attended.reshape(tok_rows, head_count, HD)
    row_delta = jnp.transpose(jnp.sum(grad_heads.astype(jnp.float32) * attended3, axis=-1))

    def pair_grads(
        query_set, grad_set, total_set, delta_set, query_anchor, key_set, value_set, key_anchor
    ):
        query_pos = query_anchor * tok_rows + row_ids
        key_pos = key_anchor * tok_rows + row_ids
        same_seq = (query_pos // seq_length)[:, None] == (key_pos // seq_length)[None, :]
        scores = (
            jnp.einsum("qhd,khd->hqk", query_set, key_set, preferred_element_type=jnp.float32)
            * score_scale
        )
        prob_rows = jnp.where(same_seq[None], jnp.exp(scores - total_set[..., None]), 0.0)
        value_part = jnp.einsum(
            "hqk,qhd->khd",
            prob_rows.astype(jnp.bfloat16),
            grad_set,
            preferred_element_type=jnp.float32,
        )
        prob_grad = jnp.einsum(
            "qhd,khd->hqk", grad_set, value_set, preferred_element_type=jnp.float32
        )
        score_grad = (prob_rows * (prob_grad - delta_set[..., None])).astype(jnp.bfloat16)
        query_part = (
            jnp.einsum("hqk,khd->qhd", score_grad, key_set, preferred_element_type=jnp.float32)
            * score_scale
        )
        key_part = (
            jnp.einsum("hqk,qhd->khd", score_grad, query_set, preferred_element_type=jnp.float32)
            * score_scale
        )
        return (query_part, key_part, value_part)

    zero_heads = jnp.zeros((tok_rows, head_count, HD), jnp.float32)

    def key_turn(running):
        key_set, value_set, key_acc, value_acc, anchor, query_acc = running
        query_part, key_part, value_part = pair_grads(
            queries, grad_heads, log_total, row_delta, seq_place, key_set, value_set, anchor
        )
        moved_rows = shifted((key_set, value_set), "seq", 1)
        moved_grads = shifted((key_acc + key_part, value_acc + value_part), "seq", 1)
        return (
            moved_rows[0],
            moved_rows[1],
            moved_grads[0],
            moved_grads[1],
            (anchor - 1) % seq_count,
            query_acc + query_part,
        )

    def two_key_turns(turn_index, running):
        return key_turn(key_turn(running))

    finished = lax.fori_loop(
        0,
        seq_count // 2,
        two_key_turns,
        (key_rows, value_rows, zero_heads, zero_heads, seq_place, zero_heads),
    )
    query_grad, key_grad, value_grad = (finished[5], finished[2], finished[3])
    mixed_grad = rotate_back((query_grad, key_grad, value_grad))[0].astype(jnp.bfloat16)
    qkv_grad = jnp.einsum("td,te->de", normed_low, mixed_grad, preferred_element_type=jnp.float32)
    grad_normed = jnp.einsum(
        "te,de->td", mixed_grad, qkv_weight, preferred_element_type=jnp.float32
    )
    input_part, first_gain_grad, shift_one_grad, scale_one_grad = first_back(grad_normed)
    input_grad = (middle_grad + input_part)[None]
    mod_grad = jnp.concatenate(
        [
            shift_one_grad,
            scale_one_grad,
            gate_one_grad,
            shift_two_grad,
            scale_two_grad,
            gate_two_grad,
        ]
    )
    ada_grad = cond_low.astype(jnp.float32)[:, None] * mod_grad[None, :]
    cond_grad = jnp.dot(ada_weight.astype(jnp.float32), mod_grad, precision=highest)
    table_local = table_pick.astype(jnp.float32)[:, None] * silu_back(cond_grad)[0][None, :]
    layer_sums = (
        lax.psum_scatter(table_local, ("seq", "mlp"), scatter_dimension=0, tiled=True),
        lax.psum_scatter(ada_grad, ("seq", "mlp"), scatter_dimension=1, tiled=True),
        lax.psum_scatter(mod_grad, ("seq", "mlp"), scatter_dimension=0, tiled=True),
        lax.psum_scatter(first_gain_grad, ("seq", "mlp"), scatter_dimension=0, tiled=True),
        lax.psum_scatter(qkv_grad, ("seq", "mlp"), scatter_dimension=0, tiled=True),
        lax.psum_scatter(out_grad, ("seq", "mlp"), scatter_dimension=0, tiled=True),
        lax.psum_scatter(second_gain_grad, ("seq", "mlp"), scatter_dimension=0, tiled=True),
        lax.psum_scatter(bias_slot, ("seq", "mlp"), scatter_dimension=0, tiled=True),
        lax.psum_scatter(down_bias_grad, ("seq", "mlp"), scatter_dimension=0, tiled=True),
    )
    feed_summed = (
        lax.psum_scatter(up_grad, "seq", scatter_dimension=0, tiled=True),
        lax.psum_scatter(down_grad, "seq", scatter_dimension=1, tiled=True),
    )
    totals = lax.psum(
        (
            layer_sums[0],
            layer_sums[1],
            layer_sums[2],
            layer_sums[3],
            layer_sums[4],
            layer_sums[5],
            layer_sums[6],
            layer_sums[7],
            layer_sums[8],
            feed_summed[0],
            feed_summed[1],
        ),
        "grp",
    )
    return (
        output,
        input_grad,
        totals[0],
        totals[1],
        totals[2],
        totals[3],
        totals[4],
        totals[5],
        totals[6],
        totals[9],
        totals[7],
        totals[10],
        totals[8],
    )


LOG_SCALE = math.log2(math.e) / math.sqrt(HD)
NT = (((1,), (1,)), ((), ()))
TN = (((0,), (0,)), ((), ()))
F32 = jnp.float32
BF16 = jnp.bfloat16
WHOLE_VMEM = 60 * 1024 * 1024


def params(*semantics):
    return pltpu.CompilerParams(vmem_limit_bytes=WHOLE_VMEM, dimension_semantics=semantics)


def low_lanes(value):
    return lax.broadcasted_iota(jnp.int32, value.shape, 1) < HD


def swap_heads(value):
    return pltpu.roll(value, HD, 1)


def exchange(top, bottom):
    keep = low_lanes(top)
    return (
        jnp.where(keep, top, swap_heads(bottom)),
        jnp.where(keep, swap_heads(top), bottom),
    )


def fold(value):
    half = value.shape[0] // 2
    top = value[:half]
    return jnp.where(low_lanes(top), top, swap_heads(value[half:]))


def unfold_into(target, base, packed, fill):
    half = packed.shape[0]
    value = packed.astype(F32)
    keep = low_lanes(value)
    target[base : base + half, :] = jnp.where(keep, value, fill).astype(BF16)
    target[base + half : base + 2 * half, :] = jnp.where(keep, swap_heads(value), fill).astype(BF16)


def turn(value, cosine, sine):
    lane = lax.broadcasted_iota(jnp.int32, value.shape, 1) % HD
    quarter = HD // 2
    other = jnp.where(
        lane < quarter, pltpu.roll(value, 2 * HD - quarter, 1), pltpu.roll(value, quarter, 1)
    )
    return value * cosine + other * sine


def normalise(values):
    centred = values - jnp.mean(values, axis=-1, keepdims=True)
    spread = jnp.mean(centred * centred, axis=-1, keepdims=True)
    inverse = lax.rsqrt(spread + 1e-05)
    return centred * inverse, inverse


def project_kernel(x_ref, vec_ref, w_ref, cos_ref, sin_ref, normed_ref, pack_ref):
    rows = x_ref.shape[1]
    width = x_ref.shape[2]
    x = x_ref[...].reshape(2 * rows, width).astype(F32)
    n, _ = normalise(x)
    normed = n * vec_ref[0:1, :] * (1.0 + vec_ref[1:2, :]) + vec_ref[2:3, :]
    normed = normed.astype(BF16)
    normed_ref[...] = normed.reshape(2, rows, width)
    cosine = cos_ref[...].reshape(2 * rows, 2 * HD)
    sine = sin_ref[...].reshape(2 * rows, 2 * HD)
    for part in range(3):
        mixed = jnp.dot(
            normed, w_ref[:, part * width : (part + 1) * width], preferred_element_type=F32
        )
        for pair in range(width // (2 * HD)):
            value = mixed[:, pair * 2 * HD : (pair + 1) * 2 * HD]
            if part < 2:
                value = turn(value, cosine, sine)
            even, odd = exchange(value[:rows], value[rows:])
            pack_ref[2 * pair, part] = even.astype(BF16)
            pack_ref[2 * pair + 1, part] = odd.astype(BF16)


def project(x2, vecs, weight, cosine, sine, rows=256):
    half, width = x2.shape[1:]
    heads = width // HD
    tok = lambda last: pl.BlockSpec((2, rows, last), lambda i: (0, i, 0))
    return pl.pallas_call(
        project_kernel,
        grid=(half // rows,),
        in_specs=[
            tok(width),
            pl.BlockSpec(vecs.shape, lambda i: (0, 0)),
            pl.BlockSpec(weight.shape, lambda i: (0, 0)),
            tok(2 * HD),
            tok(2 * HD),
        ],
        out_specs=[tok(width), pl.BlockSpec((heads, 3, rows, 2 * HD), lambda i: (0, 0, i, 0))],
        out_shape=[
            jax.ShapeDtypeStruct((2, half, width), BF16),
            jax.ShapeDtypeStruct((heads, 3, half, 2 * HD), BF16),
        ],
        compiler_params=params("arbitrary"),
        name="project",
    )(x2, vecs, weight, cosine, sine)


def attend_rows(q, k_ref, v_ref, keys, out_put, log_put, block=512):
    top = None
    for start in range(0, keys, block):
        s = lax.dot_general(q, k_ref[start : start + block, :], NT, preferred_element_type=F32)
        s = s * LOG_SCALE
        peak = jnp.max(s, axis=1, keepdims=True)
        new_top = peak if top is None else jnp.maximum(top, peak)
        p = jnp.exp2(s - new_top).astype(BF16)
        part = jnp.dot(p, v_ref[start : start + block, :], preferred_element_type=F32)
        acc = part if top is None else acc * jnp.exp2(top - new_top) + part
        top = new_top
    out_put(fold(acc / swap_heads(acc)).astype(BF16))
    log_put((top + jnp.log2(acc)).T[HD : HD + 8])


def load_forward(source, base, q_s, k_s, v_s):
    unfold_into(q_s, base, source[0], 0.0)
    unfold_into(k_s, base, source[1], 0.0)
    unfold_into(v_s, base, source[2], 1.0)


def full_step(step, pieces, o_ref, log_ref, q_s, k_s, v_s):
    piece_rows = 2 * pieces[0].shape[1]
    total = piece_rows * len(pieces)

    @pl.when(step == 0)
    def _():
        for place, piece in enumerate(pieces):
            load_forward(piece, place * piece_rows, q_s, k_s, v_s)

    def put_out(value):
        o_ref[step] = value

    def put_log(value):
        log_ref[step] = value

    q = q_s[pl.ds(pl.multiple_of(step * piece_rows, piece_rows), piece_rows), :]
    attend_rows(q, k_s, v_s, total, put_out, put_log)


def forward_second_kernel(p0, p1, p2, p3, o_ref, log_ref, q_s, k_s, v_s):
    full_step(pl.program_id(0), (p0, p1, p2, p3), o_ref, log_ref, q_s, k_s, v_s)


def forward_first_kernel(
    group_ref, pack_ref, p0, p1, p2, p3, o_ref, log_ref, ol_ref, logl_ref, q_s, k_s, v_s
):
    step = pl.program_id(0)
    group = group_ref[0]

    @pl.when(group == 0)
    def _():
        rows = 2 * p0.shape[1]
        load_forward(pack_ref.at[0], 0, q_s, k_s, v_s)

        def put_out(value):
            ol_ref[step] = value

        def put_log(value):
            logl_ref[step] = value

        attend_rows(q_s[0:rows, :], k_s, v_s, rows, put_out, put_log)

    @pl.when((group == 1) & (step < 4))
    def _():
        full_step(step, (p0, p1, p2, p3), o_ref, log_ref, q_s, k_s, v_s)


def whole(shape):
    zeros = (0,) * len(shape)
    return pl.BlockSpec(shape, lambda *_: zeros)


def forward_scratch(half):
    return [pltpu.VMEM((8 * half, 2 * HD), BF16)] * 3


def forward_first(group, packs, pieces):
    heads, _, half, lanes = packs.shape
    o4, l4 = (4, half, lanes), (4, 8, 2 * half)
    o12, l12 = (heads, half, lanes), (heads, 8, 2 * half)
    shapes = [(o4, BF16), (l4, F32), (o12, BF16), (l12, F32)]
    return pl.pallas_call(
        forward_first_kernel,
        grid_spec=pltpu.PrefetchScalarGridSpec(
            num_scalar_prefetch=1,
            grid=(heads,),
            in_specs=[pl.BlockSpec((1, 3, half, lanes), lambda i, g: (i * (1 - g[0]), 0, 0, 0))]
            + [whole(pieces[0].shape)] * 4,
            out_specs=[whole(shape) for shape, _ in shapes],
            scratch_shapes=forward_scratch(half),
        ),
        out_shape=[jax.ShapeDtypeStruct(shape, kind) for shape, kind in shapes],
        compiler_params=params("arbitrary"),
        cost_estimate=pl.CostEstimate(
            flops=40_000_000_000, bytes_accessed=8_000_000, transcendentals=0
        ),
        name="forward_first",
    )(group, packs, *pieces)


def forward_second(pieces):
    _, half, lanes = pieces[0].shape
    shapes = [((4, half, lanes), BF16), ((4, 8, 2 * half), F32)]
    return pl.pallas_call(
        forward_second_kernel,
        grid=(4,),
        in_specs=[whole(pieces[0].shape)] * 4,
        out_specs=[whole(shape) for shape, _ in shapes],
        out_shape=[jax.ShapeDtypeStruct(shape, kind) for shape, kind in shapes],
        scratch_shapes=forward_scratch(half),
        compiler_params=params("arbitrary"),
        cost_estimate=pl.CostEstimate(
            flops=40_000_000_000, bytes_accessed=8_000_000, transcendentals=0
        ),
        name="forward_second",
    )(*pieces)


def tile_grads(q, do, k, v, log_row, delta_row):
    s = lax.dot_general(k, q, NT, preferred_element_type=F32)
    p = jnp.exp2(s * LOG_SCALE - log_row)
    dp = lax.dot_general(v, do, NT, preferred_element_type=F32)
    ds = (p * (dp - delta_row)).astype(BF16)
    dv = jnp.dot(p.astype(BF16), do, preferred_element_type=F32)
    dk = jnp.dot(ds, q, preferred_element_type=F32)
    dq = lax.dot_general(k, ds, TN, preferred_element_type=F32)
    return dq, dk, dv


def load_backward(source, do, o, base, q_s, k_s, v_s, do_s, delta_s):
    half = do.shape[0]
    unfold_into(q_s, base, source[0], 0.0)
    unfold_into(k_s, base, source[1], 0.0)
    unfold_into(v_s, base, source[2], 0.0)
    unfold_into(do_s, base, do, 0.0)
    product = (do.astype(F32) * o.astype(F32)).T
    first = jnp.sum(product[:HD], axis=0, keepdims=True)
    second = jnp.sum(product[HD:], axis=0, keepdims=True)
    delta_s[:, base : base + half] = jnp.broadcast_to(first, (8, half))
    delta_s[:, base + half : base + 2 * half] = jnp.broadcast_to(second, (8, half))


def full_back_step(step, piece_rows, log_ref, put, q_s, k_s, v_s, do_s, delta_s, dq_s):
    scale = 1.0 / math.sqrt(HD)
    block = pl.ds(pl.multiple_of(step * piece_rows, piece_rows), piece_rows)
    k = k_s[block, :]
    v = v_s[block, :]
    dk = dv = None
    parts = []
    for place in range(4):
        rows = slice(place * piece_rows, (place + 1) * piece_rows)
        dq, dk_part, dv_part = tile_grads(
            q_s[rows, :], do_s[rows, :], k, v, log_ref[place, 0:1, :], delta_s[0:1, rows]
        )
        dk = dk_part if dk is None else dk + dk_part
        dv = dv_part if dv is None else dv + dv_part
        dq_s[:, rows] = jnp.where(step == 0, dq, dq_s[:, rows] + dq)
    put(step, 1, fold(dk * scale).astype(BF16))
    put(step, 2, fold(dv).astype(BF16))

    @pl.when(step == 3)
    def _():
        for place in range(4):
            rows = slice(place * piece_rows, (place + 1) * piece_rows)
            put(place, 0, fold(dq_s[:, rows].T * scale).astype(BF16))


def backward_first_kernel(
    group_ref, a0, a1, a2, a3, b0, b1, b2, b3, d0, d1, d2, d3,
    oa_ref, ob_ref, la_ref, lb_ref, grad_ref, q_s, k_s, v_s, do_s, delta_s, dq_s, log_s,
):
    step = pl.program_id(0)
    group = group_ref[0]
    piece_rows = 2 * a0.shape[1]
    dos = (d0, d1, d2, d3)
    for value, pieces, o_ref, l_ref in (
        (1, (a0, a1, a2, a3), oa_ref, la_ref),
        (0, (b0, b1, b2, b3), ob_ref, lb_ref),
    ):

        @pl.when((step == 0) & (group == value))
        def _(pieces=pieces, o_ref=o_ref, l_ref=l_ref):
            for place in range(4):
                load_backward(
                    pieces[place], dos[place][...], o_ref[place], place * piece_rows,
                    q_s, k_s, v_s, do_s, delta_s,
                )
            log_s[...] = l_ref[...]

    def put(place, part, value):
        grad_ref[place, part] = value

    full_back_step(step, piece_rows, log_s, put, q_s, k_s, v_s, do_s, delta_s, dq_s)


def backward_second_kernel(
    group_ref, pack_ref, dol_ref, ol_ref, ll_ref, b0, b1, b2, b3, d0, d1, d2, d3,
    o_ref, l_ref, grad_ref, gradl_ref, q_s, k_s, v_s, do_s, delta_s, dq_s,
):
    step = pl.program_id(0)
    group = group_ref[0]
    piece_rows = 2 * b0.shape[1]
    scale = 1.0 / math.sqrt(HD)

    @pl.when(group == 0)
    def _():
        load_backward(
            pack_ref.at[0], dol_ref[0], ol_ref[0], 0, q_s, k_s, v_s, do_s, delta_s
        )
        rows = slice(0, piece_rows)
        dq, dk, dv = tile_grads(
            q_s[rows, :], do_s[rows, :], k_s[rows, :], v_s[rows, :],
            ll_ref[0, 0:1, :], delta_s[0:1, rows],
        )
        gradl_ref[step, 0] = fold(dq.T * scale).astype(BF16)
        gradl_ref[step, 1] = fold(dk * scale).astype(BF16)
        gradl_ref[step, 2] = fold(dv).astype(BF16)

    @pl.when((group == 1) & (step < 4))
    def _():
        @pl.when(step == 0)
        def _():
            for place, (piece, do) in enumerate(((b0, d0), (b1, d1), (b2, d2), (b3, d3))):
                load_backward(
                    piece, do[...], o_ref[place], place * piece_rows,
                    q_s, k_s, v_s, do_s, delta_s,
                )

        def put(place, part, value):
            grad_ref[place, part] = value

        full_back_step(step, piece_rows, l_ref, put, q_s, k_s, v_s, do_s, delta_s, dq_s)


def backward_scratch(half):
    return [pltpu.VMEM((8 * half, 2 * HD), BF16)] * 4 + [
        pltpu.VMEM((8, 8 * half), F32),
        pltpu.VMEM((2 * HD, 8 * half), F32),
    ]


def backward_first(group, a, b, do, oa, ob, la, lb):
    _, half, lanes = a[0].shape
    operands = (*a, *b, *do, oa, ob, la, lb)
    out = (4, 3, half, lanes)
    return pl.pallas_call(
        backward_first_kernel,
        grid_spec=pltpu.PrefetchScalarGridSpec(
            num_scalar_prefetch=1,
            grid=(4,),
            in_specs=[whole(value.shape) for value in operands],
            out_specs=whole(out),
            scratch_shapes=backward_scratch(half) + [pltpu.VMEM(la.shape, F32)],
        ),
        out_shape=jax.ShapeDtypeStruct(out, BF16),
        compiler_params=params("arbitrary"),
        cost_estimate=pl.CostEstimate(
            flops=60_000_000_000, bytes_accessed=8_000_000, transcendentals=0
        ),
        name="backward_first",
    )(group, *operands)


def backward_second(group, packs, dol, ol, ll, b, do, ob, lb):
    heads, _, half, lanes = packs.shape
    each = lambda shape: pl.BlockSpec(
        (1,) + shape[1:], lambda i, g: (i * (1 - g[0]),) + (0,) * (len(shape) - 1)
    )
    operands = (*b, *do, ob, lb)
    outs = [(4, 3, half, lanes), (heads, 3, half, lanes)]
    return pl.pallas_call(
        backward_second_kernel,
        grid_spec=pltpu.PrefetchScalarGridSpec(
            num_scalar_prefetch=1,
            grid=(heads,),
            in_specs=[each(packs.shape), each(dol.shape), each(ol.shape), each(ll.shape)]
            + [whole(value.shape) for value in operands],
            out_specs=[whole(shape) for shape in outs],
            scratch_shapes=backward_scratch(half),
        ),
        out_shape=[jax.ShapeDtypeStruct(shape, BF16) for shape in outs],
        compiler_params=params("arbitrary"),
        cost_estimate=pl.CostEstimate(
            flops=60_000_000_000, bytes_accessed=8_000_000, transcendentals=0
        ),
        name="backward_second",
    )(group, packs, dol, ol, ll, *operands)


def middle_kernel(
    x_ref, cot_ref, att_ref, vec_ref, upb_ref, ow_ref, up_ref, down_ref,
    out_ref, attlow_ref, hidden_ref, act_ref, gfeed_ref, gpre_ref, mgrad_ref, gbranch_ref,
    gatt_ref, sums_ref, upsum_ref, att_s, slope_s,
):
    step = pl.program_id(0)
    rows, width = x_ref.shape[1:]
    both = 2 * rows
    pairs = width // (2 * HD)
    gate_one, gain, scale, shift = (vec_ref[i : i + 1, :] for i in range(4))
    gate_two, down_bias = vec_ref[4:5, :], vec_ref[5:6, :]
    for pair in range(pairs):
        lanes = slice(pair * 2 * HD, (pair + 1) * 2 * HD)
        top, bottom = exchange(
            att_ref[2 * pair].astype(F32), att_ref[2 * pair + 1].astype(F32)
        )
        att_s[:rows, lanes] = top.astype(BF16)
        att_s[rows:, lanes] = bottom.astype(BF16)
    att = att_s[...]
    attlow_ref[...] = att.reshape(2, rows, width)
    branch = jnp.dot(att, ow_ref[...], preferred_element_type=F32)
    middle = x_ref[...].reshape(both, width).astype(F32) + gate_one * branch
    n, inverse = normalise(middle)
    hidden = (n * gain * (1.0 + scale) + shift).astype(BF16)
    hidden_ref[...] = hidden.reshape(2, rows, width)
    units = up_ref.shape[1]
    chunk = math.gcd(units, 768)
    feed = None
    for start in range(0, units, chunk):
        cols = slice(start, start + chunk)
        pre = jnp.dot(hidden, up_ref[:, cols], preferred_element_type=F32) + upb_ref[0:1, cols]
        square = pre * pre
        root = math.sqrt(2.0 / math.pi)
        tanh = jnp.tanh(pre * (root + (root * 0.044715) * square))
        half_up = 0.5 + 0.5 * tanh
        act = (pre * half_up).astype(BF16)
        slope_s[:, cols] = half_up + (0.5 * pre) * (1.0 - tanh * tanh) * (
            root + (3.0 * root * 0.044715) * square
        )
        act_ref[:, :, cols] = act.reshape(2, rows, chunk)
        part = jnp.dot(act, down_ref[cols, :], preferred_element_type=F32)
        feed = part if feed is None else feed + part
    feed = feed + down_bias
    out_ref[...] = (middle + gate_two * feed).astype(BF16).reshape(2, rows, width)
    cot = cot_ref[...].reshape(both, width).astype(F32)
    gfeed = (gate_two * cot).astype(BF16)
    gfeed_ref[...] = gfeed.reshape(2, rows, width)
    ghidden = None
    up_sums = []
    for start in range(0, units, chunk):
        cols = slice(start, start + chunk)
        gact = lax.dot_general(gfeed, down_ref[cols, :], NT, preferred_element_type=F32)
        gpre = (gact * slope_s[:, cols]).astype(BF16)
        gpre_ref[:, :, cols] = gpre.reshape(2, rows, chunk)
        up_sums.append(jnp.sum(gpre.astype(F32), axis=0, keepdims=True))
        part = lax.dot_general(gpre, up_ref[:, cols], NT, preferred_element_type=F32)
        ghidden = part if ghidden is None else ghidden + part
    e = ghidden * ((1.0 + scale) * gain)
    mgrad = cot + inverse * (
        e - jnp.mean(e, axis=-1, keepdims=True) - n * jnp.mean(e * n, axis=-1, keepdims=True)
    )
    mgrad_ref[...] = mgrad.reshape(2, rows, width)
    gbranch = (gate_one * mgrad).astype(BF16)
    gbranch_ref[...] = gbranch.reshape(2, rows, width)
    gatt = lax.dot_general(gbranch, ow_ref[...], NT, preferred_element_type=F32)
    for pair in range(pairs):
        value = gatt[:, pair * 2 * HD : (pair + 1) * 2 * HD]
        even, odd = exchange(value[:rows], value[rows:])
        gatt_ref[2 * pair] = even.astype(BF16)
        gatt_ref[2 * pair + 1] = odd.astype(BF16)
    add = lambda value: jnp.sum(value, axis=0, keepdims=True)

    @pl.when(step == 0)
    def _():
        sums_ref[...] = jnp.zeros_like(sums_ref)
        upsum_ref[...] = jnp.zeros_like(upsum_ref)

    sums_ref[0:1, :] += add(ghidden)
    sums_ref[1:2, :] += add(ghidden * n)
    sums_ref[2:3, :] += add(cot * feed)
    sums_ref[3:4, :] += add(gfeed.astype(F32))
    sums_ref[4:5, :] += add(mgrad * branch)
    for index, value in enumerate(up_sums):
        upsum_ref[0:1, index * chunk : (index + 1) * chunk] += value


def once(shape):
    zeros = (0,) * len(shape)
    return pl.BlockSpec(shape, lambda *_: zeros, pipeline_mode=pl.Buffered(1))


def middle_pass(x2, cot2, att, vecs, up_bias, out_weight, up_full, down_full, rows=128):
    half, width = x2.shape[1:]
    heads = width // HD
    units = up_full.shape[1]
    tok = lambda last: pl.BlockSpec((2, rows, last), lambda i: (0, i, 0))
    pack = pl.BlockSpec((heads, rows, 2 * HD), lambda i: (0, i, 0))
    token = lambda last, kind: jax.ShapeDtypeStruct((2, half, last), kind)
    return pl.pallas_call(
        middle_kernel,
        grid=(half // rows,),
        in_specs=[
            tok(width), tok(width), pack, whole(vecs.shape), whole(up_bias.shape),
            once(out_weight.shape), once(up_full.shape), once(down_full.shape),
        ],
        out_specs=[
            tok(width), tok(width), tok(width), tok(units), tok(width), tok(units), tok(width),
            tok(width), pack, whole((8, width)), whole((8, units)),
        ],
        out_shape=[
            token(width, BF16), token(width, BF16), token(width, BF16), token(units, BF16),
            token(width, BF16), token(units, BF16), token(width, F32), token(width, BF16),
            jax.ShapeDtypeStruct((heads, half, 2 * HD), BF16),
            jax.ShapeDtypeStruct((8, width), F32),
            jax.ShapeDtypeStruct((8, units), F32),
        ],
        scratch_shapes=[pltpu.VMEM((2 * rows, width), BF16), pltpu.VMEM((2 * rows, units), F32)],
        compiler_params=params("arbitrary"),
        name="middle_pass",
    )(x2, cot2, att, vecs, up_bias, out_weight, up_full, down_full)


def unrotate_kernel(pack_ref, cos_ref, sin_ref, mixed_ref):
    rows = cos_ref.shape[1]
    cosine = cos_ref[...].reshape(2 * rows, 2 * HD)
    sine = -sin_ref[...].reshape(2 * rows, 2 * HD)
    heads = pack_ref.shape[0]
    width = heads * HD
    for part in range(3):
        for pair in range(heads // 2):
            top, bottom = exchange(
                pack_ref[2 * pair, part].astype(F32), pack_ref[2 * pair + 1, part].astype(F32)
            )
            value = jnp.concatenate([top, bottom], axis=0)
            if part < 2:
                value = turn(value, cosine, sine)
            start = part * width + pair * 2 * HD
            mixed_ref[:, :, start : start + 2 * HD] = value.astype(BF16).reshape(2, rows, 2 * HD)


def unrotate(packs, cosine, sine, rows=128):
    heads, _, half, lanes = packs.shape
    tok = lambda last: pl.BlockSpec((2, rows, last), lambda i: (0, i, 0))
    return pl.pallas_call(
        unrotate_kernel,
        grid=(half // rows,),
        in_specs=[
            pl.BlockSpec((heads, 3, rows, lanes), lambda i: (0, 0, i, 0)),
            tok(lanes),
            tok(lanes),
        ],
        out_specs=tok(3 * heads * HD),
        out_shape=jax.ShapeDtypeStruct((2, half, 3 * heads * HD), BF16),
        compiler_params=params("arbitrary"),
        name="unrotate",
    )(packs, cosine, sine)


def input_kernel(mixed_ref, w_ref, x_ref, mgrad_ref, vec_ref, grad_ref, sums_ref):
    step = pl.program_id(0)
    rows, width = x_ref.shape[1:]
    both = 2 * rows
    gnormed = lax.dot_general(
        mixed_ref[...].reshape(both, mixed_ref.shape[2]), w_ref[...], NT,
        preferred_element_type=F32,
    )
    n, inverse = normalise(x_ref[...].reshape(both, width).astype(F32))
    e = gnormed * ((1.0 + vec_ref[1:2, :]) * vec_ref[0:1, :])
    grad = mgrad_ref[...].reshape(both, width) + inverse * (
        e - jnp.mean(e, axis=-1, keepdims=True) - n * jnp.mean(e * n, axis=-1, keepdims=True)
    )
    grad_ref[...] = grad.reshape(2, rows, width)

    @pl.when(step == 0)
    def _():
        sums_ref[...] = jnp.zeros_like(sums_ref)

    sums_ref[0:1, :] += jnp.sum(gnormed, axis=0, keepdims=True)
    sums_ref[1:2, :] += jnp.sum(gnormed * n, axis=0, keepdims=True)


def input_pass(mixed, weight, x2, mgrad, vecs, rows=128):
    half, width = x2.shape[1:]
    tok = lambda last: pl.BlockSpec((2, rows, last), lambda i: (0, i, 0))
    return pl.pallas_call(
        input_kernel,
        grid=(half // rows,),
        in_specs=[
            tok(mixed.shape[2]), once(weight.shape), tok(width), tok(width), whole(vecs.shape)
        ],
        out_specs=[tok(width), whole((8, width))],
        out_shape=[
            jax.ShapeDtypeStruct((2, half, width), F32),
            jax.ShapeDtypeStruct((8, width), F32),
        ],
        compiler_params=params("arbitrary"),
        cost_estimate=pl.CostEstimate(
            flops=6_000_000_000, bytes_accessed=20_000_000, transcendentals=0
        ),
        name="input_pass",
    )(mixed, weight, x2, mgrad, vecs)


def along(value, steps):
    pairs = [(place, (place + steps) % 4) for place in range(4)]
    return lax.ppermute(value, "seq", pairs)


def along_second(value, steps):
    pairs = [(4 + place, 4 + (place + steps) % 4) for place in range(4)]
    return lax.ppermute(value, ("grp", "seq"), pairs)


def to_first(value):
    return lax.ppermute(value, "grp", [(1, 0)])


def to_second(value):
    return lax.ppermute(value, "grp", [(0, 1)])


def pick(stack, index):
    return lax.dynamic_index_in_dim(stack, index, 0, keepdims=False)


def four_shards(
    tokens, step_index, time_table, ada_weight, ada_bias, first_gain, qkv_weight, out_weight,
    second_gain, up_weight, up_bias, down_weight, down_bias, cotangent,
):
    place = lax.axis_index("seq")
    group = lax.axis_index("grp")
    mlp_count = lax.axis_size("mlp")
    second = group == 1
    token_rows, width = tokens.shape[1:]
    half = token_rows // 2
    heads = width // HD
    slot = lambda steps: (place + steps) % 4
    group_row = jnp.full((1,), group, jnp.int32)

    up_full = lax.all_gather(up_weight, "mlp", axis=1, tiled=True)
    down_full = lax.all_gather(down_weight, "mlp", axis=0, tiled=True)
    up_bias_full = lax.all_gather(up_bias.astype(F32), "mlp", axis=0, tiled=True)

    step_value = jnp.sum(jnp.where(jnp.arange(4, dtype=jnp.int32) == place, step_index[0], 0))
    embedded = lax.dynamic_slice_in_dim(time_table, step_value, 1, 0)[0].astype(F32)
    condition, silu_back = jax.vjp(jax.nn.silu, embedded)
    cond_low = condition.astype(BF16)
    modulation = jnp.dot(cond_low[None, :], ada_weight, preferred_element_type=F32)[
        0
    ] + ada_bias.astype(F32)
    shift_one, scale_one, gate_one, shift_two, scale_two, gate_two = jnp.split(modulation, 6)

    positions = jnp.arange(token_rows, dtype=jnp.int32) + jnp.where(second, place * token_rows, 0)
    frequency = jnp.exp(jnp.arange(HD // 2, dtype=F32) * (-2.0 * math.log(10000.0) / HD))
    angles = positions.astype(F32)[:, None] * frequency[None, :]
    cosine, sine = jnp.cos(angles), jnp.sin(angles)
    cosine = jnp.concatenate([cosine] * 4, axis=1).reshape(2, half, 2 * HD)
    sine = jnp.concatenate([-sine, sine] * 2, axis=1).reshape(2, half, 2 * HD)

    x2 = tokens.reshape(2, half, width)
    blank = jnp.zeros((width,), F32)
    gain_one = first_gain.astype(F32)
    gain_two = second_gain.astype(F32)
    vec_one = jnp.stack([gain_one, scale_one, shift_one] + [blank] * 5)
    vec_two = jnp.stack(
        [gate_one, gain_two, scale_two, shift_two, gate_two, down_bias.astype(F32), blank, blank]
    )
    normed, packs = project(x2, vec_one, qkv_weight, cosine, sine)

    crossed = to_first(packs[8:])
    a = [pick(packs, 2 * slot(0))] + [
        along_second(pick(packs, 2 * slot(s)), s) for s in (1, 2, 3)
    ]
    b_from = jnp.where(second, packs[1:8:2], crossed)
    b = [pick(b_from, slot(0))] + [along(pick(b_from, slot(s)), s) for s in (1, 2, 3)]
    oa, la, o_own, l_own = forward_first(group_row, packs, a)
    ob, lb = forward_second(b)

    def home(pieces):
        parts = [pieces[0]] + [along(pieces[s], -s) for s in (1, 2, 3)]
        return jnp.roll(jnp.stack(parts), place, axis=0)

    def join(from_a, from_b, from_first, own):
        interleaved = jnp.stack([from_a, from_b], axis=1).reshape((8,) + from_a.shape[1:])
        return jnp.where(second, jnp.concatenate([interleaved, from_first]), own)

    a_home = home(oa)
    b_home = home(ob)
    att = join(a_home, b_home, to_second(b_home), o_own)

    up_bias_row = jnp.broadcast_to(up_bias_full[None, :], (8, up_bias_full.shape[0]))
    (
        output, att_low, hidden, act, grad_feed, grad_pre, middle_grad, grad_branch, grad_att,
        middle_sums, up_sums,
    ) = middle_pass(
        x2, cotangent.reshape(2, half, width), att, vec_two, up_bias_row, out_weight, up_full,
        down_full,
    )
    flat = lambda value: value.reshape(token_rows, value.shape[2])
    across = lambda left, right: lax.dot_general(
        flat(left), flat(right), TN, preferred_element_type=F32
    )

    crossed_grad = to_first(grad_att[8:])
    f_from = jnp.where(second, grad_att[0:8:2], crossed_grad)
    do_f = [pick(f_from, slot(0))] + [along(pick(f_from, slot(s)), s) for s in (1, 2, 3)]
    do_b = [pick(grad_att, 2 * slot(0) % 8 + 1)] + [
        along_second(pick(grad_att, 2 * slot(s) + 1), s) for s in (1, 2, 3)
    ]
    out_grad = across(att_low, grad_branch)
    up_grad = across(hidden, grad_pre)
    down_grad = across(act, grad_feed)
    grad_f = backward_first(group_row, a, b, do_f, oa, ob, la, lb)
    grad_s, grad_own = backward_second(
        group_row, packs, grad_att, o_own, l_own, b, do_b, ob, lb
    )
    f_home = home(grad_f)
    s_home = home(grad_s)
    grads = join(f_home, s_home, to_second(f_home), grad_own)
    mixed_grad = unrotate(grads, cosine, sine)
    qkv_grad = across(normed, mixed_grad)
    input_grad, input_sums = input_pass(mixed_grad, qkv_weight, x2, middle_grad, vec_one)

    shift_one_grad = input_sums[0]
    first_gain_grad = (1.0 + scale_one) * input_sums[1]
    scale_one_grad = gain_one * input_sums[1]
    shift_two_grad = middle_sums[0]
    second_gain_grad = (1.0 + scale_two) * middle_sums[1]
    scale_two_grad = gain_two * middle_sums[1]
    mod_grad = jnp.concatenate(
        [
            shift_one_grad, scale_one_grad, middle_sums[4], shift_two_grad, scale_two_grad,
            middle_sums[2],
        ]
    )
    cond_grad = jnp.dot(ada_weight.astype(F32), mod_grad, precision=highest)
    table_row = silu_back(cond_grad)[0]
    small = jnp.concatenate(
        [
            mod_grad, first_gain_grad, second_gain_grad, up_sums[0], middle_sums[3],
            table_row, condition,
        ]
    )
    step_row = jnp.full((1,), step_value, jnp.int32)
    small_all = lax.all_gather(small, ("grp", "seq", "mlp"), axis=0)
    steps_all = lax.all_gather(step_row, ("grp", "seq", "mlp"), axis=0, tiled=True)
    rank = place * mlp_count + lax.axis_index("mlp")
    ranks = 4 * mlp_count

    def share(start, size):
        each = size // ranks
        return lax.dynamic_slice_in_dim(small_all, start + rank * each, each, 1)

    mod_size = 6 * width
    units = up_full.shape[1]
    mod_share = share(0, mod_size)
    start = mod_size
    first_share = jnp.sum(share(start, width), axis=0)
    start += width
    second_share = jnp.sum(share(start, width), axis=0)
    start += width
    up_bias_share = jnp.sum(share(start, units), axis=0)
    start += units
    down_bias_share = jnp.sum(share(start, width), axis=0)
    start += width
    cond_size = condition.shape[0]
    rows_all = small_all[:, start : start + cond_size]
    cond_all = small_all[:, start + cond_size :].astype(BF16).astype(F32)
    ada_share = lax.dot_general(cond_all, mod_share, TN, precision=highest)
    table_each = time_table.shape[0] // ranks
    own_rows = rank * table_each + jnp.arange(table_each, dtype=jnp.int32)
    chosen = (own_rows[:, None] == steps_all[None, :]).astype(F32)
    table_share = jnp.dot(chosen, rows_all, precision=highest)

    both_axes = ("seq", "mlp")
    big = (
        lax.psum_scatter(qkv_grad, both_axes, scatter_dimension=0, tiled=True),
        lax.psum_scatter(out_grad, both_axes, scatter_dimension=0, tiled=True),
        lax.psum_scatter(
            lax.psum_scatter(up_grad, "mlp", scatter_dimension=1, tiled=True),
            "seq", scatter_dimension=0, tiled=True,
        ),
        lax.psum_scatter(
            lax.psum_scatter(down_grad, "mlp", scatter_dimension=0, tiled=True),
            "seq", scatter_dimension=1, tiled=True,
        ),
    )
    qkv_total, out_total, up_total, down_total = lax.psum(big, "grp")
    return (
        output.reshape(1, token_rows, width),
        input_grad.reshape(1, token_rows, width),
        table_share,
        ada_share,
        jnp.sum(mod_share, axis=0),
        first_share,
        qkv_total,
        out_total,
        second_share,
        up_total,
        up_bias_share,
        down_total,
        down_bias_share,
    )


def solution(mesh):
    in_specs = (
        P(("grp", "mlp"), "seq", None),
        P(("grp", "mlp"), None),
        P(),
        P(),
        P(),
        P(),
        P(),
        P(),
        P(),
        P(None, "mlp"),
        P("mlp"),
        P("mlp", None),
        P(),
        P(("grp", "mlp"), "seq", None),
    )
    out_specs = (
        P(("grp", "mlp"), "seq", None),
        P(("grp", "mlp"), "seq", None),
        P(("seq", "mlp"), None),
        P(None, ("seq", "mlp")),
        P(("seq", "mlp")),
        P(("seq", "mlp")),
        P(("seq", "mlp"), None),
        P(("seq", "mlp"), None),
        P(("seq", "mlp")),
        P("seq", "mlp"),
        P(("seq", "mlp")),
        P("mlp", "seq"),
        P(("seq", "mlp")),
    )
    body = four_shards if mesh.shape["seq"] == 4 and mesh.shape["grp"] == 2 else shards
    return jax.shard_map(body, mesh=mesh, in_specs=in_specs, out_specs=out_specs, check_vma=False)
```

```python
import math

import jax
import jax.numpy as jnp
from jax import lax
from jax.experimental import pallas as pl
from jax.experimental.pallas import tpu as pltpu
from jax.sharding import PartitionSpec as P

HD = 64


highest = lax.Precision.HIGHEST


def shifted(value, axis, steps):
    count = lax.axis_size(axis)
    pairs = [(source, (source + steps) % count) for source in range(count)]
    return lax.ppermute(value, axis, pairs)


def layer_norm(values, norm_gain):
    centred = values - jnp.mean(values, axis=-1, keepdims=True)
    spread = jnp.mean(centred * centred, axis=-1, keepdims=True)
    return centred * lax.rsqrt(spread + 1e-05) * norm_gain


def modulate(values, norm_gain, shift_part, scale_part):
    return layer_norm(values, norm_gain) * (1.0 + scale_part) + shift_part


def gelu_tanh(values):
    return jax.nn.gelu(values, approximate=True)


def rotate_pairs(values, positions):
    half_dim = HD // 2
    frequency = jnp.exp(jnp.arange(half_dim, dtype=jnp.float32) * (-2.0 * math.log(10000.0) / HD))
    angles = positions.astype(jnp.float32)[:, None] * frequency[None, :]
    cosine = jnp.cos(angles)[:, None, :]
    sine_part = jnp.sin(angles)[:, None, :]
    leading = values[..., :half_dim]
    trailing = values[..., half_dim:]
    return jnp.concatenate(
        [leading * cosine - trailing * sine_part, trailing * cosine + leading * sine_part], axis=-1
    )


def shards(
    tokens,
    step_index,
    time_table,
    ada_weight,
    ada_bias,
    first_gain,
    qkv_weight,
    out_weight,
    second_gain,
    up_weight,
    up_bias,
    down_weight,
    down_bias,
    cotangent,
):
    seq_count = lax.axis_size("seq")
    seq_place = lax.axis_index("seq")
    group_index = lax.axis_index("grp")
    mlp_place = lax.axis_index("mlp")
    tok_rows = tokens.shape[1]
    model_width = tokens.shape[2]
    head_count = model_width // HD
    score_scale = 1.0 / math.sqrt(HD)
    line_len = tok_rows * seq_count
    seq_length = jnp.where(group_index == 0, line_len // 4, line_len).astype(jnp.int32)
    row_ids = jnp.arange(tok_rows, dtype=jnp.int32)
    own_pos = seq_place * tok_rows + row_ids
    positions = own_pos % seq_length
    quarter = seq_place // (seq_count // 4)
    step_value = jnp.sum(jnp.where(jnp.arange(4, dtype=jnp.int32) == quarter, step_index[0], 0))
    table_pick = jnp.arange(time_table.shape[0], dtype=jnp.int32) == step_value
    embedded = jnp.dot(
        table_pick.astype(jnp.bfloat16)[None, :], time_table, preferred_element_type=jnp.float32
    )[0]
    condition, silu_back = jax.vjp(jax.nn.silu, embedded)
    cond_low = condition.astype(jnp.bfloat16)
    modulation = jnp.dot(cond_low[None, :], ada_weight, preferred_element_type=jnp.float32)[
        0
    ] + ada_bias.astype(jnp.float32)
    shift_one, scale_one, gate_one, shift_two, scale_two, gate_two = jnp.split(modulation, 6)
    inputs = tokens[0].astype(jnp.float32)
    normed, first_back = jax.vjp(
        modulate, inputs, first_gain.astype(jnp.float32), shift_one, scale_one
    )
    normed_low = normed.astype(jnp.bfloat16)
    mixed_rows = jnp.dot(normed_low, qkv_weight, preferred_element_type=jnp.float32)

    def rotate_all(mixed_in):
        query_part = rotate_pairs(
            mixed_in[:, :model_width].reshape(tok_rows, head_count, HD), positions
        )
        key_part = rotate_pairs(
            mixed_in[:, model_width : 2 * model_width].reshape(tok_rows, head_count, HD), positions
        )
        return (
            query_part,
            key_part,
            mixed_in[:, 2 * model_width :].reshape(tok_rows, head_count, HD),
        )

    rotated, rotate_back = jax.vjp(rotate_all, mixed_rows)
    queries = rotated[0].astype(jnp.bfloat16)
    key_rows = rotated[1].astype(jnp.bfloat16)
    value_rows = rotated[2].astype(jnp.bfloat16)
    start_state = (
        jnp.full((head_count, tok_rows), -1e30, jnp.float32),
        jnp.zeros((head_count, tok_rows), jnp.float32),
        jnp.zeros((head_count, tok_rows, HD), jnp.float32),
    )
    key_piece = lax.all_gather(key_rows.reshape(tok_rows, model_width), "seq", axis=0, tiled=True)
    value_piece = lax.all_gather(
        value_rows.reshape(tok_rows, model_width), "seq", axis=0, tiled=True
    )
    piece_rows = key_piece.shape[0]
    sub_rows = math.gcd(piece_rows, 512)

    def one_block(block_index, block_state):
        run_max, run_total, run_acc = block_state
        offset = block_index * sub_rows
        key_block = lax.dynamic_slice_in_dim(key_piece, offset, sub_rows, 0).reshape(
            sub_rows, head_count, HD
        )
        value_block = lax.dynamic_slice_in_dim(value_piece, offset, sub_rows, 0).reshape(
            sub_rows, head_count, HD
        )
        key_pos = offset + jnp.arange(sub_rows, dtype=jnp.int32)
        same_seq = (own_pos // seq_length)[:, None] == (key_pos // seq_length)[None, :]
        scores = (
            jnp.einsum("qhd,khd->hqk", queries, key_block, preferred_element_type=jnp.float32)
            * score_scale
        )
        masked = jnp.where(same_seq[None], scores, -1e30)
        new_max = jnp.maximum(run_max, jnp.max(masked, axis=-1))
        shrink = jnp.exp(run_max - new_max)
        weights = jnp.where(same_seq[None], jnp.exp(masked - new_max[..., None]), 0.0)
        run_total = run_total * shrink + jnp.sum(weights, axis=-1)
        run_acc = run_acc * shrink[..., None] + jnp.einsum(
            "hqk,khd->hqd",
            weights.astype(jnp.bfloat16),
            value_block,
            preferred_element_type=jnp.float32,
        )
        return (new_max, run_total, run_acc)

    run_max, run_total, run_acc = lax.fori_loop(0, piece_rows // sub_rows, one_block, start_state)
    log_total = run_max + jnp.log(run_total)
    attended3 = jnp.transpose(run_acc / run_total[..., None], (1, 0, 2))
    attended_low = attended3.reshape(tok_rows, model_width).astype(jnp.bfloat16)
    branch = jnp.dot(attended_low, out_weight, preferred_element_type=jnp.float32)
    middle = inputs + gate_one * branch
    hidden, second_back = jax.vjp(
        modulate, middle, second_gain.astype(jnp.float32), shift_two, scale_two
    )
    hidden_low = hidden.astype(jnp.bfloat16)
    gathered = lax.all_gather(hidden_low, "mlp", axis=0, tiled=True)
    pre_act = jnp.dot(gathered, up_weight, preferred_element_type=jnp.float32) + up_bias.astype(
        jnp.float32
    )
    activated, gelu_back = jax.vjp(gelu_tanh, pre_act)
    act_low = activated.astype(jnp.bfloat16)
    feed_terms = jnp.dot(act_low, down_weight, preferred_element_type=jnp.float32)
    feed_out = lax.psum_scatter(
        feed_terms, "mlp", scatter_dimension=0, tiled=True
    ) + down_bias.astype(jnp.float32)
    output = (middle + gate_two * feed_out).astype(jnp.bfloat16)[None]
    grad_out = cotangent[0].astype(jnp.float32)
    gate_two_grad = jnp.sum(grad_out * feed_out, axis=0)
    grad_feed = (gate_two * grad_out).astype(jnp.bfloat16)
    down_bias_grad = jnp.sum(grad_feed, axis=0, dtype=jnp.float32)
    grad_rows = lax.all_gather(grad_feed, "mlp", axis=0, tiled=True)
    down_grad = jnp.einsum("tf,td->fd", act_low, grad_rows, preferred_element_type=jnp.float32)
    grad_act = jnp.einsum("td,fd->tf", grad_rows, down_weight, preferred_element_type=jnp.float32)
    grad_pre = gelu_back(grad_act)[0].astype(jnp.bfloat16)
    up_grad = jnp.einsum("td,tf->df", gathered, grad_pre, preferred_element_type=jnp.float32)
    local_units = up_weight.shape[1]
    bias_slot = lax.dynamic_update_slice_in_dim(
        jnp.zeros((local_units * lax.axis_size("mlp"),), jnp.float32),
        jnp.sum(grad_pre, axis=0, dtype=jnp.float32),
        mlp_place * local_units,
        0,
    )
    hidden_terms = jnp.einsum("tf,df->td", grad_pre, up_weight, preferred_element_type=jnp.float32)
    grad_hidden = lax.psum_scatter(hidden_terms, "mlp", scatter_dimension=0, tiled=True)
    middle_part, second_gain_grad, shift_two_grad, scale_two_grad = second_back(grad_hidden)
    middle_grad = grad_out + middle_part
    gate_one_grad = jnp.sum(middle_grad * branch, axis=0)
    grad_branch = (gate_one * middle_grad).astype(jnp.bfloat16)
    out_grad = jnp.einsum(
        "td,te->de", attended_low, grad_branch, preferred_element_type=jnp.float32
    )
    grad_attended = jnp.einsum(
        "te,de->td", grad_branch, out_weight, preferred_element_type=jnp.float32
    ).astype(jnp.bfloat16)
    grad_heads = grad_attended.reshape(tok_rows, head_count, HD)
    row_delta = jnp.transpose(jnp.sum(grad_heads.astype(jnp.float32) * attended3, axis=-1))

    def pair_grads(
        query_set, grad_set, total_set, delta_set, query_anchor, key_set, value_set, key_anchor
    ):
        query_pos = query_anchor * tok_rows + row_ids
        key_pos = key_anchor * tok_rows + row_ids
        same_seq = (query_pos // seq_length)[:, None] == (key_pos // seq_length)[None, :]
        scores = (
            jnp.einsum("qhd,khd->hqk", query_set, key_set, preferred_element_type=jnp.float32)
            * score_scale
        )
        prob_rows = jnp.where(same_seq[None], jnp.exp(scores - total_set[..., None]), 0.0)
        value_part = jnp.einsum(
            "hqk,qhd->khd",
            prob_rows.astype(jnp.bfloat16),
            grad_set,
            preferred_element_type=jnp.float32,
        )
        prob_grad = jnp.einsum(
            "qhd,khd->hqk", grad_set, value_set, preferred_element_type=jnp.float32
        )
        score_grad = (prob_rows * (prob_grad - delta_set[..., None])).astype(jnp.bfloat16)
        query_part = (
            jnp.einsum("hqk,khd->qhd", score_grad, key_set, preferred_element_type=jnp.float32)
            * score_scale
        )
        key_part = (
            jnp.einsum("hqk,qhd->khd", score_grad, query_set, preferred_element_type=jnp.float32)
            * score_scale
        )
        return (query_part, key_part, value_part)

    zero_heads = jnp.zeros((tok_rows, head_count, HD), jnp.float32)

    def key_turn(running):
        key_set, value_set, key_acc, value_acc, anchor, query_acc = running
        query_part, key_part, value_part = pair_grads(
            queries, grad_heads, log_total, row_delta, seq_place, key_set, value_set, anchor
        )
        moved_rows = shifted((key_set, value_set), "seq", 1)
        moved_grads = shifted((key_acc + key_part, value_acc + value_part), "seq", 1)
        return (
            moved_rows[0],
            moved_rows[1],
            moved_grads[0],
            moved_grads[1],
            (anchor - 1) % seq_count,
            query_acc + query_part,
        )

    def two_key_turns(turn_index, running):
        return key_turn(key_turn(running))

    finished = lax.fori_loop(
        0,
        seq_count // 2,
        two_key_turns,
        (key_rows, value_rows, zero_heads, zero_heads, seq_place, zero_heads),
    )
    query_grad, key_grad, value_grad = (finished[5], finished[2], finished[3])
    mixed_grad = rotate_back((query_grad, key_grad, value_grad))[0].astype(jnp.bfloat16)
    qkv_grad = jnp.einsum("td,te->de", normed_low, mixed_grad, preferred_element_type=jnp.float32)
    grad_normed = jnp.einsum(
        "te,de->td", mixed_grad, qkv_weight, preferred_element_type=jnp.float32
    )
    input_part, first_gain_grad, shift_one_grad, scale_one_grad = first_back(grad_normed)
    input_grad = (middle_grad + input_part)[None]
    mod_grad = jnp.concatenate(
        [
            shift_one_grad,
            scale_one_grad,
            gate_one_grad,
            shift_two_grad,
            scale_two_grad,
            gate_two_grad,
        ]
    )
    ada_grad = cond_low.astype(jnp.float32)[:, None] * mod_grad[None, :]
    cond_grad = jnp.dot(ada_weight.astype(jnp.float32), mod_grad, precision=highest)
    table_local = table_pick.astype(jnp.float32)[:, None] * silu_back(cond_grad)[0][None, :]
    layer_sums = (
        lax.psum_scatter(table_local, ("seq", "mlp"), scatter_dimension=0, tiled=True),
        lax.psum_scatter(ada_grad, ("seq", "mlp"), scatter_dimension=1, tiled=True),
        lax.psum_scatter(mod_grad, ("seq", "mlp"), scatter_dimension=0, tiled=True),
        lax.psum_scatter(first_gain_grad, ("seq", "mlp"), scatter_dimension=0, tiled=True),
        lax.psum_scatter(qkv_grad, ("seq", "mlp"), scatter_dimension=0, tiled=True),
        lax.psum_scatter(out_grad, ("seq", "mlp"), scatter_dimension=0, tiled=True),
        lax.psum_scatter(second_gain_grad, ("seq", "mlp"), scatter_dimension=0, tiled=True),
        lax.psum_scatter(bias_slot, ("seq", "mlp"), scatter_dimension=0, tiled=True),
        lax.psum_scatter(down_bias_grad, ("seq", "mlp"), scatter_dimension=0, tiled=True),
    )
    feed_summed = (
        lax.psum_scatter(up_grad, "seq", scatter_dimension=0, tiled=True),
        lax.psum_scatter(down_grad, "seq", scatter_dimension=1, tiled=True),
    )
    totals = lax.psum(
        (
            layer_sums[0],
            layer_sums[1],
            layer_sums[2],
            layer_sums[3],
            layer_sums[4],
            layer_sums[5],
            layer_sums[6],
            layer_sums[7],
            layer_sums[8],
            feed_summed[0],
            feed_summed[1],
        ),
        "grp",
    )
    return (
        output,
        input_grad,
        totals[0],
        totals[1],
        totals[2],
        totals[3],
        totals[4],
        totals[5],
        totals[6],
        totals[9],
        totals[7],
        totals[10],
        totals[8],
    )


LOG_SCALE = math.log2(math.e) / math.sqrt(HD)
NT = (((1,), (1,)), ((), ()))
TN = (((0,), (0,)), ((), ()))
F32 = jnp.float32
BF16 = jnp.bfloat16
WHOLE_VMEM = 60 * 1024 * 1024


def params(*semantics):
    return pltpu.CompilerParams(vmem_limit_bytes=WHOLE_VMEM, dimension_semantics=semantics)


def low_lanes(value):
    return lax.broadcasted_iota(jnp.int32, value.shape, 1) < HD


def swap_heads(value):
    return pltpu.roll(value, HD, 1)


def exchange(top, bottom):
    keep = low_lanes(top)
    return (
        jnp.where(keep, top, swap_heads(bottom)),
        jnp.where(keep, swap_heads(top), bottom),
    )


def fold(value):
    half = value.shape[0] // 2
    top = value[:half]
    return jnp.where(low_lanes(top), top, swap_heads(value[half:]))


def unfold_into(target, base, packed, fill):
    half = packed.shape[0]
    value = packed.astype(F32)
    keep = low_lanes(value)
    target[base : base + half, :] = jnp.where(keep, value, fill).astype(BF16)
    target[base + half : base + 2 * half, :] = jnp.where(keep, swap_heads(value), fill).astype(BF16)


def turn(value, cosine, sine):
    lane = lax.broadcasted_iota(jnp.int32, value.shape, 1) % HD
    quarter = HD // 2
    other = jnp.where(
        lane < quarter, pltpu.roll(value, 2 * HD - quarter, 1), pltpu.roll(value, quarter, 1)
    )
    return value * cosine + other * sine


def normalise(values):
    centred = values - jnp.mean(values, axis=-1, keepdims=True)
    spread = jnp.mean(centred * centred, axis=-1, keepdims=True)
    inverse = lax.rsqrt(spread + 1e-05)
    return centred * inverse, inverse


def project_kernel(x_ref, vec_ref, w_ref, cos_ref, sin_ref, normed_ref, pack_ref):
    rows = x_ref.shape[1]
    width = x_ref.shape[2]
    x = x_ref[...].reshape(2 * rows, width).astype(F32)
    n, _ = normalise(x)
    normed = n * vec_ref[0:1, :] * (1.0 + vec_ref[1:2, :]) + vec_ref[2:3, :]
    normed = normed.astype(BF16)
    normed_ref[...] = normed.reshape(2, rows, width)
    cosine = cos_ref[...].reshape(2 * rows, 2 * HD)
    sine = sin_ref[...].reshape(2 * rows, 2 * HD)
    for part in range(3):
        mixed = jnp.dot(
            normed, w_ref[:, part * width : (part + 1) * width], preferred_element_type=F32
        )
        for pair in range(width // (2 * HD)):
            value = mixed[:, pair * 2 * HD : (pair + 1) * 2 * HD]
            if part < 2:
                value = turn(value, cosine, sine)
            even, odd = exchange(value[:rows], value[rows:])
            pack_ref[2 * pair, part] = even.astype(BF16)
            pack_ref[2 * pair + 1, part] = odd.astype(BF16)


def project(x2, vecs, weight, cosine, sine, rows=256):
    half, width = x2.shape[1:]
    heads = width // HD
    tok = lambda last: pl.BlockSpec((2, rows, last), lambda i: (0, i, 0))
    return pl.pallas_call(
        project_kernel,
        grid=(half // rows,),
        in_specs=[
            tok(width),
            pl.BlockSpec(vecs.shape, lambda i: (0, 0)),
            pl.BlockSpec(weight.shape, lambda i: (0, 0)),
            tok(2 * HD),
            tok(2 * HD),
        ],
        out_specs=[tok(width), pl.BlockSpec((heads, 3, rows, 2 * HD), lambda i: (0, 0, i, 0))],
        out_shape=[
            jax.ShapeDtypeStruct((2, half, width), BF16),
            jax.ShapeDtypeStruct((heads, 3, half, 2 * HD), BF16),
        ],
        compiler_params=params("arbitrary"),
        name="project",
    )(x2, vecs, weight, cosine, sine)


def attend_rows(q, k_ref, v_ref, keys, out_put, log_put, block=512):
    top = None
    for start in range(0, keys, block):
        s = lax.dot_general(q, k_ref[start : start + block, :], NT, preferred_element_type=F32)
        s = s * LOG_SCALE
        peak = jnp.max(s, axis=1, keepdims=True)
        new_top = peak if top is None else jnp.maximum(top, peak)
        p = jnp.exp2(s - new_top).astype(BF16)
        part = jnp.dot(p, v_ref[start : start + block, :], preferred_element_type=F32)
        acc = part if top is None else acc * jnp.exp2(top - new_top) + part
        top = new_top
    out_put(fold(acc / swap_heads(acc)).astype(BF16))
    log_put((top + jnp.log2(acc)).T[HD : HD + 8])


def load_values(source, base, k_s, v_s):
    unfold_into(k_s, base, source[1], 0.0)
    unfold_into(v_s, base, source[2], 1.0)


def packed_queries(packed):
    value = packed.astype(F32)
    return jnp.concatenate([value, swap_heads(value)]).astype(BF16)


def reach(src, dst, sems, index, group, place):
    return pltpu.make_async_remote_copy(
        src_ref=src, dst_ref=dst, send_sem=sems[0].at[index], recv_sem=sems[1].at[index],
        device_id={"grp": group, "seq": place}, device_id_type=pl.DeviceIdType.MESH,
    )


def greet(group, place):
    barrier = pltpu.get_barrier_semaphore()
    for other in range(2):
        for steps in range(4):
            if other or steps:
                pl.semaphore_signal(
                    barrier, 1,
                    device_id={"grp": (group + other) % 2, "seq": (place + steps) % 4},
                    device_id_type=pl.DeviceIdType.MESH,
                )
    pl.semaphore_wait(barrier, 7)


def forward_kernel(
    packs, att, pieces, results, logs, logs_own, crossed, k_s, v_s, send_sems, recv_sems
):
    group = lax.axis_index("grp")
    place = lax.axis_index("seq")
    sems = (send_sems, recv_sems)
    heads = packs.shape[0]
    rows = 2 * packs.shape[2]
    ahead = lambda s: (place + s) % 4
    behind = lambda s: (place + 4 - s) % 4

    def first(s):
        return reach(packs.at[2 * ahead(s)], pieces.at[0, s], sems, s - 1, 1, ahead(s))

    def second_values(s):
        source = packs.at[2 * ahead(s) + 1, pl.ds(1, 2)]
        return reach(source, pieces.at[1, s, pl.ds(1, 2)], sems, 2 + s, 1, ahead(s))

    def second_queries(s):
        source = packs.at[2 * ahead(s) + 1, 0]
        return reach(source, pieces.at[1, s, 0], sems, 5 + s, 1, ahead(s))

    def cross(s):
        return reach(packs.at[8 + ahead(s)], crossed.at[s], sems, 9 + s, 0, place)

    def onward(s):
        return reach(crossed.at[s], pieces.at[1, s], sems, 12 + s, 0, ahead(s))

    def home(kind, s, head):
        start = (16, 20, 24)[kind]
        return reach(
            results.at[min(kind, 1), s], att.at[head], sems, start + s, 1, behind(s)
        )

    greet(group, place)

    def full(kind, head, before, after):
        sel = min(kind, 1)
        for s in range(4):
            load_values(pieces.at[sel, s], s * rows, k_s, v_s)

        def step(s, carry):
            before(s)

            def put_out(value):
                results[sel, s] = value

            def put_log(value):
                logs[sel, s] = value

            q = packed_queries(pieces[sel, s, 0])
            attend_rows(q, k_s, v_s, 4 * rows, put_out, put_log)
            after(s)
            return carry

        lax.fori_loop(0, 4, step, 0)

    @pl.when(group == 1)
    def _():
        for s in (1, 2, 3):
            first(s).start()
        for s in (1, 2, 3, 0):
            cross(s).start()
        pieces[0, 0] = packs[2 * place]
        pieces[1, 0] = packs[2 * place + 1]
        for s in (1, 2, 3):
            first(s).wait_send()
        for s in (1, 2, 3):
            second_values(s).start()
        for s in (1, 2, 3):
            first(s).wait_recv()

        def before(s):
            @pl.when(s == 2)
            def _():
                for other in (1, 2, 3):
                    second_queries(other).start()

        def after(s):
            @pl.when(s == 0)
            def _():
                att[2 * place] = results[0, 0]

            @pl.when(s > 0)
            def _():
                home(0, s, 2 * place).start()

        full(0, 2 * place, before, after)
        for s in (1, 2, 3):
            second_values(s).wait_recv()

    @pl.when(group == 0)
    def _():
        def local(head, carry):
            load_values(packs.at[head], 0, k_s, v_s)

            def put_out(value):
                att[head] = value

            def put_log(value):
                logs_own[head] = value

            attend_rows(packed_queries(packs[head, 0]), k_s, v_s, rows, put_out, put_log)
            for s in (1, 2, 3):

                @pl.when(head == 4 * s - 1)
                def _(s=s):
                    cross(s).wait_recv()
                    onward(s).start()

            return carry

        lax.fori_loop(0, heads, local, 0)
        cross(0).wait_recv()
        pieces[1, 0] = crossed[0]
        for s in (1, 2, 3):
            onward(s).wait_recv()

    def before(s):
        @pl.when((group == 1) & (s > 0))
        def _():
            second_queries(s).wait_recv()

    def after(s):
        @pl.when((group == 1) & (s == 0))
        def _():
            att[2 * place + 1] = results[1, 0]

        @pl.when((group == 1) & (s > 0))
        def _():
            home(1, s, 2 * place + 1).start()

        @pl.when(group == 0)
        def _():
            home(2, s, 8 + place).start()

    full(1, 0, before, after)

    @pl.when(group == 1)
    def _():
        for s in (1, 2, 3):
            second_values(s).wait_send()
            second_queries(s).wait_send()
            for kind in (0, 1):
                home(kind, s, 2 * place + kind).wait_send()
        for s in range(4):
            cross(s).wait_send()
        for s in (1, 2, 3):
            for kind in (0, 1):
                home(kind, s, 2 * ahead(s) + kind).wait_recv()
        for s in range(4):
            home(2, s, 8 + ahead(s)).wait_recv()

    @pl.when(group == 0)
    def _():
        for s in (1, 2, 3):
            onward(s).wait_send()
        for s in range(4):
            home(2, s, 8 + place).wait_send()


def in_vmem(count):
    return [pl.BlockSpec(memory_space=pltpu.VMEM)] * count


def forward_attention(packs):
    heads, _, half, lanes = packs.shape
    shapes = [
        ((heads, half, lanes), BF16),
        ((2, 4, 3, half, lanes), BF16),
        ((2, 4, half, lanes), BF16),
        ((2, 4, 8, 2 * half), F32),
        ((heads, 8, 2 * half), F32),
    ]
    return pl.pallas_call(
        forward_kernel,
        in_specs=in_vmem(1),
        out_specs=in_vmem(len(shapes)),
        out_shape=[jax.ShapeDtypeStruct(shape, kind) for shape, kind in shapes],
        scratch_shapes=[
            pltpu.VMEM((4, 3, half, lanes), BF16),
            pltpu.VMEM((8 * half, lanes), BF16),
            pltpu.VMEM((8 * half, lanes), BF16),
            pltpu.SemaphoreType.DMA((28,)),
            pltpu.SemaphoreType.DMA((28,)),
        ],
        compiler_params=pltpu.CompilerParams(
            collective_id=1, has_side_effects=True, vmem_limit_bytes=WHOLE_VMEM
        ),
        cost_estimate=pl.CostEstimate(
            flops=100_000_000_000, bytes_accessed=8_000_000, transcendentals=0
        ),
        name="forward_attention",
    )(packs)


def tile_grads(q, do, k, v, log_row, delta_row):
    s = lax.dot_general(k, q, NT, preferred_element_type=F32)
    p = jnp.exp2(s * LOG_SCALE - log_row)
    dp = lax.dot_general(v, do, NT, preferred_element_type=F32)
    ds = (p * (dp - delta_row)).astype(BF16)
    dv = jnp.dot(p.astype(BF16), do, preferred_element_type=F32)
    dk = jnp.dot(ds, q, preferred_element_type=F32)
    dq = lax.dot_general(k, ds, TN, preferred_element_type=F32)
    return dq, dk, dv


def load_backward(source, do, o, base, q_s, k_s, v_s, do_s, delta_s):
    half = do.shape[0]
    unfold_into(q_s, base, source[0], 0.0)
    unfold_into(k_s, base, source[1], 0.0)
    unfold_into(v_s, base, source[2], 0.0)
    unfold_into(do_s, base, do, 0.0)
    product = (do.astype(F32) * o.astype(F32)).T
    first = jnp.sum(product[:HD], axis=0, keepdims=True)
    second = jnp.sum(product[HD:], axis=0, keepdims=True)
    delta_s[:, base : base + half] = jnp.broadcast_to(first, (8, half))
    delta_s[:, base + half : base + 2 * half] = jnp.broadcast_to(second, (8, half))


def backward_kernel(
    packs, gatt, att, pieces, results, logs, logs_own, back,
    dos, crossed, staged, q_s, k_s, v_s, do_s, delta_s, dq_s, send_sems, recv_sems,
):
    group = lax.axis_index("grp")
    place = lax.axis_index("seq")
    sems = (send_sems, recv_sems)
    heads = packs.shape[0]
    rows = 2 * packs.shape[2]
    scale = 1.0 / math.sqrt(HD)
    ahead = lambda s: (place + s) % 4
    behind = lambda s: (place + 4 - s) % 4
    stores = (q_s, k_s, v_s, do_s, delta_s)

    def first(s):
        return reach(gatt.at[2 * ahead(s)], dos.at[0, s], sems, s - 1, 1, ahead(s))

    def second(s):
        return reach(gatt.at[2 * ahead(s) + 1], dos.at[1, s], sems, 2 + s, 1, ahead(s))

    def cross(s):
        return reach(gatt.at[8 + ahead(s)], crossed.at[s], sems, 6 + s, 0, place)

    def onward(s):
        return reach(crossed.at[s], dos.at[1, s], sems, 9 + s, 0, ahead(s))

    def home_values(kind, s, head):
        source = staged.at[min(kind, 1), s, pl.ds(1, 2)]
        return reach(
            source, back.at[head, pl.ds(1, 2)], sems, (13, 17, 21)[kind] + s, 1, behind(s)
        )

    def home_queries(kind, s, head):
        source = staged.at[min(kind, 1), s, 0]
        return reach(source, back.at[head, 0], sems, (25, 29, 33)[kind] + s, 1, behind(s))

    greet(group, place)

    def full(sel, put_values, put_queries):
        for s in range(4):
            load_backward(
                pieces.at[sel, s], dos[sel, s], results[sel, s], s * rows, *stores
            )

        def step(s, carry):
            block = pl.ds(pl.multiple_of(s * rows, rows), rows)
            k = k_s[block, :]
            v = v_s[block, :]
            dk = dv = None
            for index in range(4):
                chunk = slice(index * rows, (index + 1) * rows)
                dq, dk_part, dv_part = tile_grads(
                    q_s[chunk, :], do_s[chunk, :], k, v, logs[sel, index, 0:1, :],
                    delta_s[0:1, chunk],
                )
                dk = dk_part if dk is None else dk + dk_part
                dv = dv_part if dv is None else dv + dv_part
                dq_s[:, chunk] = jnp.where(s == 0, dq, dq_s[:, chunk] + dq)
            staged[sel, s, 1] = fold(dk * scale).astype(BF16)
            staged[sel, s, 2] = fold(dv).astype(BF16)
            put_values(s)
            return carry

        lax.fori_loop(0, 4, step, 0)
        for s in (3, 2, 1, 0):
            chunk = slice(s * rows, (s + 1) * rows)
            staged[sel, s, 0] = fold(dq_s[:, chunk].T * scale).astype(BF16)
            put_queries(s)

    @pl.when(group == 1)
    def _():
        for s in (1, 2, 3):
            first(s).start()
        for s in (1, 2, 3, 0):
            cross(s).start()
        for s in (1, 2, 3):
            second(s).start()
        dos[0, 0] = gatt[2 * place]
        dos[1, 0] = gatt[2 * place + 1]
        for s in (1, 2, 3):
            first(s).wait_recv()
        head = 2 * place

        def put_values(s):
            @pl.when(s == 0)
            def _():
                back[head, 1] = staged[0, 0, 1]
                back[head, 2] = staged[0, 0, 2]

            @pl.when(s > 0)
            def _():
                home_values(0, s, head).start()

        def put_queries(s):
            if s == 0:
                back[head, 0] = staged[0, 0, 0]
            else:
                home_queries(0, s, head).start()

        full(0, put_values, put_queries)
        for s in (1, 2, 3):
            second(s).wait_recv()

    @pl.when(group == 0)
    def _():
        for s in (1, 2, 3):
            cross(s).wait_recv()
            onward(s).start()
        cross(0).wait_recv()
        dos[1, 0] = crossed[0]
        for s in (1, 2, 3):
            onward(s).wait_recv()

    def put_values(s):
        head = 2 * place + 1

        @pl.when((group == 1) & (s == 0))
        def _():
            back[head, 1] = staged[1, 0, 1]
            back[head, 2] = staged[1, 0, 2]

        @pl.when((group == 1) & (s > 0))
        def _():
            home_values(1, s, head).start()

        @pl.when(group == 0)
        def _():
            home_values(2, s, 8 + place).start()

    def put_queries(s):
        head = 2 * place + 1

        @pl.when(group == 1)
        def _():
            if s == 0:
                back[head, 0] = staged[1, 0, 0]
            else:
                home_queries(1, s, head).start()

        @pl.when(group == 0)
        def _():
            home_queries(2, s, 8 + place).start()

    full(1, put_values, put_queries)

    @pl.when(group == 0)
    def _():
        def local(head, carry):
            load_backward(packs.at[head], gatt[head], att[head], 0, *stores)
            own = slice(0, rows)
            dq, dk, dv = tile_grads(
                q_s[own, :], do_s[own, :], k_s[own, :], v_s[own, :],
                logs_own[head, 0:1, :], delta_s[0:1, own],
            )
            back[head, 0] = fold(dq.T * scale).astype(BF16)
            back[head, 1] = fold(dk * scale).astype(BF16)
            back[head, 2] = fold(dv).astype(BF16)
            return carry

        lax.fori_loop(0, heads, local, 0)
        for s in (1, 2, 3):
            onward(s).wait_send()
        for s in range(4):
            home_values(2, s, 8 + place).wait_send()
            home_queries(2, s, 8 + place).wait_send()

    @pl.when(group == 1)
    def _():
        for s in (1, 2, 3):
            first(s).wait_send()
            second(s).wait_send()
            for kind in (0, 1):
                home_values(kind, s, 2 * place + kind).wait_send()
                home_queries(kind, s, 2 * place + kind).wait_send()
        for s in range(4):
            cross(s).wait_send()
        for s in (1, 2, 3):
            for kind in (0, 1):
                home_values(kind, s, 2 * ahead(s) + kind).wait_recv()
                home_queries(kind, s, 2 * ahead(s) + kind).wait_recv()
        for s in range(4):
            home_values(2, s, 8 + ahead(s)).wait_recv()
            home_queries(2, s, 8 + ahead(s)).wait_recv()


def backward_attention(packs, gatt, att, pieces, results, logs, logs_own):
    heads, _, half, lanes = packs.shape
    return pl.pallas_call(
        backward_kernel,
        in_specs=in_vmem(7),
        out_specs=pl.BlockSpec(memory_space=pltpu.VMEM),
        out_shape=jax.ShapeDtypeStruct((heads, 3, half, lanes), BF16),
        scratch_shapes=[
            pltpu.VMEM((2, 4, half, lanes), BF16),
            pltpu.VMEM((4, half, lanes), BF16),
            pltpu.VMEM((2, 4, 3, half, lanes), BF16),
        ]
        + [pltpu.VMEM((8 * half, lanes), BF16)] * 4
        + [
            pltpu.VMEM((8, 8 * half), F32),
            pltpu.VMEM((lanes, 8 * half), F32),
            pltpu.SemaphoreType.DMA((37,)),
            pltpu.SemaphoreType.DMA((37,)),
        ],
        compiler_params=pltpu.CompilerParams(
            collective_id=2, has_side_effects=True, vmem_limit_bytes=WHOLE_VMEM
        ),
        cost_estimate=pl.CostEstimate(
            flops=120_000_000_000, bytes_accessed=8_000_000, transcendentals=0
        ),
        name="backward_attention",
    )(packs, gatt, att, pieces, results, logs, logs_own)


def whole(shape):
    zeros = (0,) * len(shape)
    return pl.BlockSpec(shape, lambda *_: zeros)


def middle_kernel(
    x_ref, cot_ref, att_ref, vec_ref, ow_ref, feed_ref,
    out_ref, attlow_ref, hidden_ref, act_ref, gfeed_ref, gpre_ref, mgrad_ref, gbranch_ref,
    gatt_ref, sums_ref, upsum_ref, att_s, slope_s,
):
    step = pl.program_id(0)
    rows, width = x_ref.shape[1:]
    both = 2 * rows
    pairs = width // (2 * HD)
    gate_one, gain, scale, shift = (vec_ref[i : i + 1, :] for i in range(4))
    gate_two, down_bias = vec_ref[4:5, :], vec_ref[5:6, :]
    for pair in range(pairs):
        lanes = slice(pair * 2 * HD, (pair + 1) * 2 * HD)
        top, bottom = exchange(
            att_ref[2 * pair].astype(F32), att_ref[2 * pair + 1].astype(F32)
        )
        att_s[:rows, lanes] = top.astype(BF16)
        att_s[rows:, lanes] = bottom.astype(BF16)
    att = att_s[...]
    attlow_ref[...] = att.reshape(2, rows, width)
    branch = jnp.dot(att, ow_ref[...], preferred_element_type=F32)
    middle = x_ref[...].reshape(both, width).astype(F32) + gate_one * branch
    n, inverse = normalise(middle)
    hidden = (n * gain * (1.0 + scale) + shift).astype(BF16)
    hidden_ref[...] = hidden.reshape(2, rows, width)
    shares, _, chunk = feed_ref.shape
    feed = None
    for index in range(shares):
        cols = slice(index * chunk, (index + 1) * chunk)
        pre = jnp.dot(hidden, feed_ref[index, :width], preferred_element_type=F32)
        pre = pre + feed_ref[index, 2 * width : 2 * width + 1].astype(F32)
        square = pre * pre
        root = math.sqrt(2.0 / math.pi)
        tanh = jnp.tanh(pre * (root + (root * 0.044715) * square))
        half_up = 0.5 + 0.5 * tanh
        act = (pre * half_up).astype(BF16)
        slope_s[:, cols] = half_up + (0.5 * pre) * (1.0 - tanh * tanh) * (
            root + (3.0 * root * 0.044715) * square
        )
        act_ref[:, :, cols] = act.reshape(2, rows, chunk)
        part = jnp.dot(act, feed_ref[index, width : 2 * width], preferred_element_type=F32)
        feed = part if feed is None else feed + part
    feed = feed + down_bias
    out_ref[...] = (middle + gate_two * feed).astype(BF16).reshape(2, rows, width)
    cot = cot_ref[...].reshape(both, width).astype(F32)
    gfeed = (gate_two * cot).astype(BF16)
    gfeed_ref[...] = gfeed.reshape(2, rows, width)
    ghidden = None
    up_sums = []
    for index in range(shares):
        cols = slice(index * chunk, (index + 1) * chunk)
        gact = lax.dot_general(
            gfeed, feed_ref[index, width : 2 * width], NT, preferred_element_type=F32
        )
        gpre = (gact * slope_s[:, cols]).astype(BF16)
        gpre_ref[:, :, cols] = gpre.reshape(2, rows, chunk)
        up_sums.append(jnp.sum(gpre.astype(F32), axis=0, keepdims=True))
        part = lax.dot_general(gpre, feed_ref[index, :width], NT, preferred_element_type=F32)
        ghidden = part if ghidden is None else ghidden + part
    e = ghidden * ((1.0 + scale) * gain)
    mgrad = cot + inverse * (
        e - jnp.mean(e, axis=-1, keepdims=True) - n * jnp.mean(e * n, axis=-1, keepdims=True)
    )
    mgrad_ref[...] = mgrad.reshape(2, rows, width)
    gbranch = (gate_one * mgrad).astype(BF16)
    gbranch_ref[...] = gbranch.reshape(2, rows, width)
    gatt = lax.dot_general(gbranch, ow_ref[...], NT, preferred_element_type=F32)
    for pair in range(pairs):
        value = gatt[:, pair * 2 * HD : (pair + 1) * 2 * HD]
        even, odd = exchange(value[:rows], value[rows:])
        gatt_ref[2 * pair] = even.astype(BF16)
        gatt_ref[2 * pair + 1] = odd.astype(BF16)
    add = lambda value: jnp.sum(value, axis=0, keepdims=True)

    @pl.when(step == 0)
    def _():
        sums_ref[...] = jnp.zeros_like(sums_ref)
        upsum_ref[...] = jnp.zeros_like(upsum_ref)

    sums_ref[0:1, :] += add(ghidden)
    sums_ref[1:2, :] += add(ghidden * n)
    sums_ref[2:3, :] += add(cot * feed)
    sums_ref[3:4, :] += add(gfeed.astype(F32))
    sums_ref[4:5, :] += add(mgrad * branch)
    for index, value in enumerate(up_sums):
        upsum_ref[0:1, index * chunk : (index + 1) * chunk] += value


def once(shape):
    zeros = (0,) * len(shape)
    return pl.BlockSpec(shape, lambda *_: zeros, pipeline_mode=pl.Buffered(1))


def middle_pass(x2, cot2, att, vecs, out_weight, feed_weights, rows=128):
    half, width = x2.shape[1:]
    heads = width // HD
    units = feed_weights.shape[0] * feed_weights.shape[2]
    tok = lambda last: pl.BlockSpec((2, rows, last), lambda i: (0, i, 0))
    pack = pl.BlockSpec((heads, rows, 2 * HD), lambda i: (0, i, 0))
    token = lambda last, kind: jax.ShapeDtypeStruct((2, half, last), kind)
    return pl.pallas_call(
        middle_kernel,
        grid=(half // rows,),
        in_specs=[
            tok(width), tok(width), pack, whole(vecs.shape), once(out_weight.shape),
            once(feed_weights.shape),
        ],
        out_specs=[
            tok(width), tok(width), tok(width), tok(units), tok(width), tok(units), tok(width),
            tok(width), pack, whole((8, width)), whole((8, units)),
        ],
        out_shape=[
            token(width, BF16), token(width, BF16), token(width, BF16), token(units, BF16),
            token(width, BF16), token(units, BF16), token(width, F32), token(width, BF16),
            jax.ShapeDtypeStruct((heads, half, 2 * HD), BF16),
            jax.ShapeDtypeStruct((8, width), F32),
            jax.ShapeDtypeStruct((8, units), F32),
        ],
        scratch_shapes=[pltpu.VMEM((2 * rows, width), BF16), pltpu.VMEM((2 * rows, units), F32)],
        compiler_params=params("arbitrary"),
        name="middle_pass",
    )(x2, cot2, att, vecs, out_weight, feed_weights)


def unrotate_kernel(pack_ref, cos_ref, sin_ref, mixed_ref):
    rows = cos_ref.shape[1]
    cosine = cos_ref[...].reshape(2 * rows, 2 * HD)
    sine = -sin_ref[...].reshape(2 * rows, 2 * HD)
    heads = pack_ref.shape[0]
    width = heads * HD
    for part in range(3):
        for pair in range(heads // 2):
            top, bottom = exchange(
                pack_ref[2 * pair, part].astype(F32), pack_ref[2 * pair + 1, part].astype(F32)
            )
            value = jnp.concatenate([top, bottom], axis=0)
            if part < 2:
                value = turn(value, cosine, sine)
            start = part * width + pair * 2 * HD
            mixed_ref[:, :, start : start + 2 * HD] = value.astype(BF16).reshape(2, rows, 2 * HD)


def unrotate(packs, cosine, sine, rows=128):
    heads, _, half, lanes = packs.shape
    tok = lambda last: pl.BlockSpec((2, rows, last), lambda i: (0, i, 0))
    return pl.pallas_call(
        unrotate_kernel,
        grid=(half // rows,),
        in_specs=[
            pl.BlockSpec((heads, 3, rows, lanes), lambda i: (0, 0, i, 0)),
            tok(lanes),
            tok(lanes),
        ],
        out_specs=tok(3 * heads * HD),
        out_shape=jax.ShapeDtypeStruct((2, half, 3 * heads * HD), BF16),
        compiler_params=params("arbitrary"),
        name="unrotate",
    )(packs, cosine, sine)


def input_kernel(mixed_ref, w_ref, x_ref, mgrad_ref, vec_ref, grad_ref, sums_ref):
    step = pl.program_id(0)
    rows, width = x_ref.shape[1:]
    both = 2 * rows
    gnormed = lax.dot_general(
        mixed_ref[...].reshape(both, mixed_ref.shape[2]), w_ref[...], NT,
        preferred_element_type=F32,
    )
    n, inverse = normalise(x_ref[...].reshape(both, width).astype(F32))
    e = gnormed * ((1.0 + vec_ref[1:2, :]) * vec_ref[0:1, :])
    grad = mgrad_ref[...].reshape(both, width) + inverse * (
        e - jnp.mean(e, axis=-1, keepdims=True) - n * jnp.mean(e * n, axis=-1, keepdims=True)
    )
    grad_ref[...] = grad.reshape(2, rows, width)

    @pl.when(step == 0)
    def _():
        sums_ref[...] = jnp.zeros_like(sums_ref)

    sums_ref[0:1, :] += jnp.sum(gnormed, axis=0, keepdims=True)
    sums_ref[1:2, :] += jnp.sum(gnormed * n, axis=0, keepdims=True)


def input_pass(mixed, weight, x2, mgrad, vecs, rows=128):
    half, width = x2.shape[1:]
    tok = lambda last: pl.BlockSpec((2, rows, last), lambda i: (0, i, 0))
    return pl.pallas_call(
        input_kernel,
        grid=(half // rows,),
        in_specs=[
            tok(mixed.shape[2]), once(weight.shape), tok(width), tok(width), whole(vecs.shape)
        ],
        out_specs=[tok(width), whole((8, width))],
        out_shape=[
            jax.ShapeDtypeStruct((2, half, width), F32),
            jax.ShapeDtypeStruct((8, width), F32),
        ],
        compiler_params=params("arbitrary"),
        cost_estimate=pl.CostEstimate(
            flops=6_000_000_000, bytes_accessed=20_000_000, transcendentals=0
        ),
        name="input_pass",
    )(mixed, weight, x2, mgrad, vecs)


def weight_grads_kernel(
    pick_ref, hidden_ref, gfeed_ref, att_ref, gbranch_ref, act_ref, gpre_ref, out_ref,
    hidden_s, gfeed_s, att_s,
):
    step = pl.program_id(0)

    @pl.when(step == 0)
    def _():
        hidden_s[...] = hidden_ref[...].T
        gfeed_s[...] = gfeed_ref[...].T
        att_s[...] = att_ref[...].T

    width = hidden_s.shape[0]
    split = width // 4
    part = split // 4
    up = jnp.dot(hidden_s[...], gpre_ref[...], preferred_element_type=F32).astype(BF16)
    down = jnp.dot(gfeed_s[...], act_ref[...], preferred_element_type=F32).astype(BF16)
    offset = pick_ref[step] * part
    rows = jnp.concatenate(
        [
            att_s[pl.ds(pl.multiple_of(offset + index * split, 16), part), :]
            for index in range(4)
        ]
    )
    out = jnp.dot(rows, gbranch_ref[...], preferred_element_type=F32).astype(BF16)
    for index in range(4):
        out_ref[0, index, :split] = up[index * split : (index + 1) * split]
        out_ref[0, index, split : 2 * split] = down[index * split : (index + 1) * split]
        out_ref[0, index, 2 * split :] = out[index * part : (index + 1) * part]


def weight_grads(picked, hidden, gfeed, att, gbranch, act, gpre):
    tokens, width = hidden.shape
    block = pl.BlockSpec((tokens, act.shape[1] // 4), lambda i, p: (0, p[i]))
    shape = (2, 4, width // 2 + width // 16, width)
    return pl.pallas_call(
        weight_grads_kernel,
        grid_spec=pltpu.PrefetchScalarGridSpec(
            num_scalar_prefetch=1,
            grid=(2,),
            in_specs=[once(hidden.shape)] * 4 + [block, block],
            out_specs=pl.BlockSpec((1,) + shape[1:], lambda i, p: (i, 0, 0, 0)),
            scratch_shapes=[pltpu.VMEM((width, tokens), BF16)] * 3,
        ),
        out_shape=jax.ShapeDtypeStruct(shape, BF16),
        compiler_params=params("arbitrary"),
        cost_estimate=pl.CostEstimate(
            flops=6_000_000_000, bytes_accessed=20_000_000, transcendentals=0
        ),
        name="weight_grads",
    )(picked, hidden, gfeed, att, gbranch, act, gpre)


def swapped(value, axis, bit):
    count = lax.axis_size(axis)
    return lax.ppermute(value, axis, [(place, place ^ bit) for place in range(count)])


def wide(value):
    return value.astype(F32)


def over_cores(sent, kept):
    return (wide(kept) + wide(swapped(sent, "mlp", 1))).astype(BF16)


def over_rows(value, row):
    other = swapped(pick(value, 1 - row), "mlp", 2)
    return (wide(pick(value, row)) + wide(other)).astype(BF16)


def over_places(value, place):
    total = wide(pick(value, place))
    for steps in (1, 2, 3):
        total = total + wide(along(pick(value, (place + steps) % 4), steps))
    return total.astype(BF16)


def over_groups(value):
    return wide(value) + wide(swapped(value, "grp", 1))


def tie(*values):
    return lax.optimization_barrier(values)


def along(value, steps):
    pairs = [(place, (place + steps) % 4) for place in range(4)]
    return lax.ppermute(value, "seq", pairs)


def pick(stack, index):
    return lax.dynamic_index_in_dim(stack, index, 0, keepdims=False)


def four_shards(
    tokens, step_index, time_table, ada_weight, ada_bias, first_gain, qkv_weight, out_weight,
    second_gain, up_weight, up_bias, down_weight, down_bias, cotangent,
):
    place = lax.axis_index("seq")
    group = lax.axis_index("grp")
    mlp_count = lax.axis_size("mlp")
    second = group == 1
    token_rows, width = tokens.shape[1:]
    half = token_rows // 2
    heads = width // HD
    slot = lambda steps: (place + steps) % 4
    group_row = jnp.full((1,), group, jnp.int32)

    share_units = up_weight.shape[1]
    bias_rows = jnp.broadcast_to(up_bias[None, :], (16, share_units))
    feed_weights = lax.all_gather(
        jnp.concatenate([up_weight, down_weight, bias_rows]), "mlp", axis=0
    )

    step_value = jnp.sum(jnp.where(jnp.arange(4, dtype=jnp.int32) == place, step_index[0], 0))
    embedded = lax.dynamic_slice_in_dim(time_table, step_value, 1, 0)[0].astype(F32)
    condition, silu_back = jax.vjp(jax.nn.silu, embedded)
    cond_low = condition.astype(BF16)
    modulation = jnp.dot(cond_low[None, :], ada_weight, preferred_element_type=F32)[
        0
    ] + ada_bias.astype(F32)
    shift_one, scale_one, gate_one, shift_two, scale_two, gate_two = jnp.split(modulation, 6)

    positions = jnp.arange(token_rows, dtype=jnp.int32) + jnp.where(second, place * token_rows, 0)
    frequency = jnp.exp(jnp.arange(HD // 2, dtype=F32) * (-2.0 * math.log(10000.0) / HD))
    angles = positions.astype(F32)[:, None] * frequency[None, :]
    cosine, sine = jnp.cos(angles), jnp.sin(angles)
    cosine = jnp.concatenate([cosine] * 4, axis=1).reshape(2, half, 2 * HD)
    sine = jnp.concatenate([-sine, sine] * 2, axis=1).reshape(2, half, 2 * HD)

    x2 = tokens.reshape(2, half, width)
    blank = jnp.zeros((width,), F32)
    gain_one = first_gain.astype(F32)
    gain_two = second_gain.astype(F32)
    vec_one = jnp.stack([gain_one, scale_one, shift_one] + [blank] * 5)
    vec_two = jnp.stack(
        [gate_one, gain_two, scale_two, shift_two, gate_two, down_bias.astype(F32), blank, blank]
    )
    normed, packs = project(x2, vec_one, qkv_weight, cosine, sine)

    att, pieces, results, logs, logs_own = forward_attention(packs)
    (
        output, att_low, hidden, act, grad_feed, grad_pre, middle_grad, grad_branch, grad_att,
        middle_sums, up_sums,
    ) = middle_pass(
        x2, cotangent.reshape(2, half, width), att, vec_two, out_weight, feed_weights
    )
    flat = lambda value: value.reshape(token_rows, value.shape[2])
    core = lax.axis_index("mlp") % 2
    row = lax.axis_index("mlp") // 2
    factors = tuple(
        flat(value) for value in (hidden, grad_feed, att_low, grad_branch, act, grad_pre)
    )
    feed_sent = weight_grads(jnp.stack([1 - core, 3 - core]).astype(jnp.int32), *factors)
    feed_kept = weight_grads(jnp.stack([core, 2 + core]).astype(jnp.int32), *factors)
    feed = over_cores(feed_sent, feed_kept)

    feed, grad_att = tie(feed, grad_att)
    feed = over_rows(feed, row)
    grads = backward_attention(packs, grad_att, att, pieces, results, logs, logs_own)
    feed, grads = tie(feed, grads)
    feed = over_places(feed, place)
    feed_total = over_groups(feed)
    mixed_grad = unrotate(grads, cosine, sine)
    blocks = flat(normed).T.reshape(4, 2, 2, width // 16, token_rows)
    blocks = jnp.transpose(blocks, (2, 1, 0, 3, 4)).reshape(2, width // 2, token_rows)
    project_back = lambda part: jnp.dot(
        part, flat(mixed_grad), preferred_element_type=F32
    ).astype(BF16).reshape(2, 4, width // 16, 3 * width)
    qkv = over_cores(
        project_back(pick(blocks, 1 - core)), project_back(pick(blocks, core))
    )
    qkv_total = over_groups(over_places(over_rows(qkv, row), place))
    input_grad, input_sums = input_pass(mixed_grad, qkv_weight, x2, middle_grad, vec_one)

    shift_one_grad = input_sums[0]
    first_gain_grad = (1.0 + scale_one) * input_sums[1]
    scale_one_grad = gain_one * input_sums[1]
    shift_two_grad = middle_sums[0]
    second_gain_grad = (1.0 + scale_two) * middle_sums[1]
    scale_two_grad = gain_two * middle_sums[1]
    mod_grad = jnp.concatenate(
        [
            shift_one_grad, scale_one_grad, middle_sums[4], shift_two_grad, scale_two_grad,
            middle_sums[2],
        ]
    )
    cond_grad = jnp.dot(ada_weight.astype(F32), mod_grad, precision=highest)
    table_row = silu_back(cond_grad)[0]
    cond_size = condition.shape[0]
    small = jnp.concatenate(
        [
            mod_grad, first_gain_grad, second_gain_grad, up_sums[0], middle_sums[3],
            table_row, condition, jnp.full((cond_size,), step_value, F32),
        ]
    )
    small_all = lax.all_gather(small, ("grp", "seq", "mlp"), axis=0)
    rank = place * mlp_count + lax.axis_index("mlp")
    ranks = 4 * mlp_count

    def share(start, size):
        each = size // ranks
        return lax.dynamic_slice_in_dim(small_all, start + rank * each, each, 1)

    mod_size = 6 * width
    units = share_units * mlp_count
    mod_share = share(0, mod_size)
    start = mod_size
    first_share = jnp.sum(share(start, width), axis=0)
    start += width
    second_share = jnp.sum(share(start, width), axis=0)
    start += width
    up_bias_share = jnp.sum(share(start, units), axis=0)
    start += units
    down_bias_share = jnp.sum(share(start, width), axis=0)
    start += width
    rows_all = small_all[:, start : start + cond_size]
    cond_all = small_all[:, start + cond_size : start + 2 * cond_size].astype(BF16).astype(F32)
    steps_all = small_all[:, start + 2 * cond_size].astype(jnp.int32)
    ada_share = lax.dot_general(cond_all, mod_share, TN, precision=highest)
    table_each = time_table.shape[0] // ranks
    own_rows = rank * table_each + jnp.arange(table_each, dtype=jnp.int32)
    chosen = (own_rows[:, None] == steps_all[None, :]).astype(F32)
    table_share = jnp.dot(chosen, rows_all, precision=highest)

    split = width // 4
    up_total = feed_total[:split]
    down_total = feed_total[split : 2 * split].T
    out_total = feed_total[2 * split :]
    return (
        output.reshape(1, token_rows, width),
        input_grad.reshape(1, token_rows, width),
        table_share,
        ada_share,
        jnp.sum(mod_share, axis=0),
        first_share,
        qkv_total,
        out_total,
        second_share,
        up_total,
        up_bias_share,
        down_total,
        down_bias_share,
    )


def solution(mesh):
    in_specs = (
        P(("grp", "mlp"), "seq", None),
        P(("grp", "mlp"), None),
        P(),
        P(),
        P(),
        P(),
        P(),
        P(),
        P(),
        P(None, "mlp"),
        P("mlp"),
        P("mlp", None),
        P(),
        P(("grp", "mlp"), "seq", None),
    )
    out_specs = (
        P(("grp", "mlp"), "seq", None),
        P(("grp", "mlp"), "seq", None),
        P(("seq", "mlp"), None),
        P(None, ("seq", "mlp")),
        P(("seq", "mlp")),
        P(("seq", "mlp")),
        P(("seq", "mlp"), None),
        P(("seq", "mlp"), None),
        P(("seq", "mlp")),
        P("seq", "mlp"),
        P(("seq", "mlp")),
        P("mlp", "seq"),
        P(("seq", "mlp")),
    )
    body = four_shards if mesh.shape["seq"] == 4 and mesh.shape["grp"] == 2 else shards
    return jax.shard_map(body, mesh=mesh, in_specs=in_specs, out_specs=out_specs, check_vma=False)
```

```python
import math

import jax
import jax.numpy as jnp
from jax import lax
from jax.experimental import pallas as pl
from jax.experimental.pallas import tpu as pltpu
from jax.sharding import PartitionSpec as P

HD = 64


highest = lax.Precision.HIGHEST


def shifted(value, axis, steps):
    count = lax.axis_size(axis)
    pairs = [(source, (source + steps) % count) for source in range(count)]
    return lax.ppermute(value, axis, pairs)


def layer_norm(values, norm_gain):
    centred = values - jnp.mean(values, axis=-1, keepdims=True)
    spread = jnp.mean(centred * centred, axis=-1, keepdims=True)
    return centred * lax.rsqrt(spread + 1e-05) * norm_gain


def modulate(values, norm_gain, shift_part, scale_part):
    return layer_norm(values, norm_gain) * (1.0 + scale_part) + shift_part


def gelu_tanh(values):
    return jax.nn.gelu(values, approximate=True)


def rotate_pairs(values, positions):
    half_dim = HD // 2
    frequency = jnp.exp(jnp.arange(half_dim, dtype=jnp.float32) * (-2.0 * math.log(10000.0) / HD))
    angles = positions.astype(jnp.float32)[:, None] * frequency[None, :]
    cosine = jnp.cos(angles)[:, None, :]
    sine_part = jnp.sin(angles)[:, None, :]
    leading = values[..., :half_dim]
    trailing = values[..., half_dim:]
    return jnp.concatenate(
        [leading * cosine - trailing * sine_part, trailing * cosine + leading * sine_part], axis=-1
    )


def shards(
    tokens,
    step_index,
    time_table,
    ada_weight,
    ada_bias,
    first_gain,
    qkv_weight,
    out_weight,
    second_gain,
    up_weight,
    up_bias,
    down_weight,
    down_bias,
    cotangent,
):
    seq_count = lax.axis_size("seq")
    seq_place = lax.axis_index("seq")
    group_index = lax.axis_index("grp")
    mlp_place = lax.axis_index("mlp")
    tok_rows = tokens.shape[1]
    model_width = tokens.shape[2]
    head_count = model_width // HD
    score_scale = 1.0 / math.sqrt(HD)
    line_len = tok_rows * seq_count
    seq_length = jnp.where(group_index == 0, line_len // 4, line_len).astype(jnp.int32)
    row_ids = jnp.arange(tok_rows, dtype=jnp.int32)
    own_pos = seq_place * tok_rows + row_ids
    positions = own_pos % seq_length
    quarter = seq_place // (seq_count // 4)
    step_value = jnp.sum(jnp.where(jnp.arange(4, dtype=jnp.int32) == quarter, step_index[0], 0))
    table_pick = jnp.arange(time_table.shape[0], dtype=jnp.int32) == step_value
    embedded = jnp.dot(
        table_pick.astype(jnp.bfloat16)[None, :], time_table, preferred_element_type=jnp.float32
    )[0]
    condition, silu_back = jax.vjp(jax.nn.silu, embedded)
    cond_low = condition.astype(jnp.bfloat16)
    modulation = jnp.dot(cond_low[None, :], ada_weight, preferred_element_type=jnp.float32)[
        0
    ] + ada_bias.astype(jnp.float32)
    shift_one, scale_one, gate_one, shift_two, scale_two, gate_two = jnp.split(modulation, 6)
    inputs = tokens[0].astype(jnp.float32)
    normed, first_back = jax.vjp(
        modulate, inputs, first_gain.astype(jnp.float32), shift_one, scale_one
    )
    normed_low = normed.astype(jnp.bfloat16)
    mixed_rows = jnp.dot(normed_low, qkv_weight, preferred_element_type=jnp.float32)

    def rotate_all(mixed_in):
        query_part = rotate_pairs(
            mixed_in[:, :model_width].reshape(tok_rows, head_count, HD), positions
        )
        key_part = rotate_pairs(
            mixed_in[:, model_width : 2 * model_width].reshape(tok_rows, head_count, HD), positions
        )
        return (
            query_part,
            key_part,
            mixed_in[:, 2 * model_width :].reshape(tok_rows, head_count, HD),
        )

    rotated, rotate_back = jax.vjp(rotate_all, mixed_rows)
    queries = rotated[0].astype(jnp.bfloat16)
    key_rows = rotated[1].astype(jnp.bfloat16)
    value_rows = rotated[2].astype(jnp.bfloat16)
    start_state = (
        jnp.full((head_count, tok_rows), -1e30, jnp.float32),
        jnp.zeros((head_count, tok_rows), jnp.float32),
        jnp.zeros((head_count, tok_rows, HD), jnp.float32),
    )
    key_piece = lax.all_gather(key_rows.reshape(tok_rows, model_width), "seq", axis=0, tiled=True)
    value_piece = lax.all_gather(
        value_rows.reshape(tok_rows, model_width), "seq", axis=0, tiled=True
    )
    piece_rows = key_piece.shape[0]
    sub_rows = math.gcd(piece_rows, 512)

    def one_block(block_index, block_state):
        run_max, run_total, run_acc = block_state
        offset = block_index * sub_rows
        key_block = lax.dynamic_slice_in_dim(key_piece, offset, sub_rows, 0).reshape(
            sub_rows, head_count, HD
        )
        value_block = lax.dynamic_slice_in_dim(value_piece, offset, sub_rows, 0).reshape(
            sub_rows, head_count, HD
        )
        key_pos = offset + jnp.arange(sub_rows, dtype=jnp.int32)
        same_seq = (own_pos // seq_length)[:, None] == (key_pos // seq_length)[None, :]
        scores = (
            jnp.einsum("qhd,khd->hqk", queries, key_block, preferred_element_type=jnp.float32)
            * score_scale
        )
        masked = jnp.where(same_seq[None], scores, -1e30)
        new_max = jnp.maximum(run_max, jnp.max(masked, axis=-1))
        shrink = jnp.exp(run_max - new_max)
        weights = jnp.where(same_seq[None], jnp.exp(masked - new_max[..., None]), 0.0)
        run_total = run_total * shrink + jnp.sum(weights, axis=-1)
        run_acc = run_acc * shrink[..., None] + jnp.einsum(
            "hqk,khd->hqd",
            weights.astype(jnp.bfloat16),
            value_block,
            preferred_element_type=jnp.float32,
        )
        return (new_max, run_total, run_acc)

    run_max, run_total, run_acc = lax.fori_loop(0, piece_rows // sub_rows, one_block, start_state)
    log_total = run_max + jnp.log(run_total)
    attended3 = jnp.transpose(run_acc / run_total[..., None], (1, 0, 2))
    attended_low = attended3.reshape(tok_rows, model_width).astype(jnp.bfloat16)
    branch = jnp.dot(attended_low, out_weight, preferred_element_type=jnp.float32)
    middle = inputs + gate_one * branch
    hidden, second_back = jax.vjp(
        modulate, middle, second_gain.astype(jnp.float32), shift_two, scale_two
    )
    hidden_low = hidden.astype(jnp.bfloat16)
    gathered = lax.all_gather(hidden_low, "mlp", axis=0, tiled=True)
    pre_act = jnp.dot(gathered, up_weight, preferred_element_type=jnp.float32) + up_bias.astype(
        jnp.float32
    )
    activated, gelu_back = jax.vjp(gelu_tanh, pre_act)
    act_low = activated.astype(jnp.bfloat16)
    feed_terms = jnp.dot(act_low, down_weight, preferred_element_type=jnp.float32)
    feed_out = lax.psum_scatter(
        feed_terms, "mlp", scatter_dimension=0, tiled=True
    ) + down_bias.astype(jnp.float32)
    output = (middle + gate_two * feed_out).astype(jnp.bfloat16)[None]
    grad_out = cotangent[0].astype(jnp.float32)
    gate_two_grad = jnp.sum(grad_out * feed_out, axis=0)
    grad_feed = (gate_two * grad_out).astype(jnp.bfloat16)
    down_bias_grad = jnp.sum(grad_feed, axis=0, dtype=jnp.float32)
    grad_rows = lax.all_gather(grad_feed, "mlp", axis=0, tiled=True)
    down_grad = jnp.einsum("tf,td->fd", act_low, grad_rows, preferred_element_type=jnp.float32)
    grad_act = jnp.einsum("td,fd->tf", grad_rows, down_weight, preferred_element_type=jnp.float32)
    grad_pre = gelu_back(grad_act)[0].astype(jnp.bfloat16)
    up_grad = jnp.einsum("td,tf->df", gathered, grad_pre, preferred_element_type=jnp.float32)
    local_units = up_weight.shape[1]
    bias_slot = lax.dynamic_update_slice_in_dim(
        jnp.zeros((local_units * lax.axis_size("mlp"),), jnp.float32),
        jnp.sum(grad_pre, axis=0, dtype=jnp.float32),
        mlp_place * local_units,
        0,
    )
    hidden_terms = jnp.einsum("tf,df->td", grad_pre, up_weight, preferred_element_type=jnp.float32)
    grad_hidden = lax.psum_scatter(hidden_terms, "mlp", scatter_dimension=0, tiled=True)
    middle_part, second_gain_grad, shift_two_grad, scale_two_grad = second_back(grad_hidden)
    middle_grad = grad_out + middle_part
    gate_one_grad = jnp.sum(middle_grad * branch, axis=0)
    grad_branch = (gate_one * middle_grad).astype(jnp.bfloat16)
    out_grad = jnp.einsum(
        "td,te->de", attended_low, grad_branch, preferred_element_type=jnp.float32
    )
    grad_attended = jnp.einsum(
        "te,de->td", grad_branch, out_weight, preferred_element_type=jnp.float32
    ).astype(jnp.bfloat16)
    grad_heads = grad_attended.reshape(tok_rows, head_count, HD)
    row_delta = jnp.transpose(jnp.sum(grad_heads.astype(jnp.float32) * attended3, axis=-1))

    def pair_grads(
        query_set, grad_set, total_set, delta_set, query_anchor, key_set, value_set, key_anchor
    ):
        query_pos = query_anchor * tok_rows + row_ids
        key_pos = key_anchor * tok_rows + row_ids
        same_seq = (query_pos // seq_length)[:, None] == (key_pos // seq_length)[None, :]
        scores = (
            jnp.einsum("qhd,khd->hqk", query_set, key_set, preferred_element_type=jnp.float32)
            * score_scale
        )
        prob_rows = jnp.where(same_seq[None], jnp.exp(scores - total_set[..., None]), 0.0)
        value_part = jnp.einsum(
            "hqk,qhd->khd",
            prob_rows.astype(jnp.bfloat16),
            grad_set,
            preferred_element_type=jnp.float32,
        )
        prob_grad = jnp.einsum(
            "qhd,khd->hqk", grad_set, value_set, preferred_element_type=jnp.float32
        )
        score_grad = (prob_rows * (prob_grad - delta_set[..., None])).astype(jnp.bfloat16)
        query_part = (
            jnp.einsum("hqk,khd->qhd", score_grad, key_set, preferred_element_type=jnp.float32)
            * score_scale
        )
        key_part = (
            jnp.einsum("hqk,qhd->khd", score_grad, query_set, preferred_element_type=jnp.float32)
            * score_scale
        )
        return (query_part, key_part, value_part)

    zero_heads = jnp.zeros((tok_rows, head_count, HD), jnp.float32)

    def key_turn(running):
        key_set, value_set, key_acc, value_acc, anchor, query_acc = running
        query_part, key_part, value_part = pair_grads(
            queries, grad_heads, log_total, row_delta, seq_place, key_set, value_set, anchor
        )
        moved_rows = shifted((key_set, value_set), "seq", 1)
        moved_grads = shifted((key_acc + key_part, value_acc + value_part), "seq", 1)
        return (
            moved_rows[0],
            moved_rows[1],
            moved_grads[0],
            moved_grads[1],
            (anchor - 1) % seq_count,
            query_acc + query_part,
        )

    def two_key_turns(turn_index, running):
        return key_turn(key_turn(running))

    finished = lax.fori_loop(
        0,
        seq_count // 2,
        two_key_turns,
        (key_rows, value_rows, zero_heads, zero_heads, seq_place, zero_heads),
    )
    query_grad, key_grad, value_grad = (finished[5], finished[2], finished[3])
    mixed_grad = rotate_back((query_grad, key_grad, value_grad))[0].astype(jnp.bfloat16)
    qkv_grad = jnp.einsum("td,te->de", normed_low, mixed_grad, preferred_element_type=jnp.float32)
    grad_normed = jnp.einsum(
        "te,de->td", mixed_grad, qkv_weight, preferred_element_type=jnp.float32
    )
    input_part, first_gain_grad, shift_one_grad, scale_one_grad = first_back(grad_normed)
    input_grad = (middle_grad + input_part)[None]
    mod_grad = jnp.concatenate(
        [
            shift_one_grad,
            scale_one_grad,
            gate_one_grad,
            shift_two_grad,
            scale_two_grad,
            gate_two_grad,
        ]
    )
    ada_grad = cond_low.astype(jnp.float32)[:, None] * mod_grad[None, :]
    cond_grad = jnp.dot(ada_weight.astype(jnp.float32), mod_grad, precision=highest)
    table_local = table_pick.astype(jnp.float32)[:, None] * silu_back(cond_grad)[0][None, :]
    layer_sums = (
        lax.psum_scatter(table_local, ("seq", "mlp"), scatter_dimension=0, tiled=True),
        lax.psum_scatter(ada_grad, ("seq", "mlp"), scatter_dimension=1, tiled=True),
        lax.psum_scatter(mod_grad, ("seq", "mlp"), scatter_dimension=0, tiled=True),
        lax.psum_scatter(first_gain_grad, ("seq", "mlp"), scatter_dimension=0, tiled=True),
        lax.psum_scatter(qkv_grad, ("seq", "mlp"), scatter_dimension=0, tiled=True),
        lax.psum_scatter(out_grad, ("seq", "mlp"), scatter_dimension=0, tiled=True),
        lax.psum_scatter(second_gain_grad, ("seq", "mlp"), scatter_dimension=0, tiled=True),
        lax.psum_scatter(bias_slot, ("seq", "mlp"), scatter_dimension=0, tiled=True),
        lax.psum_scatter(down_bias_grad, ("seq", "mlp"), scatter_dimension=0, tiled=True),
    )
    feed_summed = (
        lax.psum_scatter(up_grad, "seq", scatter_dimension=0, tiled=True),
        lax.psum_scatter(down_grad, "seq", scatter_dimension=1, tiled=True),
    )
    totals = lax.psum(
        (
            layer_sums[0],
            layer_sums[1],
            layer_sums[2],
            layer_sums[3],
            layer_sums[4],
            layer_sums[5],
            layer_sums[6],
            layer_sums[7],
            layer_sums[8],
            feed_summed[0],
            feed_summed[1],
        ),
        "grp",
    )
    return (
        output,
        input_grad,
        totals[0],
        totals[1],
        totals[2],
        totals[3],
        totals[4],
        totals[5],
        totals[6],
        totals[9],
        totals[7],
        totals[10],
        totals[8],
    )


LOG_SCALE = math.log2(math.e) / math.sqrt(HD)
NT = (((1,), (1,)), ((), ()))
TN = (((0,), (0,)), ((), ()))
F32 = jnp.float32
BF16 = jnp.bfloat16
WHOLE_VMEM = 60 * 1024 * 1024


def params(*semantics):
    return pltpu.CompilerParams(vmem_limit_bytes=WHOLE_VMEM, dimension_semantics=semantics)


def low_lanes(value):
    return lax.broadcasted_iota(jnp.int32, value.shape, 1) < HD


def swap_heads(value):
    return pltpu.roll(value, HD, 1)


def exchange(top, bottom):
    keep = low_lanes(top)
    return (
        jnp.where(keep, top, swap_heads(bottom)),
        jnp.where(keep, swap_heads(top), bottom),
    )


def fold(value):
    half = value.shape[0] // 2
    top = value[:half]
    return jnp.where(low_lanes(top), top, swap_heads(value[half:]))


def unfold_into(target, base, packed, fill):
    half = packed.shape[0]
    value = packed.astype(F32)
    keep = low_lanes(value)
    target[base : base + half, :] = jnp.where(keep, value, fill).astype(BF16)
    target[base + half : base + 2 * half, :] = jnp.where(keep, swap_heads(value), fill).astype(BF16)


def turn(value, cosine, sine):
    lane = lax.broadcasted_iota(jnp.int32, value.shape, 1) % HD
    quarter = HD // 2
    other = jnp.where(
        lane < quarter, pltpu.roll(value, 2 * HD - quarter, 1), pltpu.roll(value, quarter, 1)
    )
    return value * cosine + other * sine


def normalise(values):
    centred = values - jnp.mean(values, axis=-1, keepdims=True)
    spread = jnp.mean(centred * centred, axis=-1, keepdims=True)
    inverse = lax.rsqrt(spread + 1e-05)
    return centred * inverse, inverse


def project_kernel(x_ref, vec_ref, w_ref, cos_ref, sin_ref, normed_ref, pack_ref):
    rows = x_ref.shape[1]
    width = x_ref.shape[2]
    x = x_ref[...].reshape(2 * rows, width).astype(F32)
    n, _ = normalise(x)
    normed = n * vec_ref[0:1, :] * (1.0 + vec_ref[1:2, :]) + vec_ref[2:3, :]
    normed = normed.astype(BF16)
    normed_ref[...] = normed.reshape(2, rows, width)
    cosine = cos_ref[...].reshape(2 * rows, 2 * HD)
    sine = sin_ref[...].reshape(2 * rows, 2 * HD)
    for part in range(3):
        mixed = jnp.dot(
            normed, w_ref[:, part * width : (part + 1) * width], preferred_element_type=F32
        )
        for pair in range(width // (2 * HD)):
            value = mixed[:, pair * 2 * HD : (pair + 1) * 2 * HD]
            if part < 2:
                value = turn(value, cosine, sine)
            even, odd = exchange(value[:rows], value[rows:])
            pack_ref[2 * pair, part] = even.astype(BF16)
            pack_ref[2 * pair + 1, part] = odd.astype(BF16)


def project(x2, vecs, weight, cosine, sine, rows=256):
    half, width = x2.shape[1:]
    heads = width // HD
    tok = lambda last: pl.BlockSpec((2, rows, last), lambda i: (0, i, 0))
    return pl.pallas_call(
        project_kernel,
        grid=(half // rows,),
        in_specs=[
            tok(width),
            pl.BlockSpec(vecs.shape, lambda i: (0, 0)),
            pl.BlockSpec(weight.shape, lambda i: (0, 0)),
            tok(2 * HD),
            tok(2 * HD),
        ],
        out_specs=[tok(width), pl.BlockSpec((heads, 3, rows, 2 * HD), lambda i: (0, 0, i, 0))],
        out_shape=[
            jax.ShapeDtypeStruct((2, half, width), BF16),
            jax.ShapeDtypeStruct((heads, 3, half, 2 * HD), BF16),
        ],
        compiler_params=params("arbitrary"),
        name="project",
    )(x2, vecs, weight, cosine, sine)


def attend_rows(q, k_ref, v_ref, keys, out_put, log_put, block=512):
    top = None
    for start in range(0, keys, block):
        s = lax.dot_general(q, k_ref[start : start + block, :], NT, preferred_element_type=F32)
        s = s * LOG_SCALE
        peak = jnp.max(s, axis=1, keepdims=True)
        new_top = peak if top is None else jnp.maximum(top, peak)
        p = jnp.exp2(s - new_top).astype(BF16)
        part = jnp.dot(p, v_ref[start : start + block, :], preferred_element_type=F32)
        acc = part if top is None else acc * jnp.exp2(top - new_top) + part
        top = new_top
    out_put(fold(acc / swap_heads(acc)).astype(BF16))
    log_put((top + jnp.log2(acc)).T[HD : HD + 8])


def load_values(source, base, k_s, v_s):
    unfold_into(k_s, base, source[1], 0.0)
    unfold_into(v_s, base, source[2], 1.0)


def packed_queries(packed):
    value = packed.astype(F32)
    return jnp.concatenate([value, swap_heads(value)]).astype(BF16)


def push(src, dst, sems, index, where):
    return pltpu.make_async_remote_copy(
        src_ref=src, dst_ref=dst, send_sem=sems[0].at[index], recv_sem=sems[1].at[index],
        device_id=where, device_id_type=pl.DeviceIdType.MESH,
    )


def reach(src, dst, sems, index, group, place):
    return push(src, dst, sems, index, {"grp": group, "seq": place})


def neighbours(group, place, others):
    found = [
        {"grp": (group + other) % 2, "seq": (place + steps) % 4}
        for other in range(2)
        for steps in range(4)
        if other or steps
    ]
    return found + [{"mlp": other} for other in others]


def greet(devices):
    barrier = pltpu.get_barrier_semaphore()
    for where in devices:
        pl.semaphore_signal(barrier, 1, device_id=where, device_id_type=pl.DeviceIdType.MESH)
    pl.semaphore_wait(barrier, len(devices))


def mlp_place():
    mlp = lax.axis_index("mlp")
    row, core = mlp // 2, mlp % 2
    return row, core, (1 - row) * 2 + core, row * 2 + 1 - core


BLOCKS = 18


def added(left, right):
    return (left.astype(F32) + right.astype(F32)).astype(BF16)


def sum_steps(held, one_p, one_q, two, others, three, out, sems, base):
    group = lax.axis_index("grp")
    place = lax.axis_index("seq")
    row, _, other_row, _ = mlp_place()
    by_row = {"mlp": other_row}
    by_group = {"grp": 1 - group}
    ahead = lambda s: (place + s) % 4

    def copies(stage):
        if stage == 1:
            return [
                push(held.at[1 - row, :, pl.ds(0, 10)], one_p, sems, base, by_row),
                push(
                    held.at[:, :, pl.ds(10 + 4 * (1 - group), 4)], one_q, sems, base + 1, by_group
                ),
            ]
        if stage == 2:
            return [
                push(
                    one_p.at[:, pl.ds(5 * (1 - group), 5)], two.at[:, pl.ds(0, 5)], sems,
                    base + 2, by_group,
                ),
                push(one_q.at[1 - row], two.at[:, pl.ds(5, 4)], sems, base + 3, by_row),
            ]
        if stage == 3:
            return [
                push(two.at[ahead(s)], others.at[s - 1], sems, base + 3 + s, {"seq": ahead(s)})
                for s in (1, 2, 3)
            ]
        return [
            push(three.at[pl.ds(0, 5)], out.at[pl.ds(5 * group, 5)], sems, base + 7, by_group),
            push(
                three.at[pl.ds(5, 4)], out.at[pl.ds(10 + 4 * group, 4)], sems, base + 8, by_group
            ),
        ]

    def start(stage):
        for copy in copies(stage):
            copy.start()

    def arrive(stage):
        for copy in copies(stage):
            copy.wait()

    def step_one():
        start(1)

    def step_two():
        arrive(1)

        def add(z, carry):
            one_p[z] = added(held[row, z, 0:10], one_p[z])
            for y in range(2):
                one_q[y, z] = added(held[y, z, pl.ds(10 + 4 * group, 4)], one_q[y, z])
            return carry

        lax.fori_loop(0, 4, add, 0)
        start(2)

    def step_three():
        arrive(2)

        def add(z, carry):
            two[z, 0:5] = added(one_p[z, pl.ds(5 * group, 5)], two[z, 0:5])
            two[z, 5:9] = added(one_q[row, z], two[z, 5:9])
            return carry

        lax.fori_loop(0, 4, add, 0)

    def step_over():
        start(3)

    def step_four():
        arrive(3)

        def add(block, carry):
            total = two[place, block].astype(F32)
            for s in range(3):
                total = total + others[s, block].astype(F32)
            three[block] = total.astype(BF16)
            return carry

        lax.fori_loop(0, 9, add, 0)
        start(4)
        out[pl.ds(5 * group, 5)] = three[0:5]
        out[pl.ds(10 + 4 * group, 4)] = three[5:9]

    def step_five():
        arrive(4)

    return step_one, step_two, step_three, step_over, step_four, step_five


def sum_scratch(rows, shapes):
    return [pltpu.VMEM(shape + (rows, 2 * HD), BF16) for shape in shapes]


EARLY = [(4, 10), (2, 4, 4)]
MIDDLE = [(4, 9)]
LATE = [(3, 9), (9,)]


def forward_kernel(
    packs, att, pieces, results, logs, logs_own, crossed, k_s, v_s, send_sems, recv_sems
):
    group = lax.axis_index("grp")
    place = lax.axis_index("seq")
    sems = (send_sems, recv_sems)
    heads = packs.shape[0]
    rows = 2 * packs.shape[2]
    ahead = lambda s: (place + s) % 4
    behind = lambda s: (place + 4 - s) % 4

    def first(s):
        return reach(packs.at[2 * ahead(s)], pieces.at[0, s], sems, s - 1, 1, ahead(s))

    def second_values(s):
        source = packs.at[2 * ahead(s) + 1, pl.ds(1, 2)]
        return reach(source, pieces.at[1, s, pl.ds(1, 2)], sems, 2 + s, 1, ahead(s))

    def second_queries(s):
        source = packs.at[2 * ahead(s) + 1, 0]
        return reach(source, pieces.at[1, s, 0], sems, 5 + s, 1, ahead(s))

    def cross(s):
        return reach(packs.at[8 + ahead(s)], crossed.at[s], sems, 9 + s, 0, place)

    def onward(s):
        return reach(crossed.at[s], pieces.at[1, s], sems, 12 + s, 0, ahead(s))

    def home(kind, s, head):
        start = (16, 20, 24)[kind]
        return reach(
            results.at[min(kind, 1), s], att.at[head], sems, start + s, 1, behind(s)
        )

    greet(neighbours(group, place, []))

    def full(kind, head, before, after):
        sel = min(kind, 1)
        for s in range(4):
            load_values(pieces.at[sel, s], s * rows, k_s, v_s)

        def step(s, carry):
            before(s)

            def put_out(value):
                results[sel, s] = value

            def put_log(value):
                logs[sel, s] = value

            q = packed_queries(pieces[sel, s, 0])
            attend_rows(q, k_s, v_s, 4 * rows, put_out, put_log)
            after(s)
            return carry

        lax.fori_loop(0, 4, step, 0)

    @pl.when(group == 1)
    def _():
        for s in (1, 2, 3):
            first(s).start()
        for s in (1, 2, 3, 0):
            cross(s).start()
        pieces[0, 0] = packs[2 * place]
        pieces[1, 0] = packs[2 * place + 1]
        for s in (1, 2, 3):
            first(s).wait_send()
        for s in (1, 2, 3):
            second_values(s).start()
        for s in (1, 2, 3):
            first(s).wait_recv()

        def before(s):
            @pl.when(s == 2)
            def _():
                for other in (1, 2, 3):
                    second_queries(other).start()

        def after(s):
            @pl.when(s == 0)
            def _():
                att[2 * place] = results[0, 0]

            @pl.when(s > 0)
            def _():
                home(0, s, 2 * place).start()

        full(0, 2 * place, before, after)
        for s in (1, 2, 3):
            second_values(s).wait_recv()

    @pl.when(group == 0)
    def _():
        def local(head, carry):
            load_values(packs.at[head], 0, k_s, v_s)

            def put_out(value):
                att[head] = value

            def put_log(value):
                logs_own[head] = value

            attend_rows(packed_queries(packs[head, 0]), k_s, v_s, rows, put_out, put_log)
            for s in (1, 2, 3):

                @pl.when(head == 4 * s - 1)
                def _(s=s):
                    cross(s).wait_recv()
                    onward(s).start()

            return carry

        lax.fori_loop(0, heads, local, 0)
        cross(0).wait_recv()
        pieces[1, 0] = crossed[0]
        for s in (1, 2, 3):
            onward(s).wait_recv()

    def before(s):
        @pl.when((group == 1) & (s > 0))
        def _():
            second_queries(s).wait_recv()

    def after(s):
        @pl.when((group == 1) & (s == 0))
        def _():
            att[2 * place + 1] = results[1, 0]

        @pl.when((group == 1) & (s > 0))
        def _():
            home(1, s, 2 * place + 1).start()

        @pl.when(group == 0)
        def _():
            home(2, s, 8 + place).start()

    full(1, 0, before, after)

    @pl.when(group == 1)
    def _():
        for s in (1, 2, 3):
            second_values(s).wait_send()
            second_queries(s).wait_send()
            for kind in (0, 1):
                home(kind, s, 2 * place + kind).wait_send()
        for s in range(4):
            cross(s).wait_send()
        for s in (1, 2, 3):
            for kind in (0, 1):
                home(kind, s, 2 * ahead(s) + kind).wait_recv()
        for s in range(4):
            home(2, s, 8 + ahead(s)).wait_recv()

    @pl.when(group == 0)
    def _():
        for s in (1, 2, 3):
            onward(s).wait_send()
        for s in range(4):
            home(2, s, 8 + place).wait_send()


def in_vmem(count):
    return [pl.BlockSpec(memory_space=pltpu.VMEM)] * count


def forward_attention(packs):
    heads, _, half, lanes = packs.shape
    shapes = [
        ((heads, half, lanes), BF16),
        ((2, 4, 3, half, lanes), BF16),
        ((2, 4, half, lanes), BF16),
        ((2, 4, 8, 2 * half), F32),
        ((heads, 8, 2 * half), F32),
    ]
    return pl.pallas_call(
        forward_kernel,
        in_specs=in_vmem(1),
        out_specs=in_vmem(len(shapes)),
        out_shape=[jax.ShapeDtypeStruct(shape, kind) for shape, kind in shapes],
        scratch_shapes=[
            pltpu.VMEM((4, 3, half, lanes), BF16),
            pltpu.VMEM((8 * half, lanes), BF16),
            pltpu.VMEM((8 * half, lanes), BF16),
            pltpu.SemaphoreType.DMA((28,)),
            pltpu.SemaphoreType.DMA((28,)),
        ],
        compiler_params=pltpu.CompilerParams(
            collective_id=1, has_side_effects=True, vmem_limit_bytes=WHOLE_VMEM
        ),
        cost_estimate=pl.CostEstimate(
            flops=100_000_000_000, bytes_accessed=8_000_000, transcendentals=0
        ),
        name="forward_attention",
    )(packs)


def tile_grads(q, do, k, v, log_row, delta_row):
    s = lax.dot_general(k, q, NT, preferred_element_type=F32)
    p = jnp.exp2(s * LOG_SCALE - log_row)
    dp = lax.dot_general(v, do, NT, preferred_element_type=F32)
    ds = (p * (dp - delta_row)).astype(BF16)
    dv = jnp.dot(p.astype(BF16), do, preferred_element_type=F32)
    dk = jnp.dot(ds, q, preferred_element_type=F32)
    dq = lax.dot_general(k, ds, TN, preferred_element_type=F32)
    return dq, dk, dv


def load_backward(source, do, o, base, q_s, k_s, v_s, do_s, delta_s):
    half = do.shape[0]
    unfold_into(q_s, base, source[0], 0.0)
    unfold_into(k_s, base, source[1], 0.0)
    unfold_into(v_s, base, source[2], 0.0)
    unfold_into(do_s, base, do, 0.0)
    product = (do.astype(F32) * o.astype(F32)).T
    first = jnp.sum(product[:HD], axis=0, keepdims=True)
    second = jnp.sum(product[HD:], axis=0, keepdims=True)
    delta_s[:, base : base + half] = jnp.broadcast_to(first, (8, half))
    delta_s[:, base + half : base + 2 * half] = jnp.broadcast_to(second, (8, half))


def backward_kernel(
    packs, gatt, att, pieces, results, logs, logs_own, dos, held, back, two,
    staged, q_s, k_s, v_s, do_s, delta_s, dq_s, one_p, one_q,
    send_sems, recv_sems,
):
    group = lax.axis_index("grp")
    place = lax.axis_index("seq")
    sems = (send_sems, recv_sems)
    heads = packs.shape[0]
    rows = 2 * packs.shape[2]
    scale = 1.0 / math.sqrt(HD)
    ahead = lambda s: (place + s) % 4
    behind = lambda s: (place + 4 - s) % 4
    stores = (q_s, k_s, v_s, do_s, delta_s)

    def home_values(kind, s, head):
        source = staged.at[min(kind, 1), s, pl.ds(1, 2)]
        return reach(
            source, back.at[head, pl.ds(1, 2)], sems, (0, 4, 8)[kind] + s, 1, behind(s)
        )

    def home_queries(kind, s, head):
        source = staged.at[min(kind, 1), s, 0]
        return reach(source, back.at[head, 0], sems, (12, 16, 20)[kind] + s, 1, behind(s))

    greet(neighbours(group, place, [mlp_place()[2]]))
    sum_one, sum_two, sum_three, _, _, _ = sum_steps(
        held, one_p, one_q, two, None, None, None, sems, 24
    )
    sum_one()

    def full(sel, put_values, put_queries):
        for s in range(4):
            load_backward(
                pieces.at[sel, s], dos[sel, s], results[sel, s], s * rows, *stores
            )

        def step(s, carry):
            block = pl.ds(pl.multiple_of(s * rows, rows), rows)
            k = k_s[block, :]
            v = v_s[block, :]
            dk = dv = None
            for index in range(4):
                chunk = slice(index * rows, (index + 1) * rows)
                dq, dk_part, dv_part = tile_grads(
                    q_s[chunk, :], do_s[chunk, :], k, v, logs[sel, index, 0:1, :],
                    delta_s[0:1, chunk],
                )
                dk = dk_part if dk is None else dk + dk_part
                dv = dv_part if dv is None else dv + dv_part
                dq_s[:, chunk] = jnp.where(s == 0, dq, dq_s[:, chunk] + dq)
            staged[sel, s, 1] = fold(dk * scale).astype(BF16)
            staged[sel, s, 2] = fold(dv).astype(BF16)
            put_values(s)
            return carry

        lax.fori_loop(0, 4, step, 0)
        for s in (3, 2, 1, 0):
            chunk = slice(s * rows, (s + 1) * rows)
            staged[sel, s, 0] = fold(dq_s[:, chunk].T * scale).astype(BF16)
            put_queries(s)

    @pl.when(group == 1)
    def _():
        head = 2 * place

        def put_values(s):
            @pl.when(s == 0)
            def _():
                back[head, 1] = staged[0, 0, 1]
                back[head, 2] = staged[0, 0, 2]

            @pl.when(s > 0)
            def _():
                home_values(0, s, head).start()

            @pl.when(s == 2)
            def _():
                sum_two()

        def put_queries(s):
            if s == 0:
                back[head, 0] = staged[0, 0, 0]
            else:
                home_queries(0, s, head).start()

        full(0, put_values, put_queries)

    def put_values(s):
        head = 2 * place + 1

        @pl.when((group == 1) & (s == 0))
        def _():
            back[head, 1] = staged[1, 0, 1]
            back[head, 2] = staged[1, 0, 2]

        @pl.when((group == 1) & (s > 0))
        def _():
            home_values(1, s, head).start()

        @pl.when(group == 0)
        def _():
            home_values(2, s, 8 + place).start()

        @pl.when((group == 0) & (s == 2))
        def _():
            sum_two()

    def put_queries(s):
        head = 2 * place + 1

        @pl.when(group == 1)
        def _():
            if s == 0:
                back[head, 0] = staged[1, 0, 0]
            else:
                home_queries(1, s, head).start()

        @pl.when(group == 0)
        def _():
            home_queries(2, s, 8 + place).start()

    full(1, put_values, put_queries)

    @pl.when(group == 0)
    def _():
        def local(head, carry):
            load_backward(packs.at[head], gatt[head], att[head], 0, *stores)
            own = slice(0, rows)
            dq, dk, dv = tile_grads(
                q_s[own, :], do_s[own, :], k_s[own, :], v_s[own, :],
                logs_own[head, 0:1, :], delta_s[0:1, own],
            )
            back[head, 0] = fold(dq.T * scale).astype(BF16)
            back[head, 1] = fold(dk * scale).astype(BF16)
            back[head, 2] = fold(dv).astype(BF16)
            return carry

        lax.fori_loop(0, heads, local, 0)

    sum_three()

    @pl.when(group == 0)
    def _():
        for s in range(4):
            home_values(2, s, 8 + place).wait_send()
            home_queries(2, s, 8 + place).wait_send()

    @pl.when(group == 1)
    def _():
        for s in (1, 2, 3):
            for kind in (0, 1):
                home_values(kind, s, 2 * place + kind).wait_send()
                home_queries(kind, s, 2 * place + kind).wait_send()
        for s in (1, 2, 3):
            for kind in (0, 1):
                home_values(kind, s, 2 * ahead(s) + kind).wait_recv()
                home_queries(kind, s, 2 * ahead(s) + kind).wait_recv()
        for s in range(4):
            home_values(2, s, 8 + ahead(s)).wait_recv()
            home_queries(2, s, 8 + ahead(s)).wait_recv()


def backward_attention(packs, gatt, att, pieces, results, logs, logs_own, dos, held):
    heads, _, half, lanes = packs.shape
    share = held.shape[2:]
    return pl.pallas_call(
        backward_kernel,
        in_specs=in_vmem(9),
        out_specs=in_vmem(2),
        out_shape=[
            jax.ShapeDtypeStruct((heads, 3, half, lanes), BF16),
            jax.ShapeDtypeStruct((4, 9) + share[1:], BF16),
        ],
        scratch_shapes=[pltpu.VMEM((2, 4, 3, half, lanes), BF16)]
        + [pltpu.VMEM((8 * half, lanes), BF16)] * 4
        + [pltpu.VMEM((8, 8 * half), F32), pltpu.VMEM((lanes, 8 * half), F32)]
        + sum_scratch(share[1], EARLY)
        + [pltpu.SemaphoreType.DMA((28,)), pltpu.SemaphoreType.DMA((28,))],
        compiler_params=pltpu.CompilerParams(
            collective_id=2, has_side_effects=True, vmem_limit_bytes=WHOLE_VMEM
        ),
        cost_estimate=pl.CostEstimate(
            flops=120_000_000_000, bytes_accessed=8_000_000, transcendentals=0
        ),
        name="backward_attention",
    )(packs, gatt, att, pieces, results, logs, logs_own, dos, held)


def whole(shape):
    zeros = (0,) * len(shape)
    return pl.BlockSpec(shape, lambda *_: zeros)


def middle_kernel(
    x_ref, cot_ref, att_ref, vec_ref, ow_ref, feed_ref,
    out_ref, attlow_ref, hidden_ref, act_ref, gfeed_ref, gpre_ref, mgrad_ref, gbranch_ref,
    gatt_ref, sums_ref, upsum_ref, att_s, slope_s,
):
    step = pl.program_id(0)
    rows, width = x_ref.shape[1:]
    both = 2 * rows
    pairs = width // (2 * HD)
    gate_one, gain, scale, shift = (vec_ref[i : i + 1, :] for i in range(4))
    gate_two, down_bias = vec_ref[4:5, :], vec_ref[5:6, :]
    for pair in range(pairs):
        lanes = slice(pair * 2 * HD, (pair + 1) * 2 * HD)
        top, bottom = exchange(
            att_ref[2 * pair].astype(F32), att_ref[2 * pair + 1].astype(F32)
        )
        att_s[:rows, lanes] = top.astype(BF16)
        att_s[rows:, lanes] = bottom.astype(BF16)
    att = att_s[...]
    attlow_ref[...] = att.reshape(2, rows, width)
    branch = jnp.dot(att, ow_ref[...], preferred_element_type=F32)
    middle = x_ref[...].reshape(both, width).astype(F32) + gate_one * branch
    n, inverse = normalise(middle)
    hidden = (n * gain * (1.0 + scale) + shift).astype(BF16)
    hidden_ref[...] = hidden.reshape(2, rows, width)
    shares, _, chunk = feed_ref.shape
    feed = None
    for index in range(shares):
        cols = slice(index * chunk, (index + 1) * chunk)
        pre = jnp.dot(hidden, feed_ref[index, :width], preferred_element_type=F32)
        pre = pre + feed_ref[index, 2 * width : 2 * width + 1].astype(F32)
        square = pre * pre
        root = math.sqrt(2.0 / math.pi)
        tanh = jnp.tanh(pre * (root + (root * 0.044715) * square))
        half_up = 0.5 + 0.5 * tanh
        act = (pre * half_up).astype(BF16)
        slope_s[:, cols] = half_up + (0.5 * pre) * (1.0 - tanh * tanh) * (
            root + (3.0 * root * 0.044715) * square
        )
        act_ref[:, :, cols] = act.reshape(2, rows, chunk)
        part = jnp.dot(act, feed_ref[index, width : 2 * width], preferred_element_type=F32)
        feed = part if feed is None else feed + part
    feed = feed + down_bias
    out_ref[...] = (middle + gate_two * feed).astype(BF16).reshape(2, rows, width)
    cot = cot_ref[...].reshape(both, width).astype(F32)
    gfeed = (gate_two * cot).astype(BF16)
    gfeed_ref[...] = gfeed.reshape(2, rows, width)
    ghidden = None
    up_sums = []
    for index in range(shares):
        cols = slice(index * chunk, (index + 1) * chunk)
        gact = lax.dot_general(
            gfeed, feed_ref[index, width : 2 * width], NT, preferred_element_type=F32
        )
        gpre = (gact * slope_s[:, cols]).astype(BF16)
        gpre_ref[:, :, cols] = gpre.reshape(2, rows, chunk)
        up_sums.append(jnp.sum(gpre.astype(F32), axis=0, keepdims=True))
        part = lax.dot_general(gpre, feed_ref[index, :width], NT, preferred_element_type=F32)
        ghidden = part if ghidden is None else ghidden + part
    e = ghidden * ((1.0 + scale) * gain)
    mgrad = cot + inverse * (
        e - jnp.mean(e, axis=-1, keepdims=True) - n * jnp.mean(e * n, axis=-1, keepdims=True)
    )
    mgrad_ref[...] = mgrad.reshape(2, rows, width)
    gbranch = (gate_one * mgrad).astype(BF16)
    gbranch_ref[...] = gbranch.reshape(2, rows, width)
    gatt = lax.dot_general(gbranch, ow_ref[...], NT, preferred_element_type=F32)
    for pair in range(pairs):
        value = gatt[:, pair * 2 * HD : (pair + 1) * 2 * HD]
        even, odd = exchange(value[:rows], value[rows:])
        gatt_ref[2 * pair] = even.astype(BF16)
        gatt_ref[2 * pair + 1] = odd.astype(BF16)
    add = lambda value: jnp.sum(value, axis=0, keepdims=True)

    @pl.when(step == 0)
    def _():
        sums_ref[...] = jnp.zeros_like(sums_ref)
        upsum_ref[...] = jnp.zeros_like(upsum_ref)

    sums_ref[0:1, :] += add(ghidden)
    sums_ref[1:2, :] += add(ghidden * n)
    sums_ref[2:3, :] += add(cot * feed)
    sums_ref[3:4, :] += add(gfeed.astype(F32))
    sums_ref[4:5, :] += add(mgrad * branch)
    for index, value in enumerate(up_sums):
        upsum_ref[0:1, index * chunk : (index + 1) * chunk] += value


def once(shape):
    zeros = (0,) * len(shape)
    return pl.BlockSpec(shape, lambda *_: zeros, pipeline_mode=pl.Buffered(1))


def middle_pass(x2, cot2, att, vecs, out_weight, feed_weights, rows=128):
    half, width = x2.shape[1:]
    heads = width // HD
    units = feed_weights.shape[0] * feed_weights.shape[2]
    tok = lambda last: pl.BlockSpec((2, rows, last), lambda i: (0, i, 0))
    pack = pl.BlockSpec((heads, rows, 2 * HD), lambda i: (0, i, 0))
    token = lambda last, kind: jax.ShapeDtypeStruct((2, half, last), kind)
    return pl.pallas_call(
        middle_kernel,
        grid=(half // rows,),
        in_specs=[
            tok(width), tok(width), pack, whole(vecs.shape), once(out_weight.shape),
            once(feed_weights.shape),
        ],
        out_specs=[
            tok(width), tok(width), tok(width), tok(units), tok(width), tok(units), tok(width),
            tok(width), pack, whole((8, width)), whole((8, units)),
        ],
        out_shape=[
            token(width, BF16), token(width, BF16), token(width, BF16), token(units, BF16),
            token(width, BF16), token(units, BF16), token(width, F32), token(width, BF16),
            jax.ShapeDtypeStruct((heads, half, 2 * HD), BF16),
            jax.ShapeDtypeStruct((8, width), F32),
            jax.ShapeDtypeStruct((8, units), F32),
        ],
        scratch_shapes=[pltpu.VMEM((2 * rows, width), BF16), pltpu.VMEM((2 * rows, units), F32)],
        compiler_params=params("arbitrary"),
        name="middle_pass",
    )(x2, cot2, att, vecs, out_weight, feed_weights)


def feed_grads_kernel(
    hidden_ref, gfeed_ref, att_ref, gbranch_ref, act_ref, gpre_ref, gatt, held, dos,
    hidden_s, gfeed_s, att_s, sent, got, crossed, send_sems, recv_sems,
):
    group = lax.axis_index("grp")
    place = lax.axis_index("seq")
    _, core, _, other_core = mlp_place()
    sems = (send_sems, recv_sems)
    ahead = lambda s: (place + s) % 4

    def first(s):
        return reach(gatt.at[2 * ahead(s)], dos.at[0, s], sems, s - 1, 1, ahead(s))

    def second(s):
        return reach(gatt.at[2 * ahead(s) + 1], dos.at[1, s], sems, 2 + s, 1, ahead(s))

    def cross(s):
        return reach(gatt.at[8 + ahead(s)], crossed.at[s], sems, 6 + s, 0, place)

    def onward(s):
        return reach(crossed.at[s], dos.at[1, s], sems, 9 + s, 0, ahead(s))

    def swap(y):
        return push(sent.at[y], got.at[y], sems, 13 + y, {"mlp": other_core})

    greet(neighbours(group, place, [other_core]))

    @pl.when(group == 1)
    def _():
        for s in (1, 2, 3):
            cross(s).start()
            first(s).start()
            second(s).start()
        cross(0).start()
        dos[0, 0] = gatt[2 * place]
        dos[1, 0] = gatt[2 * place + 1]

    hidden_s[...] = hidden_ref[...].T
    gfeed_s[...] = gfeed_ref[...].T
    att_s[...] = att_ref[...].T
    width = hidden_s.shape[0]
    split = width // 4
    part = split // 4
    rows = 3 * part

    def blocks(target, y, index):
        cols = pl.ds(pl.multiple_of(index * width, width), width)
        up = jnp.dot(hidden_s[...], gpre_ref[:, cols], preferred_element_type=F32).astype(BF16)
        down = jnp.dot(gfeed_s[...], act_ref[:, cols], preferred_element_type=F32).astype(BF16)
        own = jnp.concatenate(
            [
                att_s[pl.ds(pl.multiple_of(index * part + z * split, 16), part), :]
                for z in range(4)
            ]
        )
        out = jnp.dot(own, gbranch_ref[...], preferred_element_type=F32).astype(BF16)
        for z in range(4):
            start = z * split
            pieces = (
                (up[start : start + rows],),
                (up[start + rows : start + split], down[start : start + split - rows + part]),
                (down[start + 2 * part : start + split], out[z * part : (z + 1) * part]),
            )
            for number, values in enumerate(pieces):
                base = 0
                for value in values:
                    size = value.shape[0]
                    for lane in range(width // (2 * HD)):
                        target[y, z, number * 6 + lane, base : base + size, :] = value[
                            :, lane * 2 * HD : (lane + 1) * 2 * HD
                        ]
                    base += size

    def send_row(y, carry):
        blocks(sent, y, 2 * y + 1 - core)
        swap(y).start()
        return carry

    lax.fori_loop(0, 2, send_row, 0)

    @pl.when(group == 0)
    def _():
        for s in (1, 2, 3):
            cross(s).wait_recv()
            onward(s).start()
        cross(0).wait_recv()
        dos[1, 0] = crossed[0]

    def keep_row(y, carry):
        blocks(held, y, 2 * y + core)
        return carry

    lax.fori_loop(0, 2, keep_row, 0)

    def add_row(y, carry):
        swap(y).wait()

        def add(z, inner):
            held[y, z] = added(held[y, z], got[y, z])
            return inner

        return lax.fori_loop(0, 4, add, carry)

    lax.fori_loop(0, 2, add_row, 0)

    @pl.when(group == 1)
    def _():
        for s in (1, 2, 3):
            first(s).wait()
            second(s).wait()
        for s in range(4):
            cross(s).wait_send()

    @pl.when(group == 0)
    def _():
        for s in (1, 2, 3):
            onward(s).wait()


def feed_grads(hidden, gfeed, att, gbranch, act, gpre, gatt):
    tokens, width = hidden.shape
    _, half, lanes = gatt.shape
    rows = 3 * width // 16
    share = (2, 4, BLOCKS, rows, lanes)
    return pl.pallas_call(
        feed_grads_kernel,
        in_specs=in_vmem(7),
        out_specs=in_vmem(2),
        out_shape=[
            jax.ShapeDtypeStruct(share, BF16),
            jax.ShapeDtypeStruct((2, 4, half, lanes), BF16),
        ],
        scratch_shapes=[pltpu.VMEM((width, tokens), BF16)] * 3
        + [
            pltpu.VMEM(share, BF16),
            pltpu.VMEM(share, BF16),
            pltpu.VMEM((4, half, lanes), BF16),
            pltpu.SemaphoreType.DMA((15,)),
            pltpu.SemaphoreType.DMA((15,)),
        ],
        compiler_params=pltpu.CompilerParams(
            collective_id=3, has_side_effects=True, vmem_limit_bytes=WHOLE_VMEM
        ),
        cost_estimate=pl.CostEstimate(
            flops=24_000_000_000, bytes_accessed=20_000_000, transcendentals=0
        ),
        name="feed_grads",
    )(hidden, gfeed, att, gbranch, act, gpre, gatt)


SMALL_ROWS = 40


def finish_kernel(
    packs, cosine, sine, normed_ref, vec_one, vec_two, middle_sums, up_sums, extra, feed_two,
    w_ref, x_ref, mgrad_ref, ada_ref, total, feed_total, rows_all, grad_ref,
    mixed, w_s, x_s, mgrad_s, ada_s, sums, small, sent, got, held, one_p, one_q, two, others,
    three, feed_others, feed_three, send_sems, recv_sems, own_sems,
):
    group = lax.axis_index("grp")
    place = lax.axis_index("seq")
    row, core, _, other_core = mlp_place()
    mlp = row * 2 + core
    sems = (send_sems, recv_sems)
    ahead = lambda s: (place + s) % 4
    heads = packs.shape[0]
    half = packs.shape[2]
    width = heads * HD
    lanes = 2 * HD
    parts = 3
    each = BLOCKS // parts

    loads = [
        pltpu.make_async_copy(source, target, own_sems.at[index])
        for index, (source, target) in enumerate(
            ((w_ref, w_s), (x_ref, x_s), (mgrad_ref, mgrad_s), (ada_ref, ada_s))
        )
    ]
    for load in loads:
        load.start()
    greet(
        [{"seq": ahead(s)} for s in (1, 2, 3)]
        + [{"mlp": (mlp + s) % 4} for s in (1, 2, 3)]
        + [{"grp": 1 - group}]
    )
    _, _, _, feed_over, feed_four, feed_five = sum_steps(
        None, None, None, feed_two, feed_others, feed_three, feed_total, sems, 0
    )
    sum_one, sum_two, sum_three, sum_over, sum_four, sum_five = sum_steps(
        held, one_p, one_q, two, others, three, total, sems, 9
    )
    feed_over()

    def swap(index):
        own = pl.ds(index * each, each)
        return push(
            sent.at[:, :, own], got.at[:, :, own], sems, 18 + index, {"mlp": other_core}
        )

    def unrotate(part):
        def one_pair(pair, carry):
            top, bottom = exchange(
                packs[2 * pair, part].astype(F32), packs[2 * pair + 1, part].astype(F32)
            )
            if part < 2:
                top = turn(top, cosine[0], -sine[0])
                bottom = turn(bottom, cosine[1], -sine[1])
            cols = pl.ds(pl.multiple_of(part * width + pair * lanes, lanes), lanes)
            mixed[:half, cols] = top.astype(BF16)
            mixed[half:, cols] = bottom.astype(BF16)
            return carry

        lax.fori_loop(0, heads // 2, one_pair, 0)

    def blocks(target, which, index):
        value = jnp.dot(
            normed_ref[which], mixed[:, index * width : (index + 1) * width],
            preferred_element_type=F32,
        ).astype(BF16)
        for lane in range(each):
            target[:, :, index * each + lane] = value[
                :, lane * lanes : (lane + 1) * lanes
            ].reshape(2, 4, width // 16, lanes)

    for index in (2, 0, 1):
        unrotate(index)
        blocks(sent, 1 - core, index)
        swap(index).start()
    for index in range(parts):
        blocks(held, core, index)
    for index in range(parts):
        swap(index).wait()
    for y in range(2):

        def add(z, carry, y=y):
            held[y, z] = added(held[y, z], got[y, z])
            return carry

        lax.fori_loop(0, 4, add, 0)
    sum_one()
    feed_four()
    for load in loads:
        load.wait()
    chunk = half // 2
    sums[...] = jnp.zeros_like(sums)

    def store(index):
        own = pl.ds(index * chunk, chunk)
        return pltpu.make_async_copy(mgrad_s.at[own], grad_ref.at[own], own_sems.at[4 + index])

    for index in range(4):
        own = slice(index * chunk, (index + 1) * chunk)
        gnormed = lax.dot_general(mixed[own, :], w_s[...], NT, preferred_element_type=F32)
        n, inverse = normalise(x_s[own, :].astype(F32))
        e = gnormed * ((1.0 + vec_one[1:2, :]) * vec_one[0:1, :])
        mgrad_s[own, :] = mgrad_s[own, :] + inverse * (
            e - jnp.mean(e, axis=-1, keepdims=True) - n * jnp.mean(e * n, axis=-1, keepdims=True)
        )
        store(index).start()
        sums[0:1, :] += jnp.sum(gnormed, axis=0, keepdims=True)
        sums[1:2, :] += jnp.sum(gnormed * n, axis=0, keepdims=True)
        if index == 2:
            sum_two()

    first_sum, second_sum = sums[1:2, :], middle_sums[1:2, :]
    mod = [
        sums[0:1, :], vec_one[0:1, :] * first_sum, middle_sums[4:5, :], middle_sums[0:1, :],
        vec_two[1:2, :] * second_sum, middle_sums[2:3, :],
    ]
    wholes = [
        (1.0 + vec_one[1:2, :]) * first_sum, (1.0 + vec_two[2:3, :]) * second_sum,
        middle_sums[3:4, :],
    ]
    weighted = None
    for index, value in enumerate(mod):
        part = jnp.sum(
            ada_s[:, index * width : (index + 1) * width].astype(F32) * value, axis=1,
            keepdims=True,
        )
        weighted = part if weighted is None else weighted + part
    table_row = jnp.broadcast_to(weighted, (lanes, lanes)).T[0:1] * extra[2:3, :]
    tiles = width // lanes
    for z in range(4):
        for line in range(9):
            tile = 9 * z + line
            value = mod[tile // tiles]
            start = (tile % tiles) * lanes
            small[z, line : line + 1, :] = value[:, start : start + lanes]
        for line in range(tiles):
            start = z * width + line * lanes
            small[z, 9 + line : 10 + line, :] = up_sums[0:1, start : start + lanes]
            for index, value in enumerate(wholes):
                at = 15 + index * tiles + line
                small[z, at : at + 1, :] = value[:, line * lanes : (line + 1) * lanes]
        small[z, 33:34, :] = table_row
        small[z, 34:36, :] = extra[0:2, :]
        small[z, 36:40, :] = jnp.zeros((4, lanes), F32)

    def hop_place(s):
        return push(
            small.at[ahead(s)], rows_all.at[group, mlp, place], sems, 20 + s, {"seq": ahead(s)}
        )

    def hop_place_in(s):
        return push(
            small.at[ahead(s)], rows_all.at[group, mlp, ahead(4 - s)], sems, 20 + s,
            {"seq": ahead(s)},
        )

    def hop_mlp(s, from_place):
        own = rows_all.at[group, from_place]
        return push(own, own, sems, 23 + s, {"mlp": (mlp + s) % 4})

    def hop_group(from_group):
        own = rows_all.at[from_group]
        return push(own, own, sems, 27, {"grp": 1 - group})

    for s in (1, 2, 3):
        hop_place(s).start()
    rows_all[group, mlp, place] = small[place]
    sum_three()
    sum_over()
    for s in (1, 2, 3):
        hop_place_in(s).wait()
    for s in (1, 2, 3):
        hop_mlp(s, mlp).start()
    sum_four()
    for s in (1, 2, 3):
        hop_mlp(s, mlp).wait_send()
        hop_mlp(s, (mlp + 4 - s) % 4).wait_recv()
    hop_group(group).start()
    feed_five()
    sum_five()
    hop_group(group).wait_send()
    hop_group(1 - group).wait_recv()
    for index in range(4):
        store(index).wait()


def finish(
    packs, cosine, sine, normed, vec_one, vec_two, middle_sums, up_sums, extra, feed_two, weight,
    x, mgrad, ada_weight,
):
    rows = normed.shape[1] // 8
    lanes = 2 * HD
    share = (2, 4, BLOCKS, rows, lanes)
    feed_rows = feed_two.shape[2]
    tokens, width = x.shape
    like = lambda value: pltpu.VMEM(value.shape, value.dtype)
    apart = pl.BlockSpec(memory_space=pl.ANY)
    return pl.pallas_call(
        finish_kernel,
        in_specs=in_vmem(10) + [apart] * 4,
        out_specs=in_vmem(3) + [apart],
        out_shape=[
            jax.ShapeDtypeStruct(share[2:], BF16),
            jax.ShapeDtypeStruct((BLOCKS, feed_rows, lanes), BF16),
            jax.ShapeDtypeStruct((2, 4, 4, SMALL_ROWS, lanes), F32),
            jax.ShapeDtypeStruct((tokens, width), F32),
        ],
        scratch_shapes=[
            pltpu.VMEM((tokens, 3 * width), BF16), like(weight), like(x), like(mgrad),
            like(ada_weight), pltpu.VMEM((8, width), F32), pltpu.VMEM((4, SMALL_ROWS, lanes), F32),
        ]
        + [pltpu.VMEM(share, BF16)] * 3
        + sum_scratch(rows, EARLY + MIDDLE + LATE)
        + sum_scratch(feed_rows, LATE)
        + [pltpu.SemaphoreType.DMA((28,))] * 2
        + [pltpu.SemaphoreType.DMA((8,))],
        compiler_params=pltpu.CompilerParams(
            collective_id=4, has_side_effects=True, vmem_limit_bytes=WHOLE_VMEM
        ),
        cost_estimate=pl.CostEstimate(
            flops=60_000_000_000, bytes_accessed=20_000_000, transcendentals=0
        ),
        name="finish",
    )(
        packs, cosine, sine, normed, vec_one, vec_two, middle_sums, up_sums, extra, feed_two,
        weight, x, mgrad, ada_weight,
    )


def four_shards(
    tokens, step_index, time_table, ada_weight, ada_bias, first_gain, qkv_weight, out_weight,
    second_gain, up_weight, up_bias, down_weight, down_bias, cotangent,
):
    place = lax.axis_index("seq")
    group = lax.axis_index("grp")
    mlp_count = lax.axis_size("mlp")
    second = group == 1
    token_rows, width = tokens.shape[1:]
    half = token_rows // 2
    heads = width // HD
    slot = lambda steps: (place + steps) % 4
    group_row = jnp.full((1,), group, jnp.int32)

    share_units = up_weight.shape[1]
    bias_rows = jnp.broadcast_to(up_bias[None, :], (16, share_units))
    feed_weights = lax.all_gather(
        jnp.concatenate([up_weight, down_weight, bias_rows]), "mlp", axis=0
    )

    step_value = jnp.sum(jnp.where(jnp.arange(4, dtype=jnp.int32) == place, step_index[0], 0))
    embedded = lax.dynamic_slice_in_dim(time_table, step_value, 1, 0)[0].astype(F32)
    condition, silu_back = jax.vjp(jax.nn.silu, embedded)
    cond_low = condition.astype(BF16)
    modulation = jnp.dot(cond_low[None, :], ada_weight, preferred_element_type=F32)[
        0
    ] + ada_bias.astype(F32)
    shift_one, scale_one, gate_one, shift_two, scale_two, gate_two = jnp.split(modulation, 6)

    positions = jnp.arange(token_rows, dtype=jnp.int32) + jnp.where(second, place * token_rows, 0)
    frequency = jnp.exp(jnp.arange(HD // 2, dtype=F32) * (-2.0 * math.log(10000.0) / HD))
    angles = positions.astype(F32)[:, None] * frequency[None, :]
    cosine, sine = jnp.cos(angles), jnp.sin(angles)
    cosine = jnp.concatenate([cosine] * 4, axis=1).reshape(2, half, 2 * HD)
    sine = jnp.concatenate([-sine, sine] * 2, axis=1).reshape(2, half, 2 * HD)

    x2 = tokens.reshape(2, half, width)
    blank = jnp.zeros((width,), F32)
    gain_one = first_gain.astype(F32)
    gain_two = second_gain.astype(F32)
    vec_one = jnp.stack([gain_one, scale_one, shift_one] + [blank] * 5)
    vec_two = jnp.stack(
        [gate_one, gain_two, scale_two, shift_two, gate_two, down_bias.astype(F32), blank, blank]
    )
    normed, packs = project(x2, vec_one, qkv_weight, cosine, sine)

    att, pieces, results, logs, logs_own = forward_attention(packs)
    (
        output, att_low, hidden, act, grad_feed, grad_pre, middle_grad, grad_branch, grad_att,
        middle_sums, up_sums,
    ) = middle_pass(
        x2, cotangent.reshape(2, half, width), att, vec_two, out_weight, feed_weights
    )
    flat = lambda value: value.reshape(token_rows, value.shape[2])
    feed_held, att_grads = feed_grads(
        *(flat(value) for value in (hidden, grad_feed, att_low, grad_branch, act, grad_pre)),
        grad_att,
    )
    grads, feed_two = backward_attention(
        packs, grad_att, att, pieces, results, logs, logs_own, att_grads, feed_held
    )
    blocks = flat(normed).T.reshape(4, 2, 2, width // 16, token_rows)
    blocks = jnp.transpose(blocks, (2, 1, 0, 3, 4)).reshape(2, width // 2, token_rows)
    lanes = 2 * HD
    extra = jnp.stack(
        [
            condition, jnp.full(condition.shape, step_value, F32),
            silu_back(jnp.ones_like(condition))[0],
        ]
        + [jnp.zeros_like(condition)] * 5
    )
    qkv_blocks, feed_blocks, rows_all, input_grad = finish(
        grads, cosine, sine, blocks, vec_one, vec_two, middle_sums, up_sums, extra,
        feed_two, qkv_weight, flat(x2), flat(middle_grad), ada_weight,
    )
    feed_total = feed_blocks.reshape(3, 6, 3 * width // 16, lanes)
    feed_total = jnp.transpose(feed_total, (0, 2, 1, 3)).reshape(9 * width // 16, width)
    feed_total = feed_total.astype(F32)
    qkv_total = jnp.transpose(qkv_blocks, (1, 0, 2)).reshape(width // 16, 3 * width).astype(F32)

    mlp = lax.axis_index("mlp")
    ranks = 4 * mlp_count
    rank = place * mlp_count + mlp
    rows_all = rows_all.reshape(2 * ranks, SMALL_ROWS, lanes)
    row_sums = jnp.sum(rows_all, axis=0)

    def share(value, index, count):
        value = value.reshape(value.shape[:-2] + (-1,))
        each = value.shape[-1] // count
        return lax.dynamic_slice_in_dim(value, index * each, each, value.ndim - 1)

    mod_share = share(rows_all[:, 0:9], mlp, mlp_count)
    up_bias_share = share(row_sums[9:15], mlp, mlp_count)
    first_share, second_share, down_bias_share = (
        share(row_sums[start : start + 6], rank, ranks) for start in (15, 21, 27)
    )
    cond_all = rows_all[:, 34].astype(BF16).astype(F32)
    ada_share = lax.dot_general(cond_all, mod_share, TN, precision=highest)
    table_each = time_table.shape[0] // ranks
    own_rows = rank * table_each + jnp.arange(table_each, dtype=jnp.int32)
    chosen = (own_rows[:, None] == rows_all[None, :, 35, 0].astype(jnp.int32)).astype(F32)
    table_share = jnp.dot(chosen, rows_all[:, 33], precision=highest)
    split = width // 4
    up_total = feed_total[:split]
    down_total = feed_total[split : 2 * split].T
    out_total = feed_total[2 * split :]
    return (
        output.reshape(1, token_rows, width),
        input_grad.reshape(1, token_rows, width),
        table_share,
        ada_share,
        jnp.sum(mod_share, axis=0),
        first_share,
        qkv_total,
        out_total,
        second_share,
        up_total,
        up_bias_share,
        down_total,
        down_bias_share,
    )


def solution(mesh):
    in_specs = (
        P(("grp", "mlp"), "seq", None),
        P(("grp", "mlp"), None),
        P(),
        P(),
        P(),
        P(),
        P(),
        P(),
        P(),
        P(None, "mlp"),
        P("mlp"),
        P("mlp", None),
        P(),
        P(("grp", "mlp"), "seq", None),
    )
    out_specs = (
        P(("grp", "mlp"), "seq", None),
        P(("grp", "mlp"), "seq", None),
        P(("seq", "mlp"), None),
        P(None, ("seq", "mlp")),
        P(("seq", "mlp")),
        P(("seq", "mlp")),
        P(("seq", "mlp"), None),
        P(("seq", "mlp"), None),
        P(("seq", "mlp")),
        P("seq", "mlp"),
        P(("seq", "mlp")),
        P("mlp", "seq"),
        P(("seq", "mlp")),
    )
    body = four_shards if mesh.shape["seq"] == 4 and mesh.shape["grp"] == 2 else shards
    return jax.shard_map(body, mesh=mesh, in_specs=in_specs, out_specs=out_specs, check_vma=False)
```

```python
import math

import jax
import jax.numpy as jnp
from jax import lax
from jax.experimental import pallas as pl
from jax.experimental.pallas import tpu as pltpu
from jax.sharding import PartitionSpec as P

HD = 64


highest = lax.Precision.HIGHEST


def shifted(value, axis, steps):
    count = lax.axis_size(axis)
    pairs = [(source, (source + steps) % count) for source in range(count)]
    return lax.ppermute(value, axis, pairs)


def layer_norm(values, norm_gain):
    centred = values - jnp.mean(values, axis=-1, keepdims=True)
    spread = jnp.mean(centred * centred, axis=-1, keepdims=True)
    return centred * lax.rsqrt(spread + 1e-05) * norm_gain


def modulate(values, norm_gain, shift_part, scale_part):
    return layer_norm(values, norm_gain) * (1.0 + scale_part) + shift_part


def gelu_tanh(values):
    return jax.nn.gelu(values, approximate=True)


def rotate_pairs(values, positions):
    half_dim = HD // 2
    frequency = jnp.exp(jnp.arange(half_dim, dtype=jnp.float32) * (-2.0 * math.log(10000.0) / HD))
    angles = positions.astype(jnp.float32)[:, None] * frequency[None, :]
    cosine = jnp.cos(angles)[:, None, :]
    sine_part = jnp.sin(angles)[:, None, :]
    leading = values[..., :half_dim]
    trailing = values[..., half_dim:]
    return jnp.concatenate(
        [leading * cosine - trailing * sine_part, trailing * cosine + leading * sine_part], axis=-1
    )


def shards(
    tokens,
    step_index,
    time_table,
    ada_weight,
    ada_bias,
    first_gain,
    qkv_weight,
    out_weight,
    second_gain,
    up_weight,
    up_bias,
    down_weight,
    down_bias,
    cotangent,
):
    seq_count = lax.axis_size("seq")
    seq_place = lax.axis_index("seq")
    group_index = lax.axis_index("grp")
    mlp_place = lax.axis_index("mlp")
    tok_rows = tokens.shape[1]
    model_width = tokens.shape[2]
    head_count = model_width // HD
    score_scale = 1.0 / math.sqrt(HD)
    line_len = tok_rows * seq_count
    seq_length = jnp.where(group_index == 0, line_len // 4, line_len).astype(jnp.int32)
    row_ids = jnp.arange(tok_rows, dtype=jnp.int32)
    own_pos = seq_place * tok_rows + row_ids
    positions = own_pos % seq_length
    quarter = seq_place // (seq_count // 4)
    step_value = jnp.sum(jnp.where(jnp.arange(4, dtype=jnp.int32) == quarter, step_index[0], 0))
    table_pick = jnp.arange(time_table.shape[0], dtype=jnp.int32) == step_value
    embedded = jnp.dot(
        table_pick.astype(jnp.bfloat16)[None, :], time_table, preferred_element_type=jnp.float32
    )[0]
    condition, silu_back = jax.vjp(jax.nn.silu, embedded)
    cond_low = condition.astype(jnp.bfloat16)
    modulation = jnp.dot(cond_low[None, :], ada_weight, preferred_element_type=jnp.float32)[
        0
    ] + ada_bias.astype(jnp.float32)
    shift_one, scale_one, gate_one, shift_two, scale_two, gate_two = jnp.split(modulation, 6)
    inputs = tokens[0].astype(jnp.float32)
    normed, first_back = jax.vjp(
        modulate, inputs, first_gain.astype(jnp.float32), shift_one, scale_one
    )
    normed_low = normed.astype(jnp.bfloat16)
    mixed_rows = jnp.dot(normed_low, qkv_weight, preferred_element_type=jnp.float32)

    def rotate_all(mixed_in):
        query_part = rotate_pairs(
            mixed_in[:, :model_width].reshape(tok_rows, head_count, HD), positions
        )
        key_part = rotate_pairs(
            mixed_in[:, model_width : 2 * model_width].reshape(tok_rows, head_count, HD), positions
        )
        return (
            query_part,
            key_part,
            mixed_in[:, 2 * model_width :].reshape(tok_rows, head_count, HD),
        )

    rotated, rotate_back = jax.vjp(rotate_all, mixed_rows)
    queries = rotated[0].astype(jnp.bfloat16)
    key_rows = rotated[1].astype(jnp.bfloat16)
    value_rows = rotated[2].astype(jnp.bfloat16)
    start_state = (
        jnp.full((head_count, tok_rows), -1e30, jnp.float32),
        jnp.zeros((head_count, tok_rows), jnp.float32),
        jnp.zeros((head_count, tok_rows, HD), jnp.float32),
    )
    key_piece = lax.all_gather(key_rows.reshape(tok_rows, model_width), "seq", axis=0, tiled=True)
    value_piece = lax.all_gather(
        value_rows.reshape(tok_rows, model_width), "seq", axis=0, tiled=True
    )
    piece_rows = key_piece.shape[0]
    sub_rows = math.gcd(piece_rows, 512)

    def one_block(block_index, block_state):
        run_max, run_total, run_acc = block_state
        offset = block_index * sub_rows
        key_block = lax.dynamic_slice_in_dim(key_piece, offset, sub_rows, 0).reshape(
            sub_rows, head_count, HD
        )
        value_block = lax.dynamic_slice_in_dim(value_piece, offset, sub_rows, 0).reshape(
            sub_rows, head_count, HD
        )
        key_pos = offset + jnp.arange(sub_rows, dtype=jnp.int32)
        same_seq = (own_pos // seq_length)[:, None] == (key_pos // seq_length)[None, :]
        scores = (
            jnp.einsum("qhd,khd->hqk", queries, key_block, preferred_element_type=jnp.float32)
            * score_scale
        )
        masked = jnp.where(same_seq[None], scores, -1e30)
        new_max = jnp.maximum(run_max, jnp.max(masked, axis=-1))
        shrink = jnp.exp(run_max - new_max)
        weights = jnp.where(same_seq[None], jnp.exp(masked - new_max[..., None]), 0.0)
        run_total = run_total * shrink + jnp.sum(weights, axis=-1)
        run_acc = run_acc * shrink[..., None] + jnp.einsum(
            "hqk,khd->hqd",
            weights.astype(jnp.bfloat16),
            value_block,
            preferred_element_type=jnp.float32,
        )
        return (new_max, run_total, run_acc)

    run_max, run_total, run_acc = lax.fori_loop(0, piece_rows // sub_rows, one_block, start_state)
    log_total = run_max + jnp.log(run_total)
    attended3 = jnp.transpose(run_acc / run_total[..., None], (1, 0, 2))
    attended_low = attended3.reshape(tok_rows, model_width).astype(jnp.bfloat16)
    branch = jnp.dot(attended_low, out_weight, preferred_element_type=jnp.float32)
    middle = inputs + gate_one * branch
    hidden, second_back = jax.vjp(
        modulate, middle, second_gain.astype(jnp.float32), shift_two, scale_two
    )
    hidden_low = hidden.astype(jnp.bfloat16)
    gathered = lax.all_gather(hidden_low, "mlp", axis=0, tiled=True)
    pre_act = jnp.dot(gathered, up_weight, preferred_element_type=jnp.float32) + up_bias.astype(
        jnp.float32
    )
    activated, gelu_back = jax.vjp(gelu_tanh, pre_act)
    act_low = activated.astype(jnp.bfloat16)
    feed_terms = jnp.dot(act_low, down_weight, preferred_element_type=jnp.float32)
    feed_out = lax.psum_scatter(
        feed_terms, "mlp", scatter_dimension=0, tiled=True
    ) + down_bias.astype(jnp.float32)
    output = (middle + gate_two * feed_out).astype(jnp.bfloat16)[None]
    grad_out = cotangent[0].astype(jnp.float32)
    gate_two_grad = jnp.sum(grad_out * feed_out, axis=0)
    grad_feed = (gate_two * grad_out).astype(jnp.bfloat16)
    down_bias_grad = jnp.sum(grad_feed, axis=0, dtype=jnp.float32)
    grad_rows = lax.all_gather(grad_feed, "mlp", axis=0, tiled=True)
    down_grad = jnp.einsum("tf,td->fd", act_low, grad_rows, preferred_element_type=jnp.float32)
    grad_act = jnp.einsum("td,fd->tf", grad_rows, down_weight, preferred_element_type=jnp.float32)
    grad_pre = gelu_back(grad_act)[0].astype(jnp.bfloat16)
    up_grad = jnp.einsum("td,tf->df", gathered, grad_pre, preferred_element_type=jnp.float32)
    local_units = up_weight.shape[1]
    bias_slot = lax.dynamic_update_slice_in_dim(
        jnp.zeros((local_units * lax.axis_size("mlp"),), jnp.float32),
        jnp.sum(grad_pre, axis=0, dtype=jnp.float32),
        mlp_place * local_units,
        0,
    )
    hidden_terms = jnp.einsum("tf,df->td", grad_pre, up_weight, preferred_element_type=jnp.float32)
    grad_hidden = lax.psum_scatter(hidden_terms, "mlp", scatter_dimension=0, tiled=True)
    middle_part, second_gain_grad, shift_two_grad, scale_two_grad = second_back(grad_hidden)
    middle_grad = grad_out + middle_part
    gate_one_grad = jnp.sum(middle_grad * branch, axis=0)
    grad_branch = (gate_one * middle_grad).astype(jnp.bfloat16)
    out_grad = jnp.einsum(
        "td,te->de", attended_low, grad_branch, preferred_element_type=jnp.float32
    )
    grad_attended = jnp.einsum(
        "te,de->td", grad_branch, out_weight, preferred_element_type=jnp.float32
    ).astype(jnp.bfloat16)
    grad_heads = grad_attended.reshape(tok_rows, head_count, HD)
    row_delta = jnp.transpose(jnp.sum(grad_heads.astype(jnp.float32) * attended3, axis=-1))

    def pair_grads(
        query_set, grad_set, total_set, delta_set, query_anchor, key_set, value_set, key_anchor
    ):
        query_pos = query_anchor * tok_rows + row_ids
        key_pos = key_anchor * tok_rows + row_ids
        same_seq = (query_pos // seq_length)[:, None] == (key_pos // seq_length)[None, :]
        scores = (
            jnp.einsum("qhd,khd->hqk", query_set, key_set, preferred_element_type=jnp.float32)
            * score_scale
        )
        prob_rows = jnp.where(same_seq[None], jnp.exp(scores - total_set[..., None]), 0.0)
        value_part = jnp.einsum(
            "hqk,qhd->khd",
            prob_rows.astype(jnp.bfloat16),
            grad_set,
            preferred_element_type=jnp.float32,
        )
        prob_grad = jnp.einsum(
            "qhd,khd->hqk", grad_set, value_set, preferred_element_type=jnp.float32
        )
        score_grad = (prob_rows * (prob_grad - delta_set[..., None])).astype(jnp.bfloat16)
        query_part = (
            jnp.einsum("hqk,khd->qhd", score_grad, key_set, preferred_element_type=jnp.float32)
            * score_scale
        )
        key_part = (
            jnp.einsum("hqk,qhd->khd", score_grad, query_set, preferred_element_type=jnp.float32)
            * score_scale
        )
        return (query_part, key_part, value_part)

    zero_heads = jnp.zeros((tok_rows, head_count, HD), jnp.float32)

    def key_turn(running):
        key_set, value_set, key_acc, value_acc, anchor, query_acc = running
        query_part, key_part, value_part = pair_grads(
            queries, grad_heads, log_total, row_delta, seq_place, key_set, value_set, anchor
        )
        moved_rows = shifted((key_set, value_set), "seq", 1)
        moved_grads = shifted((key_acc + key_part, value_acc + value_part), "seq", 1)
        return (
            moved_rows[0],
            moved_rows[1],
            moved_grads[0],
            moved_grads[1],
            (anchor - 1) % seq_count,
            query_acc + query_part,
        )

    def two_key_turns(turn_index, running):
        return key_turn(key_turn(running))

    finished = lax.fori_loop(
        0,
        seq_count // 2,
        two_key_turns,
        (key_rows, value_rows, zero_heads, zero_heads, seq_place, zero_heads),
    )
    query_grad, key_grad, value_grad = (finished[5], finished[2], finished[3])
    mixed_grad = rotate_back((query_grad, key_grad, value_grad))[0].astype(jnp.bfloat16)
    qkv_grad = jnp.einsum("td,te->de", normed_low, mixed_grad, preferred_element_type=jnp.float32)
    grad_normed = jnp.einsum(
        "te,de->td", mixed_grad, qkv_weight, preferred_element_type=jnp.float32
    )
    input_part, first_gain_grad, shift_one_grad, scale_one_grad = first_back(grad_normed)
    input_grad = (middle_grad + input_part)[None]
    mod_grad = jnp.concatenate(
        [
            shift_one_grad,
            scale_one_grad,
            gate_one_grad,
            shift_two_grad,
            scale_two_grad,
            gate_two_grad,
        ]
    )
    ada_grad = cond_low.astype(jnp.float32)[:, None] * mod_grad[None, :]
    cond_grad = jnp.dot(ada_weight.astype(jnp.float32), mod_grad, precision=highest)
    table_local = table_pick.astype(jnp.float32)[:, None] * silu_back(cond_grad)[0][None, :]
    layer_sums = (
        lax.psum_scatter(table_local, ("seq", "mlp"), scatter_dimension=0, tiled=True),
        lax.psum_scatter(ada_grad, ("seq", "mlp"), scatter_dimension=1, tiled=True),
        lax.psum_scatter(mod_grad, ("seq", "mlp"), scatter_dimension=0, tiled=True),
        lax.psum_scatter(first_gain_grad, ("seq", "mlp"), scatter_dimension=0, tiled=True),
        lax.psum_scatter(qkv_grad, ("seq", "mlp"), scatter_dimension=0, tiled=True),
        lax.psum_scatter(out_grad, ("seq", "mlp"), scatter_dimension=0, tiled=True),
        lax.psum_scatter(second_gain_grad, ("seq", "mlp"), scatter_dimension=0, tiled=True),
        lax.psum_scatter(bias_slot, ("seq", "mlp"), scatter_dimension=0, tiled=True),
        lax.psum_scatter(down_bias_grad, ("seq", "mlp"), scatter_dimension=0, tiled=True),
    )
    feed_summed = (
        lax.psum_scatter(up_grad, "seq", scatter_dimension=0, tiled=True),
        lax.psum_scatter(down_grad, "seq", scatter_dimension=1, tiled=True),
    )
    totals = lax.psum(
        (
            layer_sums[0],
            layer_sums[1],
            layer_sums[2],
            layer_sums[3],
            layer_sums[4],
            layer_sums[5],
            layer_sums[6],
            layer_sums[7],
            layer_sums[8],
            feed_summed[0],
            feed_summed[1],
        ),
        "grp",
    )
    return (
        output,
        input_grad,
        totals[0],
        totals[1],
        totals[2],
        totals[3],
        totals[4],
        totals[5],
        totals[6],
        totals[9],
        totals[7],
        totals[10],
        totals[8],
    )


LOG_SCALE = math.log2(math.e) / math.sqrt(HD)
NT = (((1,), (1,)), ((), ()))
TN = (((0,), (0,)), ((), ()))
F32 = jnp.float32
BF16 = jnp.bfloat16
WHOLE_VMEM = 60 * 1024 * 1024


def params(*semantics):
    return pltpu.CompilerParams(vmem_limit_bytes=WHOLE_VMEM, dimension_semantics=semantics)


def low_lanes(value):
    return lax.broadcasted_iota(jnp.int32, value.shape, 1) < HD


def swap_heads(value):
    return pltpu.roll(value, HD, 1)


def exchange(top, bottom):
    keep = low_lanes(top)
    return (
        jnp.where(keep, top, swap_heads(bottom)),
        jnp.where(keep, swap_heads(top), bottom),
    )


def fold(value):
    half = value.shape[0] // 2
    top = value[:half]
    return jnp.where(low_lanes(top), top, swap_heads(value[half:]))


def unfold_into(target, base, packed, fill):
    half = packed.shape[0]
    value = packed.astype(F32)
    keep = low_lanes(value)
    target[base : base + half, :] = jnp.where(keep, value, fill).astype(BF16)
    target[base + half : base + 2 * half, :] = jnp.where(keep, swap_heads(value), fill).astype(BF16)


def turn(value, cosine, sine):
    lane = lax.broadcasted_iota(jnp.int32, value.shape, 1) % HD
    quarter = HD // 2
    other = jnp.where(
        lane < quarter, pltpu.roll(value, 2 * HD - quarter, 1), pltpu.roll(value, quarter, 1)
    )
    return value * cosine + other * sine


def normalise(values):
    centred = values - jnp.mean(values, axis=-1, keepdims=True)
    spread = jnp.mean(centred * centred, axis=-1, keepdims=True)
    inverse = lax.rsqrt(spread + 1e-05)
    return centred * inverse, inverse


def attend_rows(q, k_ref, v_ref, keys, out_put, log_put, block=512):
    top = None
    for start in range(0, keys, block):
        s = lax.dot_general(q, k_ref[start : start + block, :], NT, preferred_element_type=F32)
        s = s * LOG_SCALE
        peak = jnp.max(s, axis=1, keepdims=True)
        new_top = peak if top is None else jnp.maximum(top, peak)
        p = jnp.exp2(s - new_top).astype(BF16)
        part = jnp.dot(p, v_ref[start : start + block, :], preferred_element_type=F32)
        acc = part if top is None else acc * jnp.exp2(top - new_top) + part
        top = new_top
    out_put(fold(acc / swap_heads(acc)).astype(BF16))
    log_put((top + jnp.log2(acc)).T[HD : HD + 8])


def load_values(source, base, k_s, v_s):
    unfold_into(k_s, base, source[1], 0.0)
    unfold_into(v_s, base, source[2], 1.0)


def packed_queries(packed):
    value = packed.astype(F32)
    return jnp.concatenate([value, swap_heads(value)]).astype(BF16)


def push(src, dst, sems, index, where):
    return pltpu.make_async_remote_copy(
        src_ref=src, dst_ref=dst, send_sem=sems[0].at[index], recv_sem=sems[1].at[index],
        device_id=where, device_id_type=pl.DeviceIdType.MESH,
    )


def reach(src, dst, sems, index, group, place):
    return push(src, dst, sems, index, {"grp": group, "seq": place})


def neighbours(group, place, others):
    found = [
        {"grp": (group + other) % 2, "seq": (place + steps) % 4}
        for other in range(2)
        for steps in range(4)
        if other or steps
    ]
    return found + [{"mlp": other} for other in others]


def greet(devices):
    barrier = pltpu.get_barrier_semaphore()
    for where in devices:
        pl.semaphore_signal(barrier, 1, device_id=where, device_id_type=pl.DeviceIdType.MESH)
    pl.semaphore_wait(barrier, len(devices))


def mlp_place():
    mlp = lax.axis_index("mlp")
    row, core = mlp // 2, mlp % 2
    return row, core, (1 - row) * 2 + core, row * 2 + 1 - core


BLOCKS = 18


def added(left, right):
    return (left.astype(F32) + right.astype(F32)).astype(BF16)


def sum_steps(held, one_p, one_q, two, others, three, out, sems, base, near=None):
    near = held if near is None else near
    group = lax.axis_index("grp")
    place = lax.axis_index("seq")
    row, _, other_row, _ = mlp_place()
    by_row = {"mlp": other_row}
    by_group = {"grp": 1 - group}
    ahead = lambda s: (place + s) % 4

    def copies(stage):
        if stage == 1:
            return [
                push(held.at[1 - row, :, pl.ds(0, 10)], one_p, sems, base, by_row),
                push(
                    held.at[:, :, pl.ds(10 + 4 * (1 - group), 4)], one_q, sems, base + 1, by_group
                ),
            ]
        if stage == 2:
            return [
                push(
                    one_p.at[:, pl.ds(5 * (1 - group), 5)], two.at[:, pl.ds(0, 5)], sems,
                    base + 2, by_group,
                ),
                push(one_q.at[1 - row], two.at[:, pl.ds(5, 4)], sems, base + 3, by_row),
            ]
        if stage == 3:
            return [
                push(two.at[ahead(s)], others.at[s - 1], sems, base + 3 + s, {"seq": ahead(s)})
                for s in (1, 2, 3)
            ]
        return [
            push(three.at[pl.ds(0, 5)], out.at[pl.ds(5 * group, 5)], sems, base + 7, by_group),
            push(
                three.at[pl.ds(5, 4)], out.at[pl.ds(10 + 4 * group, 4)], sems, base + 8, by_group
            ),
        ]

    def start(stage):
        for copy in copies(stage):
            copy.start()

    def arrive(stage):
        for copy in copies(stage):
            copy.wait()

    def step_one():
        start(1)

    def step_two():
        arrive(1)

        def add(z, carry):
            one_p[z] = added(near[row, z, 0:10], one_p[z])
            for y in range(2):
                one_q[y, z] = added(near[y, z, pl.ds(10 + 4 * group, 4)], one_q[y, z])
            return carry

        lax.fori_loop(0, 4, add, 0)
        start(2)

    def step_three():
        arrive(2)

        def add(z, carry):
            two[z, 0:5] = added(one_p[z, pl.ds(5 * group, 5)], two[z, 0:5])
            two[z, 5:9] = added(one_q[row, z], two[z, 5:9])
            return carry

        lax.fori_loop(0, 4, add, 0)

    def step_over():
        start(3)

    def step_four():
        arrive(3)

        def add(block, carry):
            total = two[place, block].astype(F32)
            for s in range(3):
                total = total + others[s, block].astype(F32)
            three[block] = total.astype(BF16)
            return carry

        lax.fori_loop(0, 9, add, 0)
        start(4)
        out[pl.ds(5 * group, 5)] = three[0:5]
        out[pl.ds(10 + 4 * group, 4)] = three[5:9]

    def step_five():
        arrive(4)

    return step_one, step_two, step_three, step_over, step_four, step_five


def sum_scratch(rows, shapes):
    return [pltpu.VMEM(shape + (rows, 2 * HD), BF16) for shape in shapes]


EARLY = [(4, 10), (2, 4, 4)]
MIDDLE = [(4, 9)]
LATE = [(3, 9), (9,)]


def forward_kernel(
    x_ref, w_ref, near, far, step_ref, table, ada_ref, params_ref,
    packs, att, pieces, results, logs, logs_own, cosine, sine, vec_one, vec_two, extra, bias_all,
    blocks, crossed, normed_s, k_s, v_s, send_sems, recv_sems,
):
    group = lax.axis_index("grp")
    place = lax.axis_index("seq")
    sems = (send_sems, recv_sems)
    heads = packs.shape[0]
    rows = 2 * packs.shape[2]
    ahead = lambda s: (place + s) % 4
    behind = lambda s: (place + 4 - s) % 4

    def first(s):
        return reach(packs.at[2 * ahead(s)], pieces.at[0, s], sems, s - 1, 1, ahead(s))

    def second_values(s):
        source = packs.at[2 * ahead(s) + 1, pl.ds(1, 2)]
        return reach(source, pieces.at[1, s, pl.ds(1, 2)], sems, 2 + s, 1, ahead(s))

    def second_queries(s):
        source = packs.at[2 * ahead(s) + 1, 0]
        return reach(source, pieces.at[1, s, 0], sems, 5 + s, 1, ahead(s))

    def cross(s):
        return reach(packs.at[8 + ahead(s)], crossed.at[s], sems, 9 + s, 0, place)

    def onward(s):
        return reach(crossed.at[s], pieces.at[1, s], sems, 12 + s, 0, ahead(s))

    def home(kind, s, head):
        start = (16, 20, 24)[kind]
        return reach(
            results.at[min(kind, 1), s], att.at[head], sems, start + s, 1, behind(s)
        )

    row, core, _, _ = mlp_place()
    mlp = row * 2 + core
    greet(neighbours(group, place, [(mlp + s) % 4 for s in (1, 2, 3)]))
    width = w_ref.shape[0]
    vectors = params_ref[...].astype(F32)
    vector = lambda index: vectors[:, index * width : (index + 1) * width]
    first_gain, second_gain, down_bias = vector(6), vector(7), vector(8)
    up_bias = vectors[:, 9 * width :]
    bias_all[mlp] = jnp.broadcast_to(up_bias, bias_all.shape[1:])

    def share_bias(s, owner):
        own = bias_all.at[owner]
        return push(own, own, sems, 27 + s, {"mlp": (mlp + s) % 4})

    for s in (1, 2, 3):
        share_bias(s, mlp).start()

    half = packs.shape[2]
    lanes = 2 * HD
    quarters = step_ref[...].astype(F32)
    own_quarter = lax.broadcasted_iota(jnp.int32, quarters.shape, 1) == place
    step = jnp.sum(jnp.where(own_quarter, quarters, 0.0), axis=1, keepdims=True)
    entries = lax.broadcasted_iota(jnp.int32, (16, table.shape[0]), 1).astype(F32)
    chosen = jnp.where(entries == step, 1.0, 0.0).astype(BF16)
    embedded = jnp.dot(chosen, table[...], preferred_element_type=F32)
    gate = 1.0 / (1.0 + jnp.exp(-embedded))
    condition = embedded * gate
    modulation = jnp.dot(condition.astype(BF16), ada_ref[...], preferred_element_type=F32)
    modulation = modulation[0:1] + vectors[:, : 6 * width]
    part = lambda index: modulation[:, index * width : (index + 1) * width]
    for target, values in (
        (vec_one, (first_gain, part(1), part(0))),
        (
            vec_two,
            (part(2), second_gain, part(4), part(3), part(5), down_bias),
        ),
        (
            extra,
            (
                condition[0:1], jnp.broadcast_to(step, (1, condition.shape[1])),
                (gate * (1.0 + embedded * (1.0 - gate)))[0:1],
            ),
        ),
    ):
        target[...] = jnp.zeros_like(target)
        for index, value in enumerate(values):
            target[index : index + 1, :] = value

    near_rows = near.shape[1]
    first_half = lax.broadcasted_iota(jnp.int32, near.shape[1:], 1) % HD < HD // 2
    for index in range(far.shape[1]):
        far_cos, far_sin = far[0, index : index + 1, :], far[1, index : index + 1, :]
        start = index * near_rows
        at = slice(start % half, start % half + near_rows)
        value = far_sin * near[0] + far_cos * near[1]
        cosine[start // half, at, :] = far_cos * near[0] - far_sin * near[1]
        sine[start // half, at, :] = jnp.where(first_half, -value, value)

    tile = half // 2

    def normal(index, carry):
        at = pl.ds(pl.multiple_of(index * tile, tile), tile)
        for side in range(2):
            n, _ = normalise(x_ref[side, at, :].astype(F32))
            value = n * vec_one[0:1, :] * (1.0 + vec_one[1:2, :]) + vec_one[2:3, :]
            normed_s[side, at, :] = value.astype(BF16)
        return carry

    lax.fori_loop(0, 2, normal, 0)

    def project(low_pair, count):
        def tokens(index, carry):
            at = pl.ds(pl.multiple_of(index * tile, tile), tile)
            normed = normed_s[:, at, :].reshape(2 * tile, width)
            turn_cos = cosine[:, at, :].reshape(2 * tile, lanes)
            turn_sin = sine[:, at, :].reshape(2 * tile, lanes)
            for kind in range(3):
                start = kind * width + low_pair * lanes
                mixed = jnp.dot(
                    normed, w_ref[:, start : start + count * lanes], preferred_element_type=F32
                )
                for pair in range(count):
                    value = mixed[:, pair * lanes : (pair + 1) * lanes]
                    if kind < 2:
                        value = turn(value, turn_cos, turn_sin)
                    even, odd = exchange(value[:tile], value[tile:])
                    head = 2 * (low_pair + pair)
                    packs[head, kind, at, :] = even.astype(BF16)
                    packs[head + 1, kind, at, :] = odd.astype(BF16)
            return carry

        lax.fori_loop(0, 2, tokens, 0)

    def full(kind, head, before, after):
        sel = min(kind, 1)
        for s in range(4):
            load_values(pieces.at[sel, s], s * rows, k_s, v_s)

        def step(s, carry):
            before(s)

            def put_out(value):
                results[sel, s] = value

            def put_log(value):
                logs[sel, s] = value

            q = packed_queries(pieces[sel, s, 0])
            attend_rows(q, k_s, v_s, 4 * rows, put_out, put_log)
            after(s)
            return carry

        lax.fori_loop(0, 4, step, 0)

    project(0, 4)

    @pl.when(group == 1)
    def _():
        for s in (1, 2, 3):
            first(s).start()

    project(4, 2)

    @pl.when(group == 1)
    def _():
        for s in (1, 2, 3, 0):
            cross(s).start()

    flipped = normed_s[...].reshape(2 * half, width).T
    part_rows = width // 16
    for which in range(2):
        for y in range(2):
            for z in range(4):
                start = ((z * 2 + y) * 2 + which) * part_rows
                at = (y * 4 + z) * part_rows
                blocks[which, at : at + part_rows, :] = flipped[start : start + part_rows]

    @pl.when(group == 1)
    def _():
        pieces[0, 0] = packs[2 * place]
        pieces[1, 0] = packs[2 * place + 1]
        for s in (1, 2, 3):
            first(s).wait_send()
        for s in (1, 2, 3):
            second_values(s).start()
        for s in (1, 2, 3):
            first(s).wait_recv()

        def before(s):
            @pl.when(s == 3)
            def _():
                for other in (1, 2, 3):
                    second_queries(other).start()

        def after(s):
            @pl.when(s == 0)
            def _():
                att[2 * place] = results[0, 0]

            @pl.when(s > 0)
            def _():
                home(0, s, 2 * place).start()

        full(0, 2 * place, before, after)
        for s in (1, 2, 3):
            second_values(s).wait_recv()

    @pl.when(group == 0)
    def _():
        def local(head, carry):
            load_values(packs.at[head], 0, k_s, v_s)

            def put_out(value):
                att[head] = value

            def put_log(value):
                logs_own[head] = value

            attend_rows(packed_queries(packs[head, 0]), k_s, v_s, rows, put_out, put_log)
            for s in (1, 2, 3):

                @pl.when(head == 4 * s - 1)
                def _(s=s):
                    cross(s).wait_recv()
                    onward(s).start()

            return carry

        lax.fori_loop(0, heads, local, 0)
        cross(0).wait_recv()
        pieces[1, 0] = crossed[0]
        for s in (1, 2, 3):
            onward(s).wait_recv()

    def before(s):
        @pl.when((group == 1) & (s > 0))
        def _():
            second_queries(s).wait_recv()

    def after(s):
        @pl.when((group == 1) & (s == 0))
        def _():
            att[2 * place + 1] = results[1, 0]

        @pl.when((group == 1) & (s > 0))
        def _():
            home(1, s, 2 * place + 1).start()

        @pl.when(group == 0)
        def _():
            home(2, s, 8 + place).start()

    full(1, 0, before, after)

    @pl.when(group == 1)
    def _():
        for s in (1, 2, 3):
            second_values(s).wait_send()
            second_queries(s).wait_send()
            for kind in (0, 1):
                home(kind, s, 2 * place + kind).wait_send()
        for s in range(4):
            cross(s).wait_send()
        for s in (1, 2, 3):
            for kind in (0, 1):
                home(kind, s, 2 * ahead(s) + kind).wait_recv()
        for s in range(4):
            home(2, s, 8 + ahead(s)).wait_recv()

    @pl.when(group == 0)
    def _():
        for s in (1, 2, 3):
            onward(s).wait_send()
        for s in range(4):
            home(2, s, 8 + place).wait_send()

    for s in (1, 2, 3):
        share_bias(s, mlp).wait_send()
        share_bias(s, (mlp + 4 - s) % 4).wait_recv()


def in_vmem(count):
    return [pl.BlockSpec(memory_space=pltpu.VMEM)] * count


def forward_attention(x2, weight, *rest):
    _, half, width = x2.shape
    heads, lanes = width // HD, 2 * HD
    shapes = [
        ((heads, 3, half, lanes), BF16),
        ((heads, half, lanes), BF16),
        ((2, 4, 3, half, lanes), BF16),
        ((2, 4, half, lanes), BF16),
        ((2, 4, 8, 2 * half), F32),
        ((heads, 8, 2 * half), F32),
        ((2, half, lanes), F32),
        ((2, half, lanes), F32),
        ((8, width), F32),
        ((8, width), F32),
        ((8, rest[3].shape[1]), F32),
        ((4, 8, rest[-1].shape[1] - 9 * width), F32),
        ((2, width // 2, 2 * half), BF16),
    ]
    return pl.pallas_call(
        forward_kernel,
        in_specs=in_vmem(2 + len(rest)),
        out_specs=in_vmem(len(shapes)),
        out_shape=[jax.ShapeDtypeStruct(shape, kind) for shape, kind in shapes],
        scratch_shapes=[
            pltpu.VMEM((4, 3, half, lanes), BF16),
            pltpu.VMEM((2, half, width), BF16),
            pltpu.VMEM((8 * half, lanes), BF16),
            pltpu.VMEM((8 * half, lanes), BF16),
            pltpu.SemaphoreType.DMA((31,)),
            pltpu.SemaphoreType.DMA((31,)),
        ],
        compiler_params=pltpu.CompilerParams(
            collective_id=1, has_side_effects=True, vmem_limit_bytes=WHOLE_VMEM
        ),
        cost_estimate=pl.CostEstimate(
            flops=100_000_000_000, bytes_accessed=8_000_000, transcendentals=0
        ),
        name="forward_attention",
    )(x2, weight, *rest)


def tile_grads(q, do, k, v, log_row, delta_row):
    s = lax.dot_general(k, q, NT, preferred_element_type=F32)
    p = jnp.exp2(s * LOG_SCALE - log_row)
    dp = lax.dot_general(v, do, NT, preferred_element_type=F32)
    ds = (p * (dp - delta_row)).astype(BF16)
    dv = jnp.dot(p.astype(BF16), do, preferred_element_type=F32)
    dk = jnp.dot(ds, q, preferred_element_type=F32)
    dq = lax.dot_general(k, ds, TN, preferred_element_type=F32)
    return dq, dk, dv


def load_backward(source, do, o, base, q_s, k_s, v_s, do_s, delta_s):
    half = do.shape[0]
    unfold_into(q_s, base, source[0], 0.0)
    unfold_into(k_s, base, source[1], 0.0)
    unfold_into(v_s, base, source[2], 0.0)
    unfold_into(do_s, base, do, 0.0)
    product = (do.astype(F32) * o.astype(F32)).T
    first = jnp.sum(product[:HD], axis=0, keepdims=True)
    second = jnp.sum(product[HD:], axis=0, keepdims=True)
    delta_s[:, base : base + half] = jnp.broadcast_to(first, (8, half))
    delta_s[:, base + half : base + 2 * half] = jnp.broadcast_to(second, (8, half))


def backward_kernel(
    packs_ref, gatt_ref, att_ref, held_ref, pieces, results, logs, logs_own, dos, back, two,
    packs, gatt, att, held, staged, q_s, k_s, v_s, do_s, delta_s, dq_s, one_p, one_q,
    send_sems, recv_sems, own_sems,
):
    group = lax.axis_index("grp")
    place = lax.axis_index("seq")
    sems = (send_sems, recv_sems)
    heads = packs.shape[0]
    rows = 2 * packs.shape[2]
    scale = 1.0 / math.sqrt(HD)
    ahead = lambda s: (place + s) % 4
    behind = lambda s: (place + 4 - s) % 4
    stores = (q_s, k_s, v_s, do_s, delta_s)

    def home_values(kind, s, head):
        source = staged.at[min(kind, 1), s, pl.ds(1, 2)]
        return reach(
            source, back.at[head, pl.ds(1, 2)], sems, (0, 4, 8)[kind] + s, 1, behind(s)
        )

    def home_queries(kind, s, head):
        source = staged.at[min(kind, 1), s, 0]
        return reach(source, back.at[head, 0], sems, (12, 16, 20)[kind] + s, 1, behind(s))

    greet(neighbours(group, place, [mlp_place()[2]]))
    sum_one, sum_two, sum_three, _, _, _ = sum_steps(
        held_ref, one_p, one_q, two, None, None, None, sems, 24, held
    )
    sum_one()
    load_held = pltpu.make_async_copy(held_ref, held, own_sems.at[3])
    load_held.start()
    local_loads = [
        pltpu.make_async_copy(source, target, own_sems.at[index])
        for index, (source, target) in enumerate(
            ((packs_ref, packs), (gatt_ref, gatt), (att_ref, att))
        )
    ]

    @pl.when(group == 0)
    def _():
        for load in local_loads:
            load.start()

    def full(sel, put_values, put_queries):
        for s in range(4):
            load_backward(
                pieces.at[sel, s], dos[sel, s], results[sel, s], s * rows, *stores
            )

        def step(s, carry):
            block = pl.ds(pl.multiple_of(s * rows, rows), rows)
            k = k_s[block, :]
            v = v_s[block, :]
            dk = dv = None
            for index in range(4):
                chunk = slice(index * rows, (index + 1) * rows)
                dq, dk_part, dv_part = tile_grads(
                    q_s[chunk, :], do_s[chunk, :], k, v, logs[sel, index, 0:1, :],
                    delta_s[0:1, chunk],
                )
                dk = dk_part if dk is None else dk + dk_part
                dv = dv_part if dv is None else dv + dv_part
                dq_s[:, chunk] = jnp.where(s == 0, dq, dq_s[:, chunk] + dq)
            staged[sel, s, 1] = fold(dk * scale).astype(BF16)
            staged[sel, s, 2] = fold(dv).astype(BF16)
            put_values(s)
            return carry

        lax.fori_loop(0, 4, step, 0)
        for s in (3, 2, 1, 0):
            chunk = slice(s * rows, (s + 1) * rows)
            staged[sel, s, 0] = fold(dq_s[:, chunk].T * scale).astype(BF16)
            put_queries(s)

    @pl.when(group == 1)
    def _():
        head = 2 * place

        def put_values(s):
            @pl.when(s == 0)
            def _():
                back[head, 1] = staged[0, 0, 1]
                back[head, 2] = staged[0, 0, 2]

            @pl.when(s > 0)
            def _():
                home_values(0, s, head).start()

            @pl.when(s == 2)
            def _():
                load_held.wait()
                sum_two()

        def put_queries(s):
            if s == 0:
                back[head, 0] = staged[0, 0, 0]
            else:
                home_queries(0, s, head).start()

        full(0, put_values, put_queries)

    def put_values(s):
        head = 2 * place + 1

        @pl.when((group == 1) & (s == 0))
        def _():
            back[head, 1] = staged[1, 0, 1]
            back[head, 2] = staged[1, 0, 2]

        @pl.when((group == 1) & (s > 0))
        def _():
            home_values(1, s, head).start()

        @pl.when(group == 0)
        def _():
            home_values(2, s, 8 + place).start()

        @pl.when((group == 0) & (s == 2))
        def _():
            load_held.wait()
            sum_two()

    def put_queries(s):
        head = 2 * place + 1

        @pl.when(group == 1)
        def _():
            if s == 0:
                back[head, 0] = staged[1, 0, 0]
            else:
                home_queries(1, s, head).start()

        @pl.when(group == 0)
        def _():
            home_queries(2, s, 8 + place).start()

    full(1, put_values, put_queries)

    @pl.when(group == 0)
    def _():
        for load in local_loads:
            load.wait()

        def local(head, carry):
            load_backward(packs.at[head], gatt[head], att[head], 0, *stores)
            own = slice(0, rows)
            dq, dk, dv = tile_grads(
                q_s[own, :], do_s[own, :], k_s[own, :], v_s[own, :],
                logs_own[head, 0:1, :], delta_s[0:1, own],
            )
            back[head, 0] = fold(dq.T * scale).astype(BF16)
            back[head, 1] = fold(dk * scale).astype(BF16)
            back[head, 2] = fold(dv).astype(BF16)
            return carry

        lax.fori_loop(0, heads, local, 0)

    sum_three()

    @pl.when(group == 0)
    def _():
        for s in range(4):
            home_values(2, s, 8 + place).wait_send()
            home_queries(2, s, 8 + place).wait_send()

    @pl.when(group == 1)
    def _():
        for s in (1, 2, 3):
            for kind in (0, 1):
                home_values(kind, s, 2 * place + kind).wait_send()
                home_queries(kind, s, 2 * place + kind).wait_send()
        for s in (1, 2, 3):
            for kind in (0, 1):
                home_values(kind, s, 2 * ahead(s) + kind).wait_recv()
                home_queries(kind, s, 2 * ahead(s) + kind).wait_recv()
        for s in range(4):
            home_values(2, s, 8 + ahead(s)).wait_recv()
            home_queries(2, s, 8 + ahead(s)).wait_recv()


def backward_attention(packs, gatt, att, pieces, results, logs, logs_own, dos, held):
    heads, _, half, lanes = packs.shape
    share = held.shape[2:]
    return pl.pallas_call(
        backward_kernel,
        in_specs=[pl.BlockSpec(memory_space=pl.ANY)] * 4 + in_vmem(5),
        out_specs=in_vmem(2),
        out_shape=[
            jax.ShapeDtypeStruct((heads, 3, half, lanes), BF16),
            jax.ShapeDtypeStruct((4, 9) + share[1:], BF16),
        ],
        scratch_shapes=[pltpu.VMEM(value.shape, BF16) for value in (packs, gatt, att, held)]
        + [pltpu.VMEM((2, 4, 3, half, lanes), BF16)]
        + [pltpu.VMEM((8 * half, lanes), BF16)] * 4
        + [pltpu.VMEM((8, 8 * half), F32), pltpu.VMEM((lanes, 8 * half), F32)]
        + sum_scratch(share[1], EARLY)
        + [pltpu.SemaphoreType.DMA((28,))] * 2
        + [pltpu.SemaphoreType.DMA((4,))],
        compiler_params=pltpu.CompilerParams(
            collective_id=2, has_side_effects=True, vmem_limit_bytes=WHOLE_VMEM
        ),
        cost_estimate=pl.CostEstimate(
            flops=120_000_000_000, bytes_accessed=8_000_000, transcendentals=0
        ),
        name="backward_attention",
    )(packs, gatt, att, held, pieces, results, logs, logs_own, dos)


def whole(shape):
    zeros = (0,) * len(shape)
    return pl.BlockSpec(shape, lambda *_: zeros)


def middle_kernel(
    x_ref, cot_ref, att_ref, vec_ref, ow_ref, up_ref, down_ref, bias_ref,
    out_ref, attlow_ref, hidden_ref, act_ref, gfeed_ref, gpre_ref, mgrad_ref, gbranch_ref,
    gatt_ref, sums_ref, upsum_ref, att_s, slope_s,
):
    step = pl.program_id(0)
    rows, width = x_ref.shape[1:]
    both = 2 * rows
    pairs = width // (2 * HD)
    gate_one, gain, scale, shift = (vec_ref[i : i + 1, :] for i in range(4))
    gate_two, down_bias = vec_ref[4:5, :], vec_ref[5:6, :]
    for pair in range(pairs):
        lanes = slice(pair * 2 * HD, (pair + 1) * 2 * HD)
        top, bottom = exchange(
            att_ref[2 * pair].astype(F32), att_ref[2 * pair + 1].astype(F32)
        )
        att_s[:rows, lanes] = top.astype(BF16)
        att_s[rows:, lanes] = bottom.astype(BF16)
    att = att_s[...]
    attlow_ref[...] = att.reshape(2, rows, width)
    branch = jnp.dot(att, ow_ref[...], preferred_element_type=F32)
    middle = x_ref[...].reshape(both, width).astype(F32) + gate_one * branch
    n, inverse = normalise(middle)
    hidden = (n * gain * (1.0 + scale) + shift).astype(BF16)
    hidden_ref[...] = hidden.reshape(2, rows, width)
    shares, _, chunk = up_ref.shape
    feed = None
    for index in range(shares):
        cols = slice(index * chunk, (index + 1) * chunk)
        pre = jnp.dot(hidden, up_ref[index], preferred_element_type=F32)
        pre = pre + bias_ref[index, 0:1]
        square = pre * pre
        root = math.sqrt(2.0 / math.pi)
        tanh = jnp.tanh(pre * (root + (root * 0.044715) * square))
        half_up = 0.5 + 0.5 * tanh
        act = (pre * half_up).astype(BF16)
        slope_s[:, cols] = half_up + (0.5 * pre) * (1.0 - tanh * tanh) * (
            root + (3.0 * root * 0.044715) * square
        )
        act_ref[:, :, cols] = act.reshape(2, rows, chunk)
        part = jnp.dot(act, down_ref[index], preferred_element_type=F32)
        feed = part if feed is None else feed + part
    feed = feed + down_bias
    out_ref[...] = (middle + gate_two * feed).astype(BF16).reshape(2, rows, width)
    cot = cot_ref[...].reshape(both, width).astype(F32)
    gfeed = (gate_two * cot).astype(BF16)
    gfeed_ref[...] = gfeed.reshape(2, rows, width)
    ghidden = None
    up_sums = []
    for index in range(shares):
        cols = slice(index * chunk, (index + 1) * chunk)
        gact = lax.dot_general(gfeed, down_ref[index], NT, preferred_element_type=F32)
        gpre = (gact * slope_s[:, cols]).astype(BF16)
        gpre_ref[:, :, cols] = gpre.reshape(2, rows, chunk)
        up_sums.append(jnp.sum(gpre.astype(F32), axis=0, keepdims=True))
        part = lax.dot_general(gpre, up_ref[index], NT, preferred_element_type=F32)
        ghidden = part if ghidden is None else ghidden + part
    e = ghidden * ((1.0 + scale) * gain)
    mgrad = cot + inverse * (
        e - jnp.mean(e, axis=-1, keepdims=True) - n * jnp.mean(e * n, axis=-1, keepdims=True)
    )
    mgrad_ref[...] = mgrad.reshape(2, rows, width)
    gbranch = (gate_one * mgrad).astype(BF16)
    gbranch_ref[...] = gbranch.reshape(2, rows, width)
    gatt = lax.dot_general(gbranch, ow_ref[...], NT, preferred_element_type=F32)
    for pair in range(pairs):
        value = gatt[:, pair * 2 * HD : (pair + 1) * 2 * HD]
        even, odd = exchange(value[:rows], value[rows:])
        gatt_ref[2 * pair] = even.astype(BF16)
        gatt_ref[2 * pair + 1] = odd.astype(BF16)
    add = lambda value: jnp.sum(value, axis=0, keepdims=True)

    @pl.when(step == 0)
    def _():
        sums_ref[...] = jnp.zeros_like(sums_ref)
        upsum_ref[...] = jnp.zeros_like(upsum_ref)

    sums_ref[0:1, :] += add(ghidden)
    sums_ref[1:2, :] += add(ghidden * n)
    sums_ref[2:3, :] += add(cot * feed)
    sums_ref[3:4, :] += add(gfeed.astype(F32))
    sums_ref[4:5, :] += add(mgrad * branch)
    for index, value in enumerate(up_sums):
        upsum_ref[0:1, index * chunk : (index + 1) * chunk] += value


def once(shape):
    zeros = (0,) * len(shape)
    return pl.BlockSpec(shape, lambda *_: zeros, pipeline_mode=pl.Buffered(1))


def middle_pass(x2, cot2, att, vecs, out_weight, up_all, down_all, bias_all, rows=128):
    half, width = x2.shape[1:]
    heads = width // HD
    units = up_all.shape[0] * up_all.shape[2]
    tok = lambda last: pl.BlockSpec((2, rows, last), lambda i: (0, i, 0))
    pack = pl.BlockSpec((heads, rows, 2 * HD), lambda i: (0, i, 0))
    token = lambda last, kind: jax.ShapeDtypeStruct((2, half, last), kind)
    return pl.pallas_call(
        middle_kernel,
        grid=(half // rows,),
        in_specs=[
            tok(width), tok(width), pack, whole(vecs.shape), once(out_weight.shape),
            once(up_all.shape), once(down_all.shape), once(bias_all.shape),
        ],
        out_specs=[
            tok(width), tok(width), tok(width), tok(units), tok(width), tok(units), tok(width),
            tok(width), pack, whole((8, width)), whole((8, units)),
        ],
        out_shape=[
            token(width, BF16), token(width, BF16), token(width, BF16), token(units, BF16),
            token(width, BF16), token(units, BF16), token(width, F32), token(width, BF16),
            jax.ShapeDtypeStruct((heads, half, 2 * HD), BF16),
            jax.ShapeDtypeStruct((8, width), F32),
            jax.ShapeDtypeStruct((8, units), F32),
        ],
        scratch_shapes=[pltpu.VMEM((2 * rows, width), BF16), pltpu.VMEM((2 * rows, units), F32)],
        compiler_params=params("arbitrary"),
        name="middle_pass",
    )(x2, cot2, att, vecs, out_weight, up_all, down_all, bias_all)


def feed_grads_kernel(
    hidden_ref, gfeed_ref, att_ref, gbranch_ref, act_ref, gpre_ref, gatt, held, dos,
    hidden_s, gfeed_s, att_s, act_s, gpre_s, sent, got, crossed, send_sems, recv_sems, own_sems,
):
    group = lax.axis_index("grp")
    place = lax.axis_index("seq")
    _, core, _, other_core = mlp_place()
    sems = (send_sems, recv_sems)
    ahead = lambda s: (place + s) % 4

    def first(s):
        return reach(gatt.at[2 * ahead(s)], dos.at[0, s], sems, s - 1, 1, ahead(s))

    def second(s):
        return reach(gatt.at[2 * ahead(s) + 1], dos.at[1, s], sems, 2 + s, 1, ahead(s))

    def cross(s):
        return reach(gatt.at[8 + ahead(s)], crossed.at[s], sems, 6 + s, 0, place)

    def onward(s):
        return reach(crossed.at[s], dos.at[1, s], sems, 9 + s, 0, ahead(s))

    def swap(y):
        return push(sent.at[y], got.at[y], sems, 13 + y, {"mlp": other_core})

    width = hidden_s.shape[0]

    def loads(order, index):
        cols = pl.ds(pl.multiple_of(index * width, width), width)
        return (
            pltpu.make_async_copy(gpre_ref.at[:, cols], gpre_s.at[order], own_sems.at[0, order]),
            pltpu.make_async_copy(act_ref.at[:, cols], act_s.at[order], own_sems.at[1, order]),
        )

    for y in range(2):
        for load in loads(y, 2 * y + 1 - core):
            load.start()
    for y in range(2):
        for load in loads(2 + y, 2 * y + core):
            load.start()
    greet(neighbours(group, place, [other_core]))

    @pl.when(group == 1)
    def _():
        for s in (1, 2, 3):
            cross(s).start()
            first(s).start()
            second(s).start()
        cross(0).start()
        dos[0, 0] = gatt[2 * place]
        dos[1, 0] = gatt[2 * place + 1]

    hidden_s[...] = hidden_ref[...].T
    gfeed_s[...] = gfeed_ref[...].T
    att_s[...] = att_ref[...].T
    split = width // 4
    part = split // 4
    rows = 3 * part

    def blocks(target, y, index, order):
        for load in loads(order, index):
            load.wait()
        up = jnp.dot(hidden_s[...], gpre_s[order], preferred_element_type=F32).astype(BF16)
        down = jnp.dot(gfeed_s[...], act_s[order], preferred_element_type=F32).astype(BF16)
        own = jnp.concatenate(
            [
                att_s[pl.ds(pl.multiple_of(index * part + z * split, 16), part), :]
                for z in range(4)
            ]
        )
        out = jnp.dot(own, gbranch_ref[...], preferred_element_type=F32).astype(BF16)
        for z in range(4):
            start = z * split
            pieces = (
                (up[start : start + rows],),
                (up[start + rows : start + split], down[start : start + split - rows + part]),
                (down[start + 2 * part : start + split], out[z * part : (z + 1) * part]),
            )
            for number, values in enumerate(pieces):
                base = 0
                for value in values:
                    size = value.shape[0]
                    for lane in range(width // (2 * HD)):
                        target[y, z, number * 6 + lane, base : base + size, :] = value[
                            :, lane * 2 * HD : (lane + 1) * 2 * HD
                        ]
                    base += size

    def send_row(y, carry):
        blocks(sent, y, 2 * y + 1 - core, y)
        swap(y).start()
        return carry

    lax.fori_loop(0, 2, send_row, 0)

    @pl.when(group == 0)
    def _():
        for s in (1, 2, 3):
            cross(s).wait_recv()
            onward(s).start()
        cross(0).wait_recv()
        dos[1, 0] = crossed[0]

    def keep_row(y, carry):
        blocks(held, y, 2 * y + core, 2 + y)
        return carry

    lax.fori_loop(0, 2, keep_row, 0)

    def add_row(y, carry):
        swap(y).wait()

        def add(z, inner):
            held[y, z] = added(held[y, z], got[y, z])
            return inner

        return lax.fori_loop(0, 4, add, carry)

    lax.fori_loop(0, 2, add_row, 0)

    @pl.when(group == 1)
    def _():
        for s in (1, 2, 3):
            first(s).wait()
            second(s).wait()
        for s in range(4):
            cross(s).wait_send()

    @pl.when(group == 0)
    def _():
        for s in (1, 2, 3):
            onward(s).wait()


def feed_grads(hidden, gfeed, att, gbranch, act, gpre, gatt):
    tokens, width = hidden.shape
    _, half, lanes = gatt.shape
    rows = 3 * width // 16
    share = (2, 4, BLOCKS, rows, lanes)
    return pl.pallas_call(
        feed_grads_kernel,
        in_specs=in_vmem(4) + [pl.BlockSpec(memory_space=pl.ANY)] * 2 + in_vmem(1),
        out_specs=in_vmem(2),
        out_shape=[
            jax.ShapeDtypeStruct(share, BF16),
            jax.ShapeDtypeStruct((2, 4, half, lanes), BF16),
        ],
        scratch_shapes=[pltpu.VMEM((width, tokens), BF16)] * 3
        + [pltpu.VMEM((4, tokens, width), BF16)] * 2
        + [
            pltpu.VMEM(share, BF16),
            pltpu.VMEM(share, BF16),
            pltpu.VMEM((4, half, lanes), BF16),
            pltpu.SemaphoreType.DMA((15,)),
            pltpu.SemaphoreType.DMA((15,)),
            pltpu.SemaphoreType.DMA((2, 4)),
        ],
        compiler_params=pltpu.CompilerParams(
            collective_id=3, has_side_effects=True, vmem_limit_bytes=WHOLE_VMEM
        ),
        cost_estimate=pl.CostEstimate(
            flops=24_000_000_000, bytes_accessed=20_000_000, transcendentals=0
        ),
        name="feed_grads",
    )(hidden, gfeed, att, gbranch, act, gpre, gatt)


SMALL_ROWS = 40


def finish_kernel(
    packs, cosine, sine, normed_ref, vec_one, vec_two, middle_sums, up_sums, extra, feed_two,
    w_ref, x_ref, mgrad_ref, ada_ref,
    qkv_out, up_out, down_out, out_out, sums_out, ada_out, table_out, grad_ref,
    total, feed_total, rows_all, mixed, w_s, x_s, mgrad_s, ada_s, sums, small, sent, got, held, one_p, one_q, two, others,
    three, feed_others, feed_three, send_sems, recv_sems, own_sems,
):
    group = lax.axis_index("grp")
    place = lax.axis_index("seq")
    row, core, _, other_core = mlp_place()
    mlp = row * 2 + core
    sems = (send_sems, recv_sems)
    ahead = lambda s: (place + s) % 4
    heads = packs.shape[0]
    half = packs.shape[2]
    width = heads * HD
    lanes = 2 * HD
    parts = 3
    each = BLOCKS // parts

    loads = [
        pltpu.make_async_copy(source, target, own_sems.at[index])
        for index, (source, target) in enumerate(
            ((w_ref, w_s), (x_ref, x_s), (mgrad_ref, mgrad_s), (ada_ref, ada_s))
        )
    ]
    for load in loads:
        load.start()
    greet(
        [{"seq": ahead(s)} for s in (1, 2, 3)]
        + [{"mlp": (mlp + s) % 4} for s in (1, 2, 3)]
        + [{"grp": 1 - group}]
    )
    _, _, _, feed_over, feed_four, feed_five = sum_steps(
        None, None, None, feed_two, feed_others, feed_three, feed_total, sems, 0
    )
    sum_one, sum_two, sum_three, sum_over, sum_four, sum_five = sum_steps(
        held, one_p, one_q, two, others, three, total, sems, 9
    )
    feed_over()

    def swap(index):
        own = pl.ds(index * each, each)
        return push(
            sent.at[:, :, own], got.at[:, :, own], sems, 18 + index, {"mlp": other_core}
        )

    def unrotate(part):
        def one_pair(pair, carry):
            top, bottom = exchange(
                packs[2 * pair, part].astype(F32), packs[2 * pair + 1, part].astype(F32)
            )
            if part < 2:
                top = turn(top, cosine[0], -sine[0])
                bottom = turn(bottom, cosine[1], -sine[1])
            cols = pl.ds(pl.multiple_of(part * width + pair * lanes, lanes), lanes)
            mixed[:half, cols] = top.astype(BF16)
            mixed[half:, cols] = bottom.astype(BF16)
            return carry

        lax.fori_loop(0, heads // 2, one_pair, 0)

    def blocks(target, which, index):
        value = jnp.dot(
            normed_ref[which], mixed[:, index * width : (index + 1) * width],
            preferred_element_type=F32,
        ).astype(BF16)
        for lane in range(each):
            target[:, :, index * each + lane] = value[
                :, lane * lanes : (lane + 1) * lanes
            ].reshape(2, 4, width // 16, lanes)

    for index in (2, 0, 1):
        unrotate(index)
        blocks(sent, 1 - core, index)
        swap(index).start()
    for index in range(parts):
        blocks(held, core, index)
    for index in range(parts):
        swap(index).wait()
    for y in range(2):

        def add(z, carry, y=y):
            held[y, z] = added(held[y, z], got[y, z])
            return carry

        lax.fori_loop(0, 4, add, 0)
    sum_one()
    feed_four()
    for load in loads:
        load.wait()
    chunk = half // 2
    sums[...] = jnp.zeros_like(sums)

    def store(index):
        own = pl.ds(index * chunk, chunk)
        return pltpu.make_async_copy(mgrad_s.at[own], grad_ref.at[own], own_sems.at[4 + index])

    for index in range(4):
        own = slice(index * chunk, (index + 1) * chunk)
        gnormed = lax.dot_general(mixed[own, :], w_s[...], NT, preferred_element_type=F32)
        n, inverse = normalise(x_s[own, :].astype(F32))
        e = gnormed * ((1.0 + vec_one[1:2, :]) * vec_one[0:1, :])
        mgrad_s[own, :] = mgrad_s[own, :] + inverse * (
            e - jnp.mean(e, axis=-1, keepdims=True) - n * jnp.mean(e * n, axis=-1, keepdims=True)
        )
        store(index).start()
        sums[0:1, :] += jnp.sum(gnormed, axis=0, keepdims=True)
        sums[1:2, :] += jnp.sum(gnormed * n, axis=0, keepdims=True)
        if index == 2:
            sum_two()

    first_sum, second_sum = sums[1:2, :], middle_sums[1:2, :]
    mod = [
        sums[0:1, :], vec_one[0:1, :] * first_sum, middle_sums[4:5, :], middle_sums[0:1, :],
        vec_two[1:2, :] * second_sum, middle_sums[2:3, :],
    ]
    wholes = [
        (1.0 + vec_one[1:2, :]) * first_sum, (1.0 + vec_two[2:3, :]) * second_sum,
        middle_sums[3:4, :],
    ]
    weighted = None
    for index, value in enumerate(mod):
        part = jnp.sum(
            ada_s[:, index * width : (index + 1) * width].astype(F32) * value, axis=1,
            keepdims=True,
        )
        weighted = part if weighted is None else weighted + part
    table_row = jnp.broadcast_to(weighted, (lanes, lanes)).T[0:1] * extra[2:3, :]
    tiles = width // lanes
    for z in range(4):
        for line in range(9):
            tile = 9 * z + line
            value = mod[tile // tiles]
            start = (tile % tiles) * lanes
            small[z, line : line + 1, :] = value[:, start : start + lanes]
        for line in range(tiles):
            start = z * width + line * lanes
            small[z, 9 + line : 10 + line, :] = up_sums[0:1, start : start + lanes]
            for index, value in enumerate(wholes):
                at = 15 + index * tiles + line
                small[z, at : at + 1, :] = value[:, line * lanes : (line + 1) * lanes]
        small[z, 33:34, :] = table_row
        small[z, 34:36, :] = extra[0:2, :]
        small[z, 36:40, :] = jnp.zeros((4, lanes), F32)

    def hop_place(s):
        return push(
            small.at[ahead(s)], rows_all.at[group, mlp, place], sems, 20 + s, {"seq": ahead(s)}
        )

    def hop_place_in(s):
        return push(
            small.at[ahead(s)], rows_all.at[group, mlp, ahead(4 - s)], sems, 20 + s,
            {"seq": ahead(s)},
        )

    def hop_mlp(s, from_place):
        own = rows_all.at[group, from_place]
        return push(own, own, sems, 23 + s, {"mlp": (mlp + s) % 4})

    def hop_group(from_group):
        own = rows_all.at[from_group]
        return push(own, own, sems, 27, {"grp": 1 - group})

    for s in (1, 2, 3):
        hop_place(s).start()
    rows_all[group, mlp, place] = small[place]
    sum_three()
    sum_over()
    for s in (1, 2, 3):
        hop_place_in(s).wait()
    for s in (1, 2, 3):
        hop_mlp(s, mlp).start()
    sum_four()
    for s in (1, 2, 3):
        hop_mlp(s, mlp).wait_send()
        hop_mlp(s, (mlp + 4 - s) % 4).wait_recv()
    hop_group(group).start()
    feed_five()
    share_rows = feed_total.shape[1]
    part_rows = share_rows // 3
    for lane in range(tiles):
        at = slice(lane * lanes, (lane + 1) * lanes)
        one, two_, three_ = (feed_total[6 * index + lane].astype(F32) for index in range(3))
        up_out[:share_rows, at] = one
        up_out[share_rows:, at] = two_[:part_rows]
        down_out[: 2 * part_rows, at] = two_[part_rows:]
        down_out[2 * part_rows :, at] = three_[: 2 * part_rows]
        out_out[:, at] = three_[2 * part_rows :]
    sum_five()
    for block in range(BLOCKS):
        qkv_out[:, block * lanes : (block + 1) * lanes] = total[block].astype(F32)
    hop_group(group).wait_send()
    hop_group(1 - group).wait_recv()
    every = rows_all[...].reshape(32, SMALL_ROWS, lanes)
    sums_out[...] = jnp.sum(every, axis=0)
    conditions = every[:, 34].astype(BF16).astype(F32)
    for line in range(9):
        ada_out[:, line * lanes : (line + 1) * lanes] = lax.dot_general(
            conditions, every[:, line], TN, precision=highest, preferred_element_type=F32
        )
    table_rows = table_out.shape[0]
    first_row = (place * 4 + mlp) * table_rows
    owned = first_row + lax.broadcasted_iota(jnp.int32, (table_rows, 32), 0)
    steps = every[:, 35].T[:table_rows]
    chosen = jnp.where(owned.astype(F32) == steps, 1.0, 0.0)
    table_out[...] = jnp.dot(chosen, every[:, 33], precision=highest, preferred_element_type=F32)
    for index in range(4):
        store(index).wait()


def finish(
    packs, cosine, sine, normed, vec_one, vec_two, middle_sums, up_sums, extra, feed_two, weight,
    x, mgrad, ada_weight, table_rows,
):
    rows = normed.shape[1] // 8
    lanes = 2 * HD
    share = (2, 4, BLOCKS, rows, lanes)
    feed_rows = feed_two.shape[2]
    tokens, width = x.shape
    like = lambda value: pltpu.VMEM(value.shape, value.dtype)
    apart = pl.BlockSpec(memory_space=pl.ANY)
    return pl.pallas_call(
        finish_kernel,
        in_specs=in_vmem(10) + [apart] * 4,
        out_specs=in_vmem(7) + [apart],
        out_shape=[
            jax.ShapeDtypeStruct(shape, F32)
            for shape in (
                (width // 16, 3 * width), (width // 4, width), (width // 4, width),
                (width // 16, width), (SMALL_ROWS, lanes), (lanes, 9 * lanes),
                (table_rows, lanes), (tokens, width),
            )
        ],
        scratch_shapes=[
            pltpu.VMEM(share[2:], BF16), pltpu.VMEM((BLOCKS, feed_rows, lanes), BF16),
            pltpu.VMEM((2, 4, 4, SMALL_ROWS, lanes), F32),
            pltpu.VMEM((tokens, 3 * width), BF16), like(weight), like(x), like(mgrad),
            like(ada_weight), pltpu.VMEM((8, width), F32), pltpu.VMEM((4, SMALL_ROWS, lanes), F32),
        ]
        + [pltpu.VMEM(share, BF16)] * 3
        + sum_scratch(rows, EARLY + MIDDLE + LATE)
        + sum_scratch(feed_rows, LATE)
        + [pltpu.SemaphoreType.DMA((28,))] * 2
        + [pltpu.SemaphoreType.DMA((8,))],
        compiler_params=pltpu.CompilerParams(
            collective_id=4, has_side_effects=True, vmem_limit_bytes=WHOLE_VMEM
        ),
        cost_estimate=pl.CostEstimate(
            flops=60_000_000_000, bytes_accessed=20_000_000, transcendentals=0
        ),
        name="finish",
    )(
        packs, cosine, sine, normed, vec_one, vec_two, middle_sums, up_sums, extra, feed_two,
        weight, x, mgrad, ada_weight,
    )


def four_shards(
    tokens, step_index, time_table, ada_weight, ada_bias, first_gain, qkv_weight, out_weight,
    second_gain, up_weight, up_bias, down_weight, down_bias, cotangent,
):
    place = lax.axis_index("seq")
    group = lax.axis_index("grp")
    mlp_count = lax.axis_size("mlp")
    token_rows, width = tokens.shape[1:]
    half = token_rows // 2
    lanes = 2 * HD
    up_all = lax.all_gather(up_weight, "mlp", axis=0)
    down_all = lax.all_gather(down_weight, "mlp", axis=0)

    frequency = jnp.exp(jnp.arange(HD // 2, dtype=F32) * (-2.0 * math.log(10000.0) / HD))
    frequency = jnp.concatenate([frequency] * 4)[None, :]
    near_rows = 32
    offset = jnp.where(group == 1, place * token_rows, 0)
    far_rows = offset + near_rows * jnp.arange(token_rows // near_rows, dtype=jnp.int32)

    def circle(positions):
        angles = positions.astype(F32)[:, None] * frequency
        return jnp.stack([jnp.cos(angles), jnp.sin(angles)])

    x2 = tokens.reshape(2, half, width)
    parameters = jnp.concatenate([ada_bias, first_gain, second_gain, down_bias, up_bias])[None, :]
    (
        packs, att, pieces, results, logs, logs_own, cosine, sine, vec_one, vec_two, extra,
        bias_all, blocks,
    ) = forward_attention(
        x2, qkv_weight, circle(jnp.arange(near_rows, dtype=jnp.int32)), circle(far_rows),
        step_index, time_table, ada_weight, parameters,
    )

    (
        output, att_low, hidden, act, grad_feed, grad_pre, middle_grad, grad_branch, grad_att,
        middle_sums, up_sums,
    ) = middle_pass(
        x2, cotangent.reshape(2, half, width), att, vec_two, out_weight, up_all, down_all,
        bias_all,
    )
    flat = lambda value: value.reshape(token_rows, value.shape[2])
    feed_held, att_grads = feed_grads(
        *(flat(value) for value in (hidden, grad_feed, att_low, grad_branch, act, grad_pre)),
        grad_att,
    )
    grads, feed_two = backward_attention(
        packs, grad_att, att, pieces, results, logs, logs_own, att_grads, feed_held
    )
    ranks = 4 * mlp_count
    (
        qkv_total, up_total, down_total, out_total, row_sums, ada_rows, table_share, input_grad,
    ) = finish(
        grads, cosine, sine, blocks, vec_one, vec_two, middle_sums, up_sums, extra, feed_two,
        qkv_weight, flat(x2), flat(middle_grad), ada_weight, time_table.shape[0] // ranks,
    )
    mlp = lax.axis_index("mlp")
    rank = place * mlp_count + mlp

    def share(value, index, count):
        each = value.shape[-1] // count
        return lax.dynamic_slice_in_dim(value, index * each, each, value.ndim - 1)

    mod_sums, up_bias_sums, first_sums, second_sums, down_bias_sums = (
        row_sums[start:end].reshape(-1)
        for start, end in ((0, 9), (9, 15), (15, 21), (21, 27), (27, 33))
    )
    return (
        output.reshape(1, token_rows, width),
        input_grad.reshape(1, token_rows, width),
        table_share,
        share(ada_rows, mlp, mlp_count),
        share(mod_sums, mlp, mlp_count),
        share(first_sums, rank, ranks),
        qkv_total,
        out_total,
        share(second_sums, rank, ranks),
        up_total,
        share(up_bias_sums, mlp, mlp_count),
        down_total.T,
        share(down_bias_sums, rank, ranks),
    )


def solution(mesh):
    in_specs = (
        P(("grp", "mlp"), "seq", None),
        P(("grp", "mlp"), None),
        P(),
        P(),
        P(),
        P(),
        P(),
        P(),
        P(),
        P(None, "mlp"),
        P("mlp"),
        P("mlp", None),
        P(),
        P(("grp", "mlp"), "seq", None),
    )
    out_specs = (
        P(("grp", "mlp"), "seq", None),
        P(("grp", "mlp"), "seq", None),
        P(("seq", "mlp"), None),
        P(None, ("seq", "mlp")),
        P(("seq", "mlp")),
        P(("seq", "mlp")),
        P(("seq", "mlp"), None),
        P(("seq", "mlp"), None),
        P(("seq", "mlp")),
        P("seq", "mlp"),
        P(("seq", "mlp")),
        P("mlp", "seq"),
        P(("seq", "mlp")),
    )
    body = four_shards if mesh.shape["seq"] == 4 and mesh.shape["grp"] == 2 else shards
    return jax.shard_map(body, mesh=mesh, in_specs=in_specs, out_specs=out_specs, check_vma=False)
```

```python
import math

import jax
import jax.numpy as jnp
from jax import lax
from jax.experimental import pallas as pl
from jax.experimental.pallas import tpu as pltpu
from jax.sharding import PartitionSpec as P

HD = 64


highest = lax.Precision.HIGHEST


def shifted(value, axis, steps):
    count = lax.axis_size(axis)
    pairs = [(source, (source + steps) % count) for source in range(count)]
    return lax.ppermute(value, axis, pairs)


def layer_norm(values, norm_gain):
    centred = values - jnp.mean(values, axis=-1, keepdims=True)
    spread = jnp.mean(centred * centred, axis=-1, keepdims=True)
    return centred * lax.rsqrt(spread + 1e-05) * norm_gain


def modulate(values, norm_gain, shift_part, scale_part):
    return layer_norm(values, norm_gain) * (1.0 + scale_part) + shift_part


def gelu_tanh(values):
    return jax.nn.gelu(values, approximate=True)


def rotate_pairs(values, positions):
    half_dim = HD // 2
    frequency = jnp.exp(jnp.arange(half_dim, dtype=jnp.float32) * (-2.0 * math.log(10000.0) / HD))
    angles = positions.astype(jnp.float32)[:, None] * frequency[None, :]
    cosine = jnp.cos(angles)[:, None, :]
    sine_part = jnp.sin(angles)[:, None, :]
    leading = values[..., :half_dim]
    trailing = values[..., half_dim:]
    return jnp.concatenate(
        [leading * cosine - trailing * sine_part, trailing * cosine + leading * sine_part], axis=-1
    )


def shards(
    tokens,
    step_index,
    time_table,
    ada_weight,
    ada_bias,
    first_gain,
    qkv_weight,
    out_weight,
    second_gain,
    up_weight,
    up_bias,
    down_weight,
    down_bias,
    cotangent,
):
    seq_count = lax.axis_size("seq")
    seq_place = lax.axis_index("seq")
    group_index = lax.axis_index("grp")
    mlp_place = lax.axis_index("mlp")
    tok_rows = tokens.shape[1]
    model_width = tokens.shape[2]
    head_count = model_width // HD
    score_scale = 1.0 / math.sqrt(HD)
    line_len = tok_rows * seq_count
    seq_length = jnp.where(group_index == 0, line_len // 4, line_len).astype(jnp.int32)
    row_ids = jnp.arange(tok_rows, dtype=jnp.int32)
    own_pos = seq_place * tok_rows + row_ids
    positions = own_pos % seq_length
    quarter = seq_place // (seq_count // 4)
    step_value = jnp.sum(jnp.where(jnp.arange(4, dtype=jnp.int32) == quarter, step_index[0], 0))
    table_pick = jnp.arange(time_table.shape[0], dtype=jnp.int32) == step_value
    embedded = jnp.dot(
        table_pick.astype(jnp.bfloat16)[None, :], time_table, preferred_element_type=jnp.float32
    )[0]
    condition, silu_back = jax.vjp(jax.nn.silu, embedded)
    cond_low = condition.astype(jnp.bfloat16)
    modulation = jnp.dot(cond_low[None, :], ada_weight, preferred_element_type=jnp.float32)[
        0
    ] + ada_bias.astype(jnp.float32)
    shift_one, scale_one, gate_one, shift_two, scale_two, gate_two = jnp.split(modulation, 6)
    inputs = tokens[0].astype(jnp.float32)
    normed, first_back = jax.vjp(
        modulate, inputs, first_gain.astype(jnp.float32), shift_one, scale_one
    )
    normed_low = normed.astype(jnp.bfloat16)
    mixed_rows = jnp.dot(normed_low, qkv_weight, preferred_element_type=jnp.float32)

    def rotate_all(mixed_in):
        query_part = rotate_pairs(
            mixed_in[:, :model_width].reshape(tok_rows, head_count, HD), positions
        )
        key_part = rotate_pairs(
            mixed_in[:, model_width : 2 * model_width].reshape(tok_rows, head_count, HD), positions
        )
        return (
            query_part,
            key_part,
            mixed_in[:, 2 * model_width :].reshape(tok_rows, head_count, HD),
        )

    rotated, rotate_back = jax.vjp(rotate_all, mixed_rows)
    queries = rotated[0].astype(jnp.bfloat16)
    key_rows = rotated[1].astype(jnp.bfloat16)
    value_rows = rotated[2].astype(jnp.bfloat16)
    start_state = (
        jnp.full((head_count, tok_rows), -1e30, jnp.float32),
        jnp.zeros((head_count, tok_rows), jnp.float32),
        jnp.zeros((head_count, tok_rows, HD), jnp.float32),
    )
    key_piece = lax.all_gather(key_rows.reshape(tok_rows, model_width), "seq", axis=0, tiled=True)
    value_piece = lax.all_gather(
        value_rows.reshape(tok_rows, model_width), "seq", axis=0, tiled=True
    )
    piece_rows = key_piece.shape[0]
    sub_rows = math.gcd(piece_rows, 512)

    def one_block(block_index, block_state):
        run_max, run_total, run_acc = block_state
        offset = block_index * sub_rows
        key_block = lax.dynamic_slice_in_dim(key_piece, offset, sub_rows, 0).reshape(
            sub_rows, head_count, HD
        )
        value_block = lax.dynamic_slice_in_dim(value_piece, offset, sub_rows, 0).reshape(
            sub_rows, head_count, HD
        )
        key_pos = offset + jnp.arange(sub_rows, dtype=jnp.int32)
        same_seq = (own_pos // seq_length)[:, None] == (key_pos // seq_length)[None, :]
        scores = (
            jnp.einsum("qhd,khd->hqk", queries, key_block, preferred_element_type=jnp.float32)
            * score_scale
        )
        masked = jnp.where(same_seq[None], scores, -1e30)
        new_max = jnp.maximum(run_max, jnp.max(masked, axis=-1))
        shrink = jnp.exp(run_max - new_max)
        weights = jnp.where(same_seq[None], jnp.exp(masked - new_max[..., None]), 0.0)
        run_total = run_total * shrink + jnp.sum(weights, axis=-1)
        run_acc = run_acc * shrink[..., None] + jnp.einsum(
            "hqk,khd->hqd",
            weights.astype(jnp.bfloat16),
            value_block,
            preferred_element_type=jnp.float32,
        )
        return (new_max, run_total, run_acc)

    run_max, run_total, run_acc = lax.fori_loop(0, piece_rows // sub_rows, one_block, start_state)
    log_total = run_max + jnp.log(run_total)
    attended3 = jnp.transpose(run_acc / run_total[..., None], (1, 0, 2))
    attended_low = attended3.reshape(tok_rows, model_width).astype(jnp.bfloat16)
    branch = jnp.dot(attended_low, out_weight, preferred_element_type=jnp.float32)
    middle = inputs + gate_one * branch
    hidden, second_back = jax.vjp(
        modulate, middle, second_gain.astype(jnp.float32), shift_two, scale_two
    )
    hidden_low = hidden.astype(jnp.bfloat16)
    gathered = lax.all_gather(hidden_low, "mlp", axis=0, tiled=True)
    pre_act = jnp.dot(gathered, up_weight, preferred_element_type=jnp.float32) + up_bias.astype(
        jnp.float32
    )
    activated, gelu_back = jax.vjp(gelu_tanh, pre_act)
    act_low = activated.astype(jnp.bfloat16)
    feed_terms = jnp.dot(act_low, down_weight, preferred_element_type=jnp.float32)
    feed_out = lax.psum_scatter(
        feed_terms, "mlp", scatter_dimension=0, tiled=True
    ) + down_bias.astype(jnp.float32)
    output = (middle + gate_two * feed_out).astype(jnp.bfloat16)[None]
    grad_out = cotangent[0].astype(jnp.float32)
    gate_two_grad = jnp.sum(grad_out * feed_out, axis=0)
    grad_feed = (gate_two * grad_out).astype(jnp.bfloat16)
    down_bias_grad = jnp.sum(grad_feed, axis=0, dtype=jnp.float32)
    grad_rows = lax.all_gather(grad_feed, "mlp", axis=0, tiled=True)
    down_grad = jnp.einsum("tf,td->fd", act_low, grad_rows, preferred_element_type=jnp.float32)
    grad_act = jnp.einsum("td,fd->tf", grad_rows, down_weight, preferred_element_type=jnp.float32)
    grad_pre = gelu_back(grad_act)[0].astype(jnp.bfloat16)
    up_grad = jnp.einsum("td,tf->df", gathered, grad_pre, preferred_element_type=jnp.float32)
    local_units = up_weight.shape[1]
    bias_slot = lax.dynamic_update_slice_in_dim(
        jnp.zeros((local_units * lax.axis_size("mlp"),), jnp.float32),
        jnp.sum(grad_pre, axis=0, dtype=jnp.float32),
        mlp_place * local_units,
        0,
    )
    hidden_terms = jnp.einsum("tf,df->td", grad_pre, up_weight, preferred_element_type=jnp.float32)
    grad_hidden = lax.psum_scatter(hidden_terms, "mlp", scatter_dimension=0, tiled=True)
    middle_part, second_gain_grad, shift_two_grad, scale_two_grad = second_back(grad_hidden)
    middle_grad = grad_out + middle_part
    gate_one_grad = jnp.sum(middle_grad * branch, axis=0)
    grad_branch = (gate_one * middle_grad).astype(jnp.bfloat16)
    out_grad = jnp.einsum(
        "td,te->de", attended_low, grad_branch, preferred_element_type=jnp.float32
    )
    grad_attended = jnp.einsum(
        "te,de->td", grad_branch, out_weight, preferred_element_type=jnp.float32
    ).astype(jnp.bfloat16)
    grad_heads = grad_attended.reshape(tok_rows, head_count, HD)
    row_delta = jnp.transpose(jnp.sum(grad_heads.astype(jnp.float32) * attended3, axis=-1))

    def pair_grads(
        query_set, grad_set, total_set, delta_set, query_anchor, key_set, value_set, key_anchor
    ):
        query_pos = query_anchor * tok_rows + row_ids
        key_pos = key_anchor * tok_rows + row_ids
        same_seq = (query_pos // seq_length)[:, None] == (key_pos // seq_length)[None, :]
        scores = (
            jnp.einsum("qhd,khd->hqk", query_set, key_set, preferred_element_type=jnp.float32)
            * score_scale
        )
        prob_rows = jnp.where(same_seq[None], jnp.exp(scores - total_set[..., None]), 0.0)
        value_part = jnp.einsum(
            "hqk,qhd->khd",
            prob_rows.astype(jnp.bfloat16),
            grad_set,
            preferred_element_type=jnp.float32,
        )
        prob_grad = jnp.einsum(
            "qhd,khd->hqk", grad_set, value_set, preferred_element_type=jnp.float32
        )
        score_grad = (prob_rows * (prob_grad - delta_set[..., None])).astype(jnp.bfloat16)
        query_part = (
            jnp.einsum("hqk,khd->qhd", score_grad, key_set, preferred_element_type=jnp.float32)
            * score_scale
        )
        key_part = (
            jnp.einsum("hqk,qhd->khd", score_grad, query_set, preferred_element_type=jnp.float32)
            * score_scale
        )
        return (query_part, key_part, value_part)

    zero_heads = jnp.zeros((tok_rows, head_count, HD), jnp.float32)

    def key_turn(running):
        key_set, value_set, key_acc, value_acc, anchor, query_acc = running
        query_part, key_part, value_part = pair_grads(
            queries, grad_heads, log_total, row_delta, seq_place, key_set, value_set, anchor
        )
        moved_rows = shifted((key_set, value_set), "seq", 1)
        moved_grads = shifted((key_acc + key_part, value_acc + value_part), "seq", 1)
        return (
            moved_rows[0],
            moved_rows[1],
            moved_grads[0],
            moved_grads[1],
            (anchor - 1) % seq_count,
            query_acc + query_part,
        )

    def two_key_turns(turn_index, running):
        return key_turn(key_turn(running))

    finished = lax.fori_loop(
        0,
        seq_count // 2,
        two_key_turns,
        (key_rows, value_rows, zero_heads, zero_heads, seq_place, zero_heads),
    )
    query_grad, key_grad, value_grad = (finished[5], finished[2], finished[3])
    mixed_grad = rotate_back((query_grad, key_grad, value_grad))[0].astype(jnp.bfloat16)
    qkv_grad = jnp.einsum("td,te->de", normed_low, mixed_grad, preferred_element_type=jnp.float32)
    grad_normed = jnp.einsum(
        "te,de->td", mixed_grad, qkv_weight, preferred_element_type=jnp.float32
    )
    input_part, first_gain_grad, shift_one_grad, scale_one_grad = first_back(grad_normed)
    input_grad = (middle_grad + input_part)[None]
    mod_grad = jnp.concatenate(
        [
            shift_one_grad,
            scale_one_grad,
            gate_one_grad,
            shift_two_grad,
            scale_two_grad,
            gate_two_grad,
        ]
    )
    ada_grad = cond_low.astype(jnp.float32)[:, None] * mod_grad[None, :]
    cond_grad = jnp.dot(ada_weight.astype(jnp.float32), mod_grad, precision=highest)
    table_local = table_pick.astype(jnp.float32)[:, None] * silu_back(cond_grad)[0][None, :]
    layer_sums = (
        lax.psum_scatter(table_local, ("seq", "mlp"), scatter_dimension=0, tiled=True),
        lax.psum_scatter(ada_grad, ("seq", "mlp"), scatter_dimension=1, tiled=True),
        lax.psum_scatter(mod_grad, ("seq", "mlp"), scatter_dimension=0, tiled=True),
        lax.psum_scatter(first_gain_grad, ("seq", "mlp"), scatter_dimension=0, tiled=True),
        lax.psum_scatter(qkv_grad, ("seq", "mlp"), scatter_dimension=0, tiled=True),
        lax.psum_scatter(out_grad, ("seq", "mlp"), scatter_dimension=0, tiled=True),
        lax.psum_scatter(second_gain_grad, ("seq", "mlp"), scatter_dimension=0, tiled=True),
        lax.psum_scatter(bias_slot, ("seq", "mlp"), scatter_dimension=0, tiled=True),
        lax.psum_scatter(down_bias_grad, ("seq", "mlp"), scatter_dimension=0, tiled=True),
    )
    feed_summed = (
        lax.psum_scatter(up_grad, "seq", scatter_dimension=0, tiled=True),
        lax.psum_scatter(down_grad, "seq", scatter_dimension=1, tiled=True),
    )
    totals = lax.psum(
        (
            layer_sums[0],
            layer_sums[1],
            layer_sums[2],
            layer_sums[3],
            layer_sums[4],
            layer_sums[5],
            layer_sums[6],
            layer_sums[7],
            layer_sums[8],
            feed_summed[0],
            feed_summed[1],
        ),
        "grp",
    )
    return (
        output,
        input_grad,
        totals[0],
        totals[1],
        totals[2],
        totals[3],
        totals[4],
        totals[5],
        totals[6],
        totals[9],
        totals[7],
        totals[10],
        totals[8],
    )


LOG_SCALE = math.log2(math.e) / math.sqrt(HD)
NT = (((1,), (1,)), ((), ()))
TN = (((0,), (0,)), ((), ()))
F32 = jnp.float32
BF16 = jnp.bfloat16
WHOLE_VMEM = 60 * 1024 * 1024


def params(*semantics):
    return pltpu.CompilerParams(vmem_limit_bytes=WHOLE_VMEM, dimension_semantics=semantics)


def low_lanes(value):
    return lax.broadcasted_iota(jnp.int32, value.shape, 1) < HD


def swap_heads(value):
    return pltpu.roll(value, HD, 1)


def exchange(top, bottom):
    keep = low_lanes(top)
    return (
        jnp.where(keep, top, swap_heads(bottom)),
        jnp.where(keep, swap_heads(top), bottom),
    )


def fold(value):
    half = value.shape[0] // 2
    top = value[:half]
    return jnp.where(low_lanes(top), top, swap_heads(value[half:]))


def unfold_into(target, base, packed, fill):
    half = packed.shape[0]
    value = packed.astype(F32)
    keep = low_lanes(value)
    target[base : base + half, :] = jnp.where(keep, value, fill).astype(BF16)
    target[base + half : base + 2 * half, :] = jnp.where(keep, swap_heads(value), fill).astype(BF16)


def turn(value, cosine, sine):
    lane = lax.broadcasted_iota(jnp.int32, value.shape, 1) % HD
    quarter = HD // 2
    other = jnp.where(
        lane < quarter, pltpu.roll(value, 2 * HD - quarter, 1), pltpu.roll(value, quarter, 1)
    )
    return value * cosine + other * sine


def normalise(values):
    centred = values - jnp.mean(values, axis=-1, keepdims=True)
    spread = jnp.mean(centred * centred, axis=-1, keepdims=True)
    inverse = lax.rsqrt(spread + 1e-05)
    return centred * inverse, inverse


def attend_rows(q, k_ref, v_ref, keys, out_put, log_put, block=512):
    top = None
    for start in range(0, keys, block):
        s = lax.dot_general(q, k_ref[start : start + block, :], NT, preferred_element_type=F32)
        s = s * LOG_SCALE
        peak = jnp.max(s, axis=1, keepdims=True)
        new_top = peak if top is None else jnp.maximum(top, peak)
        p = jnp.exp2(s - new_top).astype(BF16)
        part = jnp.dot(p, v_ref[start : start + block, :], preferred_element_type=F32)
        acc = part if top is None else acc * jnp.exp2(top - new_top) + part
        top = new_top
    out_put(fold(acc / swap_heads(acc)).astype(BF16))
    log_put((top + jnp.log2(acc)).T[HD : HD + 8])


def load_values(source, base, k_s, v_s):
    unfold_into(k_s, base, source[1], 0.0)
    unfold_into(v_s, base, source[2], 1.0)


def packed_queries(packed):
    value = packed.astype(F32)
    return jnp.concatenate([value, swap_heads(value)]).astype(BF16)


def push(src, dst, sems, index, where):
    return pltpu.make_async_remote_copy(
        src_ref=src, dst_ref=dst, send_sem=sems[0].at[index], recv_sem=sems[1].at[index],
        device_id=where, device_id_type=pl.DeviceIdType.MESH,
    )


def reach(src, dst, sems, index, group, place):
    return push(src, dst, sems, index, {"grp": group, "seq": place})


def neighbours(group, place, others):
    found = [
        {"grp": (group + other) % 2, "seq": (place + steps) % 4}
        for other in range(2)
        for steps in range(4)
        if other or steps
    ]
    return found + [{"mlp": other} for other in others]


def greet(devices):
    barrier = pltpu.get_barrier_semaphore()
    for where in devices:
        pl.semaphore_signal(barrier, 1, device_id=where, device_id_type=pl.DeviceIdType.MESH)
    pl.semaphore_wait(barrier, len(devices))


def mlp_place():
    mlp = lax.axis_index("mlp")
    row, core = mlp // 2, mlp % 2
    return row, core, (1 - row) * 2 + core, row * 2 + 1 - core


BLOCKS = 18


def added(left, right):
    return (left.astype(F32) + right.astype(F32)).astype(BF16)


def sum_steps(held, one_p, one_q, two, others, three, out, sems, base, near=None):
    group = lax.axis_index("grp")
    place = lax.axis_index("seq")
    row, _, other_row, _ = mlp_place()
    by_row = {"mlp": other_row}
    by_group = {"grp": 1 - group}
    ahead = lambda s: (place + s) % 4

    def copies(stage):
        if stage == 1:
            return [
                push(held.at[1 - row, :, pl.ds(0, 10)], one_p, sems, base, by_row),
                push(
                    held.at[:, :, pl.ds(10 + 4 * (1 - group), 4)], one_q, sems, base + 1, by_group
                ),
            ]
        if stage == 2:
            return [
                push(
                    one_p.at[:, pl.ds(5 * (1 - group), 5)], two.at[:, pl.ds(0, 5)], sems,
                    base + 2, by_group,
                ),
                push(one_q.at[1 - row], two.at[:, pl.ds(5, 4)], sems, base + 3, by_row),
            ]
        if stage == 3:
            return [
                push(two.at[ahead(s)], others.at[s - 1], sems, base + 3 + s, {"seq": ahead(s)})
                for s in (1, 2, 3)
            ]
        return [
            push(three.at[pl.ds(0, 5)], out.at[pl.ds(5 * group, 5)], sems, base + 7, by_group),
            push(
                three.at[pl.ds(5, 4)], out.at[pl.ds(10 + 4 * group, 4)], sems, base + 8, by_group
            ),
        ]

    def start(stage):
        for copy in copies(stage):
            copy.start()

    def arrive(stage):
        for copy in copies(stage):
            copy.wait()

    def step_one():
        start(1)

    def step_two():
        arrive(1)

        def add(z, carry):
            own = held[row, z, 0:10] if near is None else near[0][z]
            one_p[z] = added(own, one_p[z])
            for y in range(2):
                own = held[y, z, pl.ds(10 + 4 * group, 4)] if near is None else near[1][y, z]
                one_q[y, z] = added(own, one_q[y, z])
            return carry

        lax.fori_loop(0, 4, add, 0)
        start(2)

    def step_three():
        arrive(2)

        def add(z, carry):
            two[z, 0:5] = added(one_p[z, pl.ds(5 * group, 5)], two[z, 0:5])
            two[z, 5:9] = added(one_q[row, z], two[z, 5:9])
            return carry

        lax.fori_loop(0, 4, add, 0)

    def step_over():
        start(3)

    def step_four():
        arrive(3)

        def add(block, carry):
            total = two[place, block].astype(F32)
            for s in range(3):
                total = total + others[s, block].astype(F32)
            three[block] = total.astype(BF16)
            return carry

        lax.fori_loop(0, 9, add, 0)
        start(4)
        out[pl.ds(5 * group, 5)] = three[0:5]
        out[pl.ds(10 + 4 * group, 4)] = three[5:9]

    def step_five():
        arrive(4)

    return step_one, step_two, step_three, step_over, step_four, step_five


def sum_scratch(rows, shapes):
    return [pltpu.VMEM(shape + (rows, 2 * HD), BF16) for shape in shapes]


EARLY = [(4, 10), (2, 4, 4)]
MIDDLE = [(4, 9)]
LATE = [(3, 9), (9,)]


def forward_kernel(
    x_ref, w_ref, near, far, step_ref, table, ada_ref, params_ref,
    packs_out, att, pieces, results, logs, logs_own, cosine, sine, vec_one, vec_two, extra,
    bias_all, blocks_out, packs, blocks, crossed, normed_s, k_s, v_s, send_sems, recv_sems,
    own_sems,
):
    group = lax.axis_index("grp")
    place = lax.axis_index("seq")
    sems = (send_sems, recv_sems)
    heads = packs.shape[0]
    rows = 2 * packs.shape[2]
    ahead = lambda s: (place + s) % 4
    behind = lambda s: (place + 4 - s) % 4

    def first(s):
        return reach(packs.at[2 * ahead(s)], pieces.at[0, s], sems, s - 1, 1, ahead(s))

    def second_values(s):
        source = packs.at[2 * ahead(s) + 1, pl.ds(1, 2)]
        return reach(source, pieces.at[1, s, pl.ds(1, 2)], sems, 2 + s, 1, ahead(s))

    def second_queries(s):
        source = packs.at[2 * ahead(s) + 1, 0]
        return reach(source, pieces.at[1, s, 0], sems, 5 + s, 1, ahead(s))

    def cross(s):
        return reach(packs.at[8 + ahead(s)], crossed.at[s], sems, 9 + s, 0, place)

    def onward(s):
        return reach(crossed.at[s], pieces.at[1, s], sems, 12 + s, 0, ahead(s))

    def home(kind, s, head):
        start = (16, 20, 24)[kind]
        return reach(
            results.at[min(kind, 1), s], att.at[head], sems, start + s, 1, behind(s)
        )

    row, core, _, _ = mlp_place()
    mlp = row * 2 + core
    greet(neighbours(group, place, [(mlp + s) % 4 for s in (1, 2, 3)]))
    width = w_ref.shape[0]
    vectors = params_ref[...].astype(F32)
    vector = lambda index: vectors[:, index * width : (index + 1) * width]
    first_gain, second_gain, down_bias = vector(6), vector(7), vector(8)
    up_bias = vectors[:, 9 * width :]
    bias_all[mlp] = jnp.broadcast_to(up_bias, bias_all.shape[1:])

    def share_bias(s, owner):
        own = bias_all.at[owner]
        return push(own, own, sems, 27 + s, {"mlp": (mlp + s) % 4})

    for s in (1, 2, 3):
        share_bias(s, mlp).start()

    half = packs.shape[2]
    lanes = 2 * HD
    quarters = step_ref[...].astype(F32)
    own_quarter = lax.broadcasted_iota(jnp.int32, quarters.shape, 1) == place
    step = jnp.sum(jnp.where(own_quarter, quarters, 0.0), axis=1, keepdims=True)
    entries = lax.broadcasted_iota(jnp.int32, (16, table.shape[0]), 1).astype(F32)
    chosen = jnp.where(entries == step, 1.0, 0.0).astype(BF16)
    embedded = jnp.dot(chosen, table[...], preferred_element_type=F32)
    gate = 1.0 / (1.0 + jnp.exp(-embedded))
    condition = embedded * gate
    modulation = jnp.dot(condition.astype(BF16), ada_ref[...], preferred_element_type=F32)
    modulation = modulation[0:1] + vectors[:, : 6 * width]
    part = lambda index: modulation[:, index * width : (index + 1) * width]
    for target, values in (
        (vec_one, (first_gain, part(1), part(0))),
        (
            vec_two,
            (part(2), second_gain, part(4), part(3), part(5), down_bias),
        ),
        (
            extra,
            (
                condition[0:1], jnp.broadcast_to(step, (1, condition.shape[1])),
                (gate * (1.0 + embedded * (1.0 - gate)))[0:1],
            ),
        ),
    ):
        target[...] = jnp.zeros_like(target)
        for index, value in enumerate(values):
            target[index : index + 1, :] = value

    near_rows = near.shape[1]
    first_half = lax.broadcasted_iota(jnp.int32, near.shape[1:], 1) % HD < HD // 2
    for index in range(far.shape[1]):
        far_cos, far_sin = far[0, index : index + 1, :], far[1, index : index + 1, :]
        start = index * near_rows
        at = slice(start % half, start % half + near_rows)
        value = far_sin * near[0] + far_cos * near[1]
        cosine[start // half, at, :] = far_cos * near[0] - far_sin * near[1]
        sine[start // half, at, :] = jnp.where(first_half, -value, value)

    tile = half // 2

    def normal(index, carry):
        at = pl.ds(pl.multiple_of(index * tile, tile), tile)
        for side in range(2):
            n, _ = normalise(x_ref[side, at, :].astype(F32))
            value = n * vec_one[0:1, :] * (1.0 + vec_one[1:2, :]) + vec_one[2:3, :]
            normed_s[side, at, :] = value.astype(BF16)
        return carry

    lax.fori_loop(0, 2, normal, 0)

    def project(low_pair, count):
        def tokens(index, carry):
            at = pl.ds(pl.multiple_of(index * tile, tile), tile)
            normed = normed_s[:, at, :].reshape(2 * tile, width)
            turn_cos = cosine[:, at, :].reshape(2 * tile, lanes)
            turn_sin = sine[:, at, :].reshape(2 * tile, lanes)
            for kind in range(3):
                start = kind * width + low_pair * lanes
                mixed = jnp.dot(
                    normed, w_ref[:, start : start + count * lanes], preferred_element_type=F32
                )
                for pair in range(count):
                    value = mixed[:, pair * lanes : (pair + 1) * lanes]
                    if kind < 2:
                        value = turn(value, turn_cos, turn_sin)
                    even, odd = exchange(value[:tile], value[tile:])
                    head = 2 * (low_pair + pair)
                    packs[head, kind, at, :] = even.astype(BF16)
                    packs[head + 1, kind, at, :] = odd.astype(BF16)
            return carry

        lax.fori_loop(0, 2, tokens, 0)

    def full(kind, head, before, after):
        sel = min(kind, 1)
        for s in range(4):
            load_values(pieces.at[sel, s], s * rows, k_s, v_s)

        def step(s, carry):
            before(s)

            def put_out(value):
                results[sel, s] = value

            def put_log(value):
                logs[sel, s] = value

            q = packed_queries(pieces[sel, s, 0])
            attend_rows(q, k_s, v_s, 4 * rows, put_out, put_log)
            after(s)
            return carry

        lax.fori_loop(0, 4, step, 0)

    project(0, 4)

    @pl.when(group == 1)
    def _():
        for s in (1, 2, 3):
            first(s).start()

    project(4, 2)

    @pl.when(group == 1)
    def _():
        for s in (1, 2, 3, 0):
            cross(s).start()

    flipped = normed_s[...].reshape(2 * half, width).T
    part_rows = width // 16
    for which in range(2):
        for y in range(2):
            for z in range(4):
                start = ((z * 2 + y) * 2 + which) * part_rows
                at = (y * 4 + z) * part_rows
                blocks[which, at : at + part_rows, :] = flipped[start : start + part_rows]
    stores = (
        pltpu.make_async_copy(packs, packs_out, own_sems.at[0]),
        pltpu.make_async_copy(blocks, blocks_out, own_sems.at[1]),
    )
    for store in stores:
        store.start()

    @pl.when(group == 1)
    def _():
        pieces[0, 0] = packs[2 * place]
        pieces[1, 0] = packs[2 * place + 1]
        for s in (1, 3, 2):
            first(s).wait_send()
            second_values(s).start()
        for s in (1, 2, 3):
            second_queries(s).start()
        for s in (1, 2, 3):
            first(s).wait_recv()

        def before(s):
            pass

        def after(s):
            @pl.when(s == 0)
            def _():
                att[2 * place] = results[0, 0]

        full(0, 2 * place, before, after)
        for s in (1, 2, 3):
            second_values(s).wait_recv()

    @pl.when(group == 0)
    def _():
        def local(head, carry):
            load_values(packs.at[head], 0, k_s, v_s)

            def put_out(value):
                att[head] = value

            def put_log(value):
                logs_own[head] = value

            attend_rows(packed_queries(packs[head, 0]), k_s, v_s, rows, put_out, put_log)
            for s in (1, 2, 3):

                @pl.when(head == 4 * s - 1)
                def _(s=s):
                    cross(s).wait_recv()
                    onward(s).start()

            return carry

        lax.fori_loop(0, heads, local, 0)
        cross(0).wait_recv()
        pieces[1, 0] = crossed[0]
        for s in (1, 2, 3):
            onward(s).wait_recv()

    def before(s):
        @pl.when((group == 1) & (s > 0))
        def _():
            second_queries(s).wait_recv()

    def after(s):
        @pl.when((group == 1) & (s == 0))
        def _():
            att[2 * place + 1] = results[1, 0]
            for other in (1, 2, 3):
                home(0, other, 2 * place).start()

        @pl.when((group == 1) & (s > 0))
        def _():
            home(1, s, 2 * place + 1).start()

        @pl.when(group == 0)
        def _():
            home(2, s, 8 + place).start()

    full(1, 0, before, after)

    @pl.when(group == 1)
    def _():
        for s in (1, 2, 3):
            second_values(s).wait_send()
            second_queries(s).wait_send()
            for kind in (0, 1):
                home(kind, s, 2 * place + kind).wait_send()
        for s in range(4):
            cross(s).wait_send()
        for s in (1, 2, 3):
            for kind in (0, 1):
                home(kind, s, 2 * ahead(s) + kind).wait_recv()
        for s in range(4):
            home(2, s, 8 + ahead(s)).wait_recv()

    @pl.when(group == 0)
    def _():
        for s in (1, 2, 3):
            onward(s).wait_send()
        for s in range(4):
            home(2, s, 8 + place).wait_send()

    for s in (1, 2, 3):
        share_bias(s, mlp).wait_send()
        share_bias(s, (mlp + 4 - s) % 4).wait_recv()
    for store in stores:
        store.wait()


def in_vmem(count):
    return [pl.BlockSpec(memory_space=pltpu.VMEM)] * count


def forward_attention(x2, weight, *rest):
    _, half, width = x2.shape
    heads, lanes = width // HD, 2 * HD
    shapes = [
        ((heads, 3, half, lanes), BF16),
        ((heads, half, lanes), BF16),
        ((2, 4, 3, half, lanes), BF16),
        ((2, 4, half, lanes), BF16),
        ((2, 4, 8, 2 * half), F32),
        ((heads, 8, 2 * half), F32),
        ((2, half, lanes), F32),
        ((2, half, lanes), F32),
        ((8, width), F32),
        ((8, width), F32),
        ((8, rest[3].shape[1]), F32),
        ((4, 8, rest[-1].shape[1] - 9 * width), F32),
        ((2, width // 2, 2 * half), BF16),
    ]
    return pl.pallas_call(
        forward_kernel,
        in_specs=in_vmem(2 + len(rest)),
        out_specs=[pl.BlockSpec(memory_space=pl.ANY)]
        + in_vmem(len(shapes) - 2)
        + [pl.BlockSpec(memory_space=pl.ANY)],
        out_shape=[jax.ShapeDtypeStruct(shape, kind) for shape, kind in shapes],
        scratch_shapes=[
            pltpu.VMEM(shapes[0][0], BF16),
            pltpu.VMEM(shapes[-1][0], BF16),
            pltpu.VMEM((4, 3, half, lanes), BF16),
            pltpu.VMEM((2, half, width), BF16),
            pltpu.VMEM((8 * half, lanes), BF16),
            pltpu.VMEM((8 * half, lanes), BF16),
            pltpu.SemaphoreType.DMA((31,)),
            pltpu.SemaphoreType.DMA((31,)),
            pltpu.SemaphoreType.DMA((2,)),
        ],
        compiler_params=pltpu.CompilerParams(
            collective_id=1, has_side_effects=True, vmem_limit_bytes=WHOLE_VMEM
        ),
        cost_estimate=pl.CostEstimate(
            flops=100_000_000_000, bytes_accessed=8_000_000, transcendentals=0
        ),
        name="forward_attention",
    )(x2, weight, *rest)


def tile_grads(q, do, k, v, log_row, delta_row):
    s = lax.dot_general(k, q, NT, preferred_element_type=F32)
    p = jnp.exp2(s * LOG_SCALE - log_row)
    dp = lax.dot_general(v, do, NT, preferred_element_type=F32)
    ds = (p * (dp - delta_row)).astype(BF16)
    dv = jnp.dot(p.astype(BF16), do, preferred_element_type=F32)
    dk = jnp.dot(ds, q, preferred_element_type=F32)
    dq = lax.dot_general(k, ds, TN, preferred_element_type=F32)
    return dq, dk, dv


def load_backward(source, do, o, base, q_s, k_s, v_s, do_s, delta_s):
    half = do.shape[0]
    unfold_into(q_s, base, source[0], 0.0)
    unfold_into(k_s, base, source[1], 0.0)
    unfold_into(v_s, base, source[2], 0.0)
    unfold_into(do_s, base, do, 0.0)
    product = (do.astype(F32) * o.astype(F32)).T
    first = jnp.sum(product[:HD], axis=0, keepdims=True)
    second = jnp.sum(product[HD:], axis=0, keepdims=True)
    delta_s[:, base : base + half] = jnp.broadcast_to(first, (8, half))
    delta_s[:, base + half : base + 2 * half] = jnp.broadcast_to(second, (8, half))


def backward_kernel(
    packs_ref, gatt_ref, att_ref, logs_ref, held_ref, pieces, results, logs, dos, back, two,
    packs, gatt, att, logs_own, near_p, near_q, staged, q_s, k_s, v_s, do_s, delta_s, dq_s, one_p, one_q,
    send_sems, recv_sems, own_sems,
):
    group = lax.axis_index("grp")
    place = lax.axis_index("seq")
    sems = (send_sems, recv_sems)
    heads = packs_ref.shape[0]
    rows = 2 * packs.shape[2]
    scale = 1.0 / math.sqrt(HD)
    ahead = lambda s: (place + s) % 4
    behind = lambda s: (place + 4 - s) % 4
    stores = (q_s, k_s, v_s, do_s, delta_s)

    def home_values(kind, s, head):
        source = staged.at[min(kind, 1), s, pl.ds(1, 2)]
        return reach(
            source, back.at[head, pl.ds(1, 2)], sems, (0, 4, 8)[kind] + s, 1, behind(s)
        )

    def home_queries(kind, s, head):
        source = staged.at[min(kind, 1), s, 0]
        return reach(source, back.at[head, 0], sems, (12, 16, 20)[kind] + s, 1, behind(s))

    greet(neighbours(group, place, [mlp_place()[2]]))
    sum_one, sum_two, sum_three, _, _, _ = sum_steps(
        held_ref, one_p, one_q, two, None, None, None, sems, 24, (near_p, near_q)
    )
    sum_one()
    held_loads = (
        pltpu.make_async_copy(
            held_ref.at[mlp_place()[0], :, pl.ds(0, 10)], near_p, own_sems.at[0]
        ),
        pltpu.make_async_copy(
            held_ref.at[:, :, pl.ds(10 + 4 * group, 4)], near_q, own_sems.at[1]
        ),
    )
    for load in held_loads:
        load.start()

    def sum_over_rows():
        for load in held_loads:
            load.wait()
        sum_two()

    def local_loads(head):
        slot = head % 2
        return [
            pltpu.make_async_copy(source.at[head], target.at[slot], own_sems.at[2 + 4 * slot + n])
            for n, (source, target) in enumerate(
                ((packs_ref, packs), (gatt_ref, gatt), (att_ref, att), (logs_ref, logs_own))
            )
        ]

    def full(sel, put_values, put_queries):
        for s in range(4):
            load_backward(
                pieces.at[sel, s], dos[sel, s], results[sel, s], s * rows, *stores
            )

        def step(turn_index, last):
            s = 0 if last else (turn_index + 1) % 4
            block = pl.ds(0 if last else pl.multiple_of(s * rows, rows), rows)
            k = k_s[block, :]
            v = v_s[block, :]
            dk = dv = None
            for index in (1, 2, 3, 0):
                chunk = slice(index * rows, (index + 1) * rows)
                dq, dk_part, dv_part = tile_grads(
                    q_s[chunk, :], do_s[chunk, :], k, v, logs[sel, index, 0:1, :],
                    delta_s[0:1, chunk],
                )
                dk = dk_part if dk is None else dk + dk_part
                dv = dv_part if dv is None else dv + dv_part
                if last:
                    dq = dq_s[:, chunk] + dq
                    staged[sel, index, 0] = fold(dq.T * scale).astype(BF16)
                    put_queries(index)
                else:
                    dq_s[:, chunk] = jnp.where(turn_index == 0, dq, dq_s[:, chunk] + dq)
            staged[sel, s, 1] = fold(dk * scale).astype(BF16)
            staged[sel, s, 2] = fold(dv).astype(BF16)
            put_values(s)

        def one_turn(turn_index, carry):
            step(turn_index, False)
            return carry

        if sel:
            lax.fori_loop(0, 3, one_turn, 0)
            step(3, True)
        else:
            lax.fori_loop(0, 4, one_turn, 0)
            for index in (1, 2, 3, 0):
                chunk = slice(index * rows, (index + 1) * rows)
                staged[sel, index, 0] = fold(dq_s[:, chunk].T * scale).astype(BF16)
                put_queries(index)

    @pl.when(group == 1)
    def _():
        head = 2 * place

        def put_values(s):
            @pl.when(s == 0)
            def _():
                back[head, 1] = staged[0, 0, 1]
                back[head, 2] = staged[0, 0, 2]

            @pl.when(s > 0)
            def _():
                home_values(0, s, head).start()

            @pl.when(s == 0)
            def _():
                sum_over_rows()

        def put_queries(s):
            if s == 0:
                back[head, 0] = staged[0, 0, 0]
            else:
                home_queries(0, s, head).start()

        full(0, put_values, put_queries)

    def put_values(s):
        head = 2 * place + 1

        @pl.when((group == 1) & (s == 0))
        def _():
            back[head, 1] = staged[1, 0, 1]
            back[head, 2] = staged[1, 0, 2]

        @pl.when((group == 1) & (s > 0))
        def _():
            home_values(1, s, head).start()

        @pl.when(group == 0)
        def _():
            home_values(2, s, 8 + place).start()

        @pl.when((group == 0) & (s == 3))
        def _():
            sum_over_rows()

    def put_queries(s):
        if s:
            head = group * (2 * place + 1) + (1 - group) * (8 + place)
            reach(
                staged.at[1, s, 0], back.at[head, 0], sems, 20 - 4 * group + s, 1, behind(s)
            ).start()
            return

        @pl.when(group == 1)
        def _():
            back[2 * place + 1, 0] = staged[1, 0, 0]

        @pl.when(group == 0)
        def _():
            home_queries(2, 0, 8 + place).start()

    full(1, put_values, put_queries)

    @pl.when(group == 0)
    def _():
        for load in local_loads(0):
            load.start()

        def local(head, carry):
            @pl.when(head + 1 < heads)
            def _():
                for load in local_loads(head + 1):
                    load.start()

            for load in local_loads(head):
                load.wait()
            slot = head % 2
            load_backward(packs.at[slot], gatt[slot], att[slot], 0, *stores)
            own = slice(0, rows)
            dq, dk, dv = tile_grads(
                q_s[own, :], do_s[own, :], k_s[own, :], v_s[own, :],
                logs_own[slot, 0:1, :], delta_s[0:1, own],
            )
            back[head, 0] = fold(dq.T * scale).astype(BF16)
            back[head, 1] = fold(dk * scale).astype(BF16)
            back[head, 2] = fold(dv).astype(BF16)
            return carry

        lax.fori_loop(0, heads, local, 0)

    sum_three()

    @pl.when(group == 0)
    def _():
        for s in range(4):
            home_values(2, s, 8 + place).wait_send()
            home_queries(2, s, 8 + place).wait_send()

    @pl.when(group == 1)
    def _():
        for s in (1, 2, 3):
            for kind in (0, 1):
                home_values(kind, s, 2 * place + kind).wait_send()
                home_queries(kind, s, 2 * place + kind).wait_send()
        for s in (1, 2, 3):
            for kind in (0, 1):
                home_values(kind, s, 2 * ahead(s) + kind).wait_recv()
                home_queries(kind, s, 2 * ahead(s) + kind).wait_recv()
        for s in range(4):
            home_values(2, s, 8 + ahead(s)).wait_recv()
            home_queries(2, s, 8 + ahead(s)).wait_recv()


def backward_attention(packs, gatt, att, pieces, results, logs, logs_own, dos, held):
    heads, _, half, lanes = packs.shape
    share = held.shape[2:]
    return pl.pallas_call(
        backward_kernel,
        in_specs=[pl.BlockSpec(memory_space=pl.ANY)] * 5 + in_vmem(4),
        out_specs=in_vmem(2),
        out_shape=[
            jax.ShapeDtypeStruct((heads, 3, half, lanes), BF16),
            jax.ShapeDtypeStruct((4, 9) + share[1:], BF16),
        ],
        scratch_shapes=[
            pltpu.VMEM((2,) + value.shape[1:], value.dtype)
            for value in (packs, gatt, att, logs_own)
        ]
        + sum_scratch(share[1], EARLY)
        + [pltpu.VMEM((2, 4, 3, half, lanes), BF16)]
        + [pltpu.VMEM((8 * half, lanes), BF16)] * 4
        + [pltpu.VMEM((8, 8 * half), F32), pltpu.VMEM((lanes, 8 * half), F32)]
        + sum_scratch(share[1], EARLY)
        + [pltpu.SemaphoreType.DMA((28,))] * 2
        + [pltpu.SemaphoreType.DMA((10,))],
        compiler_params=pltpu.CompilerParams(
            collective_id=2, has_side_effects=True, vmem_limit_bytes=WHOLE_VMEM
        ),
        cost_estimate=pl.CostEstimate(
            flops=120_000_000_000, bytes_accessed=8_000_000, transcendentals=0
        ),
        name="backward_attention",
    )(packs, gatt, att, logs_own, held, pieces, results, logs, dos)


def whole(shape):
    zeros = (0,) * len(shape)
    return pl.BlockSpec(shape, lambda *_: zeros)


def middle_kernel(
    x_ref, cot_ref, att_ref, vec_ref, ow_ref, up_ref, down_ref, bias_ref,
    out_ref, attlow_ref, hidden_ref, act_ref, gfeed_ref, gpre_ref, mgrad_ref, gbranch_ref,
    gatt_ref, sums_ref, upsum_ref, att_s, slope_s,
):
    step = pl.program_id(0)
    rows, width = x_ref.shape[1:]
    both = 2 * rows
    pairs = width // (2 * HD)
    gate_one, gain, scale, shift = (vec_ref[i : i + 1, :] for i in range(4))
    gate_two, down_bias = vec_ref[4:5, :], vec_ref[5:6, :]
    for pair in range(pairs):
        lanes = slice(pair * 2 * HD, (pair + 1) * 2 * HD)
        top, bottom = exchange(
            att_ref[2 * pair].astype(F32), att_ref[2 * pair + 1].astype(F32)
        )
        att_s[:rows, lanes] = top.astype(BF16)
        att_s[rows:, lanes] = bottom.astype(BF16)
    att = att_s[...]
    attlow_ref[...] = att.reshape(2, rows, width)
    branch = jnp.dot(att, ow_ref[...], preferred_element_type=F32)
    middle = x_ref[...].reshape(both, width).astype(F32) + gate_one * branch
    n, inverse = normalise(middle)
    hidden = (n * gain * (1.0 + scale) + shift).astype(BF16)
    hidden_ref[...] = hidden.reshape(2, rows, width)
    shares, _, chunk = up_ref.shape
    feed = None
    following = jnp.dot(hidden, up_ref[0], preferred_element_type=F32)
    for index in range(shares):
        cols = slice(index * chunk, (index + 1) * chunk)
        pre = following + bias_ref[index, 0:1]
        if index + 1 < shares:
            following = jnp.dot(hidden, up_ref[index + 1], preferred_element_type=F32)
        square = pre * pre
        root = math.sqrt(2.0 / math.pi)
        tanh = jnp.tanh(pre * (root + (root * 0.044715) * square))
        half_up = 0.5 + 0.5 * tanh
        act = (pre * half_up).astype(BF16)
        slope_s[:, cols] = half_up + (0.5 * pre) * (1.0 - tanh * tanh) * (
            root + (3.0 * root * 0.044715) * square
        )
        act_ref[:, :, cols] = act.reshape(2, rows, chunk)
        part = jnp.dot(act, down_ref[index], preferred_element_type=F32)
        feed = part if feed is None else feed + part
    feed = feed + down_bias
    out_ref[...] = (middle + gate_two * feed).astype(BF16).reshape(2, rows, width)
    cot = cot_ref[...].reshape(both, width).astype(F32)
    gfeed = (gate_two * cot).astype(BF16)
    gfeed_ref[...] = gfeed.reshape(2, rows, width)
    ghidden = None
    up_sums = []
    for index in range(shares):
        cols = slice(index * chunk, (index + 1) * chunk)
        gact = lax.dot_general(gfeed, down_ref[index], NT, preferred_element_type=F32)
        gpre = (gact * slope_s[:, cols]).astype(BF16)
        gpre_ref[:, :, cols] = gpre.reshape(2, rows, chunk)
        up_sums.append(jnp.sum(gpre.astype(F32), axis=0, keepdims=True))
        part = lax.dot_general(gpre, up_ref[index], NT, preferred_element_type=F32)
        ghidden = part if ghidden is None else ghidden + part
    e = ghidden * ((1.0 + scale) * gain)
    mgrad = cot + inverse * (
        e - jnp.mean(e, axis=-1, keepdims=True) - n * jnp.mean(e * n, axis=-1, keepdims=True)
    )
    mgrad_ref[...] = mgrad.reshape(2, rows, width)
    gbranch = (gate_one * mgrad).astype(BF16)
    gbranch_ref[...] = gbranch.reshape(2, rows, width)
    gatt = lax.dot_general(gbranch, ow_ref[...], NT, preferred_element_type=F32)
    for pair in range(pairs):
        value = gatt[:, pair * 2 * HD : (pair + 1) * 2 * HD]
        even, odd = exchange(value[:rows], value[rows:])
        gatt_ref[2 * pair] = even.astype(BF16)
        gatt_ref[2 * pair + 1] = odd.astype(BF16)
    add = lambda value: jnp.sum(value, axis=0, keepdims=True)

    @pl.when(step == 0)
    def _():
        sums_ref[...] = jnp.zeros_like(sums_ref)
        upsum_ref[...] = jnp.zeros_like(upsum_ref)

    sums_ref[0:1, :] += add(ghidden)
    sums_ref[1:2, :] += add(ghidden * n)
    sums_ref[2:3, :] += add(cot * feed)
    sums_ref[3:4, :] += add(gfeed.astype(F32))
    sums_ref[4:5, :] += add(mgrad * branch)
    for index, value in enumerate(up_sums):
        upsum_ref[0:1, index * chunk : (index + 1) * chunk] += value


def once(shape):
    zeros = (0,) * len(shape)
    return pl.BlockSpec(shape, lambda *_: zeros, pipeline_mode=pl.Buffered(1))


def middle_pass(x2, cot2, att, vecs, out_weight, up_all, down_all, bias_all, rows=128):
    half, width = x2.shape[1:]
    heads = width // HD
    units = up_all.shape[0] * up_all.shape[2]
    tok = lambda last: pl.BlockSpec((2, rows, last), lambda i: (0, i, 0))
    pack = pl.BlockSpec((heads, rows, 2 * HD), lambda i: (0, i, 0))
    token = lambda last, kind: jax.ShapeDtypeStruct((2, half, last), kind)
    return pl.pallas_call(
        middle_kernel,
        grid=(half // rows,),
        in_specs=[
            tok(width), tok(width), pack, whole(vecs.shape), once(out_weight.shape),
            once(up_all.shape), once(down_all.shape), once(bias_all.shape),
        ],
        out_specs=[
            tok(width), tok(width), tok(width), tok(units), tok(width), tok(units), tok(width),
            tok(width), pack, whole((8, width)), whole((8, units)),
        ],
        out_shape=[
            token(width, BF16), token(width, BF16), token(width, BF16), token(units, BF16),
            token(width, BF16), token(units, BF16), token(width, F32), token(width, BF16),
            jax.ShapeDtypeStruct((heads, half, 2 * HD), BF16),
            jax.ShapeDtypeStruct((8, width), F32),
            jax.ShapeDtypeStruct((8, units), F32),
        ],
        scratch_shapes=[pltpu.VMEM((2 * rows, width), BF16), pltpu.VMEM((2 * rows, units), F32)],
        compiler_params=params("arbitrary"),
        name="middle_pass",
    )(x2, cot2, att, vecs, out_weight, up_all, down_all, bias_all)


def feed_grads_kernel(
    hidden_ref, gfeed_ref, att_ref, gbranch_ref, act_ref, gpre_ref, gatt, held, dos,
    hidden_s, gfeed_s, att_s, act_s, gpre_s, sent, got, crossed, send_sems, recv_sems, own_sems,
):
    group = lax.axis_index("grp")
    place = lax.axis_index("seq")
    _, core, _, other_core = mlp_place()
    sems = (send_sems, recv_sems)
    ahead = lambda s: (place + s) % 4

    def first(s):
        return reach(gatt.at[2 * ahead(s)], dos.at[0, s], sems, s - 1, 1, ahead(s))

    def second(s):
        return reach(gatt.at[2 * ahead(s) + 1], dos.at[1, s], sems, 2 + s, 1, ahead(s))

    def cross(s):
        return reach(gatt.at[8 + ahead(s)], crossed.at[s], sems, 6 + s, 0, place)

    def onward(s):
        return reach(crossed.at[s], dos.at[1, s], sems, 9 + s, 0, ahead(s))

    def swap(y):
        return push(sent.at[y], got.at[y], sems, 13 + y, {"mlp": other_core})

    width = hidden_s.shape[0]

    def loads(order, index):
        cols = pl.ds(pl.multiple_of(index * width, width), width)
        return (
            pltpu.make_async_copy(gpre_ref.at[:, cols], gpre_s.at[order], own_sems.at[0, order]),
            pltpu.make_async_copy(act_ref.at[:, cols], act_s.at[order], own_sems.at[1, order]),
        )

    for y in range(2):
        for load in loads(y, 2 * y + 1 - core):
            load.start()
    for y in range(2):
        for load in loads(2 + y, 2 * y + core):
            load.start()
    greet(neighbours(group, place, [other_core]))

    @pl.when(group == 1)
    def _():
        for s in (1, 2, 3):
            cross(s).start()
            first(s).start()
            second(s).start()
        cross(0).start()
        dos[0, 0] = gatt[2 * place]
        dos[1, 0] = gatt[2 * place + 1]

    hidden_s[...] = hidden_ref[...].T
    gfeed_s[...] = gfeed_ref[...].T
    att_s[...] = att_ref[...].T
    split = width // 4
    part = split // 4
    rows = 3 * part

    def blocks(target, y, index, order):
        for load in loads(order, index):
            load.wait()
        up = jnp.dot(hidden_s[...], gpre_s[order], preferred_element_type=F32).astype(BF16)
        down = jnp.dot(gfeed_s[...], act_s[order], preferred_element_type=F32).astype(BF16)
        own = jnp.concatenate(
            [
                att_s[pl.ds(pl.multiple_of(index * part + z * split, 16), part), :]
                for z in range(4)
            ]
        )
        out = jnp.dot(own, gbranch_ref[...], preferred_element_type=F32).astype(BF16)
        for z in range(4):
            start = z * split
            pieces = (
                (up[start : start + rows],),
                (up[start + rows : start + split], down[start : start + split - rows + part]),
                (down[start + 2 * part : start + split], out[z * part : (z + 1) * part]),
            )
            for number, values in enumerate(pieces):
                base = 0
                for value in values:
                    size = value.shape[0]
                    for lane in range(width // (2 * HD)):
                        target[y, z, number * 6 + lane, base : base + size, :] = value[
                            :, lane * 2 * HD : (lane + 1) * 2 * HD
                        ]
                    base += size

    def send_row(y, carry):
        blocks(sent, y, 2 * y + 1 - core, y)
        swap(y).start()
        return carry

    lax.fori_loop(0, 2, send_row, 0)

    @pl.when(group == 0)
    def _():
        for s in (1, 2, 3):
            cross(s).wait_recv()
            onward(s).start()
        cross(0).wait_recv()
        dos[1, 0] = crossed[0]

    def keep_row(y, carry):
        blocks(held, y, 2 * y + core, 2 + y)
        return carry

    lax.fori_loop(0, 2, keep_row, 0)

    def add_row(y, carry):
        swap(y).wait()

        def add(z, inner):
            held[y, z] = added(held[y, z], got[y, z])
            return inner

        return lax.fori_loop(0, 4, add, carry)

    lax.fori_loop(0, 2, add_row, 0)

    @pl.when(group == 1)
    def _():
        for s in (1, 2, 3):
            first(s).wait()
            second(s).wait()
        for s in range(4):
            cross(s).wait_send()

    @pl.when(group == 0)
    def _():
        for s in (1, 2, 3):
            onward(s).wait()


def feed_grads(hidden, gfeed, att, gbranch, act, gpre, gatt):
    tokens, width = hidden.shape
    _, half, lanes = gatt.shape
    rows = 3 * width // 16
    share = (2, 4, BLOCKS, rows, lanes)
    return pl.pallas_call(
        feed_grads_kernel,
        in_specs=in_vmem(4) + [pl.BlockSpec(memory_space=pl.ANY)] * 2 + in_vmem(1),
        out_specs=in_vmem(2),
        out_shape=[
            jax.ShapeDtypeStruct(share, BF16),
            jax.ShapeDtypeStruct((2, 4, half, lanes), BF16),
        ],
        scratch_shapes=[pltpu.VMEM((width, tokens), BF16)] * 3
        + [pltpu.VMEM((4, tokens, width), BF16)] * 2
        + [
            pltpu.VMEM(share, BF16),
            pltpu.VMEM(share, BF16),
            pltpu.VMEM((4, half, lanes), BF16),
            pltpu.SemaphoreType.DMA((15,)),
            pltpu.SemaphoreType.DMA((15,)),
            pltpu.SemaphoreType.DMA((2, 4)),
        ],
        compiler_params=pltpu.CompilerParams(
            collective_id=3, has_side_effects=True, vmem_limit_bytes=WHOLE_VMEM
        ),
        cost_estimate=pl.CostEstimate(
            flops=24_000_000_000, bytes_accessed=20_000_000, transcendentals=0
        ),
        name="feed_grads",
    )(hidden, gfeed, att, gbranch, act, gpre, gatt)


SMALL_ROWS = 40


def finish_kernel(
    packs, cosine, sine, normed_ref, vec_one, vec_two, middle_sums, up_sums, extra, feed_two,
    w_ref, x_ref, mgrad_ref, ada_ref,
    qkv_out, up_out, down_out, out_out, sums_out, ada_out, table_out, grad_ref,
    total, feed_total, rows_all, mixed, w_s, x_s, mgrad_s, ada_s, sums, small, sent, got, held, one_p, one_q, two, others,
    three, feed_others, feed_three, send_sems, recv_sems, own_sems,
):
    group = lax.axis_index("grp")
    place = lax.axis_index("seq")
    row, core, _, other_core = mlp_place()
    mlp = row * 2 + core
    sems = (send_sems, recv_sems)
    ahead = lambda s: (place + s) % 4
    heads = packs.shape[0]
    half = packs.shape[2]
    width = heads * HD
    lanes = 2 * HD
    parts = 3
    each = BLOCKS // parts

    loads = [
        pltpu.make_async_copy(source, target, own_sems.at[index])
        for index, (source, target) in enumerate(
            ((w_ref, w_s), (x_ref, x_s), (mgrad_ref, mgrad_s), (ada_ref, ada_s))
        )
    ]
    for load in loads:
        load.start()
    greet(
        [{"seq": ahead(s)} for s in (1, 2, 3)]
        + [{"mlp": (mlp + s) % 4} for s in (1, 2, 3)]
        + [{"grp": 1 - group}]
    )
    _, _, _, feed_over, feed_four, feed_five = sum_steps(
        None, None, None, feed_two, feed_others, feed_three, feed_total, sems, 0
    )
    sum_one, sum_two, sum_three, sum_over, sum_four, sum_five = sum_steps(
        held, one_p, one_q, two, others, three, total, sems, 9
    )
    feed_over()

    def swap(index):
        own = pl.ds(index * each, each)
        return push(
            sent.at[:, :, own], got.at[:, :, own], sems, 18 + index, {"mlp": other_core}
        )

    def unrotate(part):
        def one_pair(pair, carry):
            top, bottom = exchange(
                packs[2 * pair, part].astype(F32), packs[2 * pair + 1, part].astype(F32)
            )
            if part < 2:
                top = turn(top, cosine[0], -sine[0])
                bottom = turn(bottom, cosine[1], -sine[1])
            cols = pl.ds(pl.multiple_of(part * width + pair * lanes, lanes), lanes)
            mixed[:half, cols] = top.astype(BF16)
            mixed[half:, cols] = bottom.astype(BF16)
            return carry

        lax.fori_loop(0, heads // 2, one_pair, 0)

    def blocks(target, which, index):
        value = jnp.dot(
            normed_ref[which], mixed[:, index * width : (index + 1) * width],
            preferred_element_type=F32,
        ).astype(BF16)
        for lane in range(each):
            target[:, :, index * each + lane] = value[
                :, lane * lanes : (lane + 1) * lanes
            ].reshape(2, 4, width // 16, lanes)

    for index in (2, 0, 1):
        unrotate(index)
        blocks(sent, 1 - core, index)
        swap(index).start()
    for index in range(parts):
        blocks(held, core, index)
    for index in range(parts):
        swap(index).wait()
    for y in range(2):

        def add(z, carry, y=y):
            held[y, z] = added(held[y, z], got[y, z])
            return carry

        lax.fori_loop(0, 4, add, 0)
    sum_one()
    for load in loads:
        load.wait()
    chunk = half // 2
    sums[...] = jnp.zeros_like(sums)

    def store(index):
        own = pl.ds(index * chunk, chunk)
        return pltpu.make_async_copy(mgrad_s.at[own], grad_ref.at[own], own_sems.at[4 + index])

    for index in range(4):
        own = slice(index * chunk, (index + 1) * chunk)
        gnormed = lax.dot_general(mixed[own, :], w_s[...], NT, preferred_element_type=F32)
        n, inverse = normalise(x_s[own, :].astype(F32))
        e = gnormed * ((1.0 + vec_one[1:2, :]) * vec_one[0:1, :])
        mgrad_s[own, :] = mgrad_s[own, :] + inverse * (
            e - jnp.mean(e, axis=-1, keepdims=True) - n * jnp.mean(e * n, axis=-1, keepdims=True)
        )
        store(index).start()
        sums[0:1, :] += jnp.sum(gnormed, axis=0, keepdims=True)
        sums[1:2, :] += jnp.sum(gnormed * n, axis=0, keepdims=True)
        if index == 1:
            feed_four()
        if index == 2:
            sum_two()

    first_sum, second_sum = sums[1:2, :], middle_sums[1:2, :]
    mod = [
        sums[0:1, :], vec_one[0:1, :] * first_sum, middle_sums[4:5, :], middle_sums[0:1, :],
        vec_two[1:2, :] * second_sum, middle_sums[2:3, :],
    ]
    wholes = [
        (1.0 + vec_one[1:2, :]) * first_sum, (1.0 + vec_two[2:3, :]) * second_sum,
        middle_sums[3:4, :],
    ]
    weighted = None
    for index, value in enumerate(mod):
        part = jnp.sum(
            ada_s[:, index * width : (index + 1) * width].astype(F32) * value, axis=1,
            keepdims=True,
        )
        weighted = part if weighted is None else weighted + part
    table_row = jnp.broadcast_to(weighted, (lanes, lanes)).T[0:1] * extra[2:3, :]
    tiles = width // lanes
    for z in range(4):
        for line in range(9):
            tile = 9 * z + line
            value = mod[tile // tiles]
            start = (tile % tiles) * lanes
            small[z, line : line + 1, :] = value[:, start : start + lanes]
        for line in range(tiles):
            start = z * width + line * lanes
            small[z, 9 + line : 10 + line, :] = up_sums[0:1, start : start + lanes]
            for index, value in enumerate(wholes):
                at = 15 + index * tiles + line
                small[z, at : at + 1, :] = value[:, line * lanes : (line + 1) * lanes]
        small[z, 33:34, :] = table_row
        small[z, 34:36, :] = extra[0:2, :]
        small[z, 36:40, :] = jnp.zeros((4, lanes), F32)

    def hop_place(s):
        return push(
            small.at[ahead(s)], rows_all.at[group, mlp, place], sems, 20 + s, {"seq": ahead(s)}
        )

    def hop_place_in(s):
        return push(
            small.at[ahead(s)], rows_all.at[group, mlp, ahead(4 - s)], sems, 20 + s,
            {"seq": ahead(s)},
        )

    def hop_mlp(s, from_place):
        own = rows_all.at[group, from_place]
        return push(own, own, sems, 23 + s, {"mlp": (mlp + s) % 4})

    def hop_group(from_group):
        own = rows_all.at[from_group]
        return push(own, own, sems, 27, {"grp": 1 - group})

    for s in (1, 2, 3):
        hop_place(s).start()
    rows_all[group, mlp, place] = small[place]
    sum_three()
    sum_over()
    feed_five()
    share_rows = feed_total.shape[1]
    part_rows = share_rows // 3
    for lane in range(tiles):
        at = slice(lane * lanes, (lane + 1) * lanes)
        one, two_, three_ = (feed_total[6 * index + lane].astype(F32) for index in range(3))
        up_out[:share_rows, at] = one
        up_out[share_rows:, at] = two_[:part_rows]
        down_out[: 2 * part_rows, at] = two_[part_rows:]
        down_out[2 * part_rows :, at] = three_[: 2 * part_rows]
        out_out[:, at] = three_[2 * part_rows :]
    for s in (1, 2, 3):
        hop_place_in(s).wait()
    for s in (1, 2, 3):
        hop_mlp(s, mlp).start()
    sum_four()
    for s in (1, 2, 3):
        hop_mlp(s, mlp).wait_send()
        hop_mlp(s, (mlp + 4 - s) % 4).wait_recv()
    hop_group(group).start()
    sum_five()
    for block in range(BLOCKS):
        qkv_out[:, block * lanes : (block + 1) * lanes] = total[block].astype(F32)
    hop_group(group).wait_send()
    hop_group(1 - group).wait_recv()
    every = rows_all[...].reshape(32, SMALL_ROWS, lanes)
    sums_out[...] = jnp.sum(every, axis=0)
    conditions = every[:, 34].astype(BF16).astype(F32)
    for line in range(9):
        ada_out[:, line * lanes : (line + 1) * lanes] = lax.dot_general(
            conditions, every[:, line], TN, precision=highest, preferred_element_type=F32
        )
    table_rows = table_out.shape[0]
    first_row = (place * 4 + mlp) * table_rows
    owned = first_row + lax.broadcasted_iota(jnp.int32, (table_rows, 32), 0)
    steps = every[:, 35].T[:table_rows]
    chosen = jnp.where(owned.astype(F32) == steps, 1.0, 0.0)
    table_out[...] = jnp.dot(chosen, every[:, 33], precision=highest, preferred_element_type=F32)
    for index in range(4):
        store(index).wait()


def finish(
    packs, cosine, sine, normed, vec_one, vec_two, middle_sums, up_sums, extra, feed_two, weight,
    x, mgrad, ada_weight, table_rows,
):
    rows = normed.shape[1] // 8
    lanes = 2 * HD
    share = (2, 4, BLOCKS, rows, lanes)
    feed_rows = feed_two.shape[2]
    tokens, width = x.shape
    like = lambda value: pltpu.VMEM(value.shape, value.dtype)
    apart = pl.BlockSpec(memory_space=pl.ANY)
    return pl.pallas_call(
        finish_kernel,
        in_specs=in_vmem(10) + [apart] * 4,
        out_specs=in_vmem(7) + [apart],
        out_shape=[
            jax.ShapeDtypeStruct(shape, F32)
            for shape in (
                (width // 16, 3 * width), (width // 4, width), (width // 4, width),
                (width // 16, width), (SMALL_ROWS, lanes), (lanes, 9 * lanes),
                (table_rows, lanes), (tokens, width),
            )
        ],
        scratch_shapes=[
            pltpu.VMEM(share[2:], BF16), pltpu.VMEM((BLOCKS, feed_rows, lanes), BF16),
            pltpu.VMEM((2, 4, 4, SMALL_ROWS, lanes), F32),
            pltpu.VMEM((tokens, 3 * width), BF16), like(weight), like(x), like(mgrad),
            like(ada_weight), pltpu.VMEM((8, width), F32), pltpu.VMEM((4, SMALL_ROWS, lanes), F32),
        ]
        + [pltpu.VMEM(share, BF16)] * 3
        + sum_scratch(rows, EARLY + MIDDLE + LATE)
        + sum_scratch(feed_rows, LATE)
        + [pltpu.SemaphoreType.DMA((28,))] * 2
        + [pltpu.SemaphoreType.DMA((8,))],
        compiler_params=pltpu.CompilerParams(
            collective_id=4, has_side_effects=True, vmem_limit_bytes=WHOLE_VMEM
        ),
        cost_estimate=pl.CostEstimate(
            flops=60_000_000_000, bytes_accessed=20_000_000, transcendentals=0
        ),
        name="finish",
    )(
        packs, cosine, sine, normed, vec_one, vec_two, middle_sums, up_sums, extra, feed_two,
        weight, x, mgrad, ada_weight,
    )


def four_shards(
    tokens, step_index, time_table, ada_weight, ada_bias, first_gain, qkv_weight, out_weight,
    second_gain, up_weight, up_bias, down_weight, down_bias, cotangent,
):
    place = lax.axis_index("seq")
    group = lax.axis_index("grp")
    mlp_count = lax.axis_size("mlp")
    token_rows, width = tokens.shape[1:]
    half = token_rows // 2
    lanes = 2 * HD
    up_all = lax.all_gather(up_weight, "mlp", axis=0)
    down_all = lax.all_gather(down_weight, "mlp", axis=0)

    frequency = jnp.exp(jnp.arange(HD // 2, dtype=F32) * (-2.0 * math.log(10000.0) / HD))
    frequency = jnp.concatenate([frequency] * 4)[None, :]
    near_rows = 32
    offset = jnp.where(group == 1, place * token_rows, 0)
    far_rows = offset + near_rows * jnp.arange(token_rows // near_rows, dtype=jnp.int32)

    def circle(positions):
        angles = positions.astype(F32)[:, None] * frequency
        return jnp.stack([jnp.cos(angles), jnp.sin(angles)])

    x2 = tokens.reshape(2, half, width)
    parameters = jnp.concatenate([ada_bias, first_gain, second_gain, down_bias, up_bias])[None, :]
    (
        packs, att, pieces, results, logs, logs_own, cosine, sine, vec_one, vec_two, extra,
        bias_all, blocks,
    ) = forward_attention(
        x2, qkv_weight, circle(jnp.arange(near_rows, dtype=jnp.int32)), circle(far_rows),
        step_index, time_table, ada_weight, parameters,
    )

    (
        output, att_low, hidden, act, grad_feed, grad_pre, middle_grad, grad_branch, grad_att,
        middle_sums, up_sums,
    ) = middle_pass(
        x2, cotangent.reshape(2, half, width), att, vec_two, out_weight, up_all, down_all,
        bias_all,
    )
    flat = lambda value: value.reshape(token_rows, value.shape[2])
    feed_held, att_grads = feed_grads(
        *(flat(value) for value in (hidden, grad_feed, att_low, grad_branch, act, grad_pre)),
        grad_att,
    )
    grads, feed_two = backward_attention(
        packs, grad_att, att, pieces, results, logs, logs_own, att_grads, feed_held
    )
    ranks = 4 * mlp_count
    (
        qkv_total, up_total, down_total, out_total, row_sums, ada_rows, table_share, input_grad,
    ) = finish(
        grads, cosine, sine, blocks, vec_one, vec_two, middle_sums, up_sums, extra, feed_two,
        qkv_weight, flat(x2), flat(middle_grad), ada_weight, time_table.shape[0] // ranks,
    )
    mlp = lax.axis_index("mlp")
    rank = place * mlp_count + mlp

    def share(value, index, count):
        each = value.shape[-1] // count
        return lax.dynamic_slice_in_dim(value, index * each, each, value.ndim - 1)

    mod_sums, up_bias_sums, first_sums, second_sums, down_bias_sums = (
        row_sums[start:end].reshape(-1)
        for start, end in ((0, 9), (9, 15), (15, 21), (21, 27), (27, 33))
    )
    return (
        output.reshape(1, token_rows, width),
        input_grad.reshape(1, token_rows, width),
        table_share,
        share(ada_rows, mlp, mlp_count),
        share(mod_sums, mlp, mlp_count),
        share(first_sums, rank, ranks),
        qkv_total,
        out_total,
        share(second_sums, rank, ranks),
        up_total,
        share(up_bias_sums, mlp, mlp_count),
        down_total.T,
        share(down_bias_sums, rank, ranks),
    )


def solution(mesh):
    in_specs = (
        P(("grp", "mlp"), "seq", None),
        P(("grp", "mlp"), None),
        P(),
        P(),
        P(),
        P(),
        P(),
        P(),
        P(),
        P(None, "mlp"),
        P("mlp"),
        P("mlp", None),
        P(),
        P(("grp", "mlp"), "seq", None),
    )
    out_specs = (
        P(("grp", "mlp"), "seq", None),
        P(("grp", "mlp"), "seq", None),
        P(("seq", "mlp"), None),
        P(None, ("seq", "mlp")),
        P(("seq", "mlp")),
        P(("seq", "mlp")),
        P(("seq", "mlp"), None),
        P(("seq", "mlp"), None),
        P(("seq", "mlp")),
        P("seq", "mlp"),
        P(("seq", "mlp")),
        P("mlp", "seq"),
        P(("seq", "mlp")),
    )
    body = four_shards if mesh.shape["seq"] == 4 and mesh.shape["grp"] == 2 else shards
    return jax.shard_map(body, mesh=mesh, in_specs=in_specs, out_specs=out_specs, check_vma=False)
```

```python
import math

import jax
import jax.numpy as jnp
from jax import lax
from jax.experimental import pallas as pl
from jax.experimental.pallas import tpu as pltpu
from jax.sharding import PartitionSpec as P

HD = 64


highest = lax.Precision.HIGHEST


def shifted(value, axis, steps):
    count = lax.axis_size(axis)
    pairs = [(source, (source + steps) % count) for source in range(count)]
    return lax.ppermute(value, axis, pairs)


def layer_norm(values, norm_gain):
    centred = values - jnp.mean(values, axis=-1, keepdims=True)
    spread = jnp.mean(centred * centred, axis=-1, keepdims=True)
    return centred * lax.rsqrt(spread + 1e-05) * norm_gain


def modulate(values, norm_gain, shift_part, scale_part):
    return layer_norm(values, norm_gain) * (1.0 + scale_part) + shift_part


def gelu_tanh(values):
    return jax.nn.gelu(values, approximate=True)


def rotate_pairs(values, positions):
    half_dim = HD // 2
    frequency = jnp.exp(jnp.arange(half_dim, dtype=jnp.float32) * (-2.0 * math.log(10000.0) / HD))
    angles = positions.astype(jnp.float32)[:, None] * frequency[None, :]
    cosine = jnp.cos(angles)[:, None, :]
    sine_part = jnp.sin(angles)[:, None, :]
    leading = values[..., :half_dim]
    trailing = values[..., half_dim:]
    return jnp.concatenate(
        [leading * cosine - trailing * sine_part, trailing * cosine + leading * sine_part], axis=-1
    )


def shards(
    tokens,
    step_index,
    time_table,
    ada_weight,
    ada_bias,
    first_gain,
    qkv_weight,
    out_weight,
    second_gain,
    up_weight,
    up_bias,
    down_weight,
    down_bias,
    cotangent,
):
    seq_count = lax.axis_size("seq")
    seq_place = lax.axis_index("seq")
    group_index = lax.axis_index("grp")
    mlp_place = lax.axis_index("mlp")
    tok_rows = tokens.shape[1]
    model_width = tokens.shape[2]
    head_count = model_width // HD
    score_scale = 1.0 / math.sqrt(HD)
    line_len = tok_rows * seq_count
    seq_length = jnp.where(group_index == 0, line_len // 4, line_len).astype(jnp.int32)
    row_ids = jnp.arange(tok_rows, dtype=jnp.int32)
    own_pos = seq_place * tok_rows + row_ids
    positions = own_pos % seq_length
    quarter = seq_place // (seq_count // 4)
    step_value = jnp.sum(jnp.where(jnp.arange(4, dtype=jnp.int32) == quarter, step_index[0], 0))
    table_pick = jnp.arange(time_table.shape[0], dtype=jnp.int32) == step_value
    embedded = jnp.dot(
        table_pick.astype(jnp.bfloat16)[None, :], time_table, preferred_element_type=jnp.float32
    )[0]
    condition, silu_back = jax.vjp(jax.nn.silu, embedded)
    cond_low = condition.astype(jnp.bfloat16)
    modulation = jnp.dot(cond_low[None, :], ada_weight, preferred_element_type=jnp.float32)[
        0
    ] + ada_bias.astype(jnp.float32)
    shift_one, scale_one, gate_one, shift_two, scale_two, gate_two = jnp.split(modulation, 6)
    inputs = tokens[0].astype(jnp.float32)
    normed, first_back = jax.vjp(
        modulate, inputs, first_gain.astype(jnp.float32), shift_one, scale_one
    )
    normed_low = normed.astype(jnp.bfloat16)
    mixed_rows = jnp.dot(normed_low, qkv_weight, preferred_element_type=jnp.float32)

    def rotate_all(mixed_in):
        query_part = rotate_pairs(
            mixed_in[:, :model_width].reshape(tok_rows, head_count, HD), positions
        )
        key_part = rotate_pairs(
            mixed_in[:, model_width : 2 * model_width].reshape(tok_rows, head_count, HD), positions
        )
        return (
            query_part,
            key_part,
            mixed_in[:, 2 * model_width :].reshape(tok_rows, head_count, HD),
        )

    rotated, rotate_back = jax.vjp(rotate_all, mixed_rows)
    queries = rotated[0].astype(jnp.bfloat16)
    key_rows = rotated[1].astype(jnp.bfloat16)
    value_rows = rotated[2].astype(jnp.bfloat16)
    start_state = (
        jnp.full((head_count, tok_rows), -1e30, jnp.float32),
        jnp.zeros((head_count, tok_rows), jnp.float32),
        jnp.zeros((head_count, tok_rows, HD), jnp.float32),
    )
    key_piece = lax.all_gather(key_rows.reshape(tok_rows, model_width), "seq", axis=0, tiled=True)
    value_piece = lax.all_gather(
        value_rows.reshape(tok_rows, model_width), "seq", axis=0, tiled=True
    )
    piece_rows = key_piece.shape[0]
    sub_rows = math.gcd(piece_rows, 512)

    def one_block(block_index, block_state):
        run_max, run_total, run_acc = block_state
        offset = block_index * sub_rows
        key_block = lax.dynamic_slice_in_dim(key_piece, offset, sub_rows, 0).reshape(
            sub_rows, head_count, HD
        )
        value_block = lax.dynamic_slice_in_dim(value_piece, offset, sub_rows, 0).reshape(
            sub_rows, head_count, HD
        )
        key_pos = offset + jnp.arange(sub_rows, dtype=jnp.int32)
        same_seq = (own_pos // seq_length)[:, None] == (key_pos // seq_length)[None, :]
        scores = (
            jnp.einsum("qhd,khd->hqk", queries, key_block, preferred_element_type=jnp.float32)
            * score_scale
        )
        masked = jnp.where(same_seq[None], scores, -1e30)
        new_max = jnp.maximum(run_max, jnp.max(masked, axis=-1))
        shrink = jnp.exp(run_max - new_max)
        weights = jnp.where(same_seq[None], jnp.exp(masked - new_max[..., None]), 0.0)
        run_total = run_total * shrink + jnp.sum(weights, axis=-1)
        run_acc = run_acc * shrink[..., None] + jnp.einsum(
            "hqk,khd->hqd",
            weights.astype(jnp.bfloat16),
            value_block,
            preferred_element_type=jnp.float32,
        )
        return (new_max, run_total, run_acc)

    run_max, run_total, run_acc = lax.fori_loop(0, piece_rows // sub_rows, one_block, start_state)
    log_total = run_max + jnp.log(run_total)
    attended3 = jnp.transpose(run_acc / run_total[..., None], (1, 0, 2))
    attended_low = attended3.reshape(tok_rows, model_width).astype(jnp.bfloat16)
    branch = jnp.dot(attended_low, out_weight, preferred_element_type=jnp.float32)
    middle = inputs + gate_one * branch
    hidden, second_back = jax.vjp(
        modulate, middle, second_gain.astype(jnp.float32), shift_two, scale_two
    )
    hidden_low = hidden.astype(jnp.bfloat16)
    gathered = lax.all_gather(hidden_low, "mlp", axis=0, tiled=True)
    pre_act = jnp.dot(gathered, up_weight, preferred_element_type=jnp.float32) + up_bias.astype(
        jnp.float32
    )
    activated, gelu_back = jax.vjp(gelu_tanh, pre_act)
    act_low = activated.astype(jnp.bfloat16)
    feed_terms = jnp.dot(act_low, down_weight, preferred_element_type=jnp.float32)
    feed_out = lax.psum_scatter(
        feed_terms, "mlp", scatter_dimension=0, tiled=True
    ) + down_bias.astype(jnp.float32)
    output = (middle + gate_two * feed_out).astype(jnp.bfloat16)[None]
    grad_out = cotangent[0].astype(jnp.float32)
    gate_two_grad = jnp.sum(grad_out * feed_out, axis=0)
    grad_feed = (gate_two * grad_out).astype(jnp.bfloat16)
    down_bias_grad = jnp.sum(grad_feed, axis=0, dtype=jnp.float32)
    grad_rows = lax.all_gather(grad_feed, "mlp", axis=0, tiled=True)
    down_grad = jnp.einsum("tf,td->fd", act_low, grad_rows, preferred_element_type=jnp.float32)
    grad_act = jnp.einsum("td,fd->tf", grad_rows, down_weight, preferred_element_type=jnp.float32)
    grad_pre = gelu_back(grad_act)[0].astype(jnp.bfloat16)
    up_grad = jnp.einsum("td,tf->df", gathered, grad_pre, preferred_element_type=jnp.float32)
    local_units = up_weight.shape[1]
    bias_slot = lax.dynamic_update_slice_in_dim(
        jnp.zeros((local_units * lax.axis_size("mlp"),), jnp.float32),
        jnp.sum(grad_pre, axis=0, dtype=jnp.float32),
        mlp_place * local_units,
        0,
    )
    hidden_terms = jnp.einsum("tf,df->td", grad_pre, up_weight, preferred_element_type=jnp.float32)
    grad_hidden = lax.psum_scatter(hidden_terms, "mlp", scatter_dimension=0, tiled=True)
    middle_part, second_gain_grad, shift_two_grad, scale_two_grad = second_back(grad_hidden)
    middle_grad = grad_out + middle_part
    gate_one_grad = jnp.sum(middle_grad * branch, axis=0)
    grad_branch = (gate_one * middle_grad).astype(jnp.bfloat16)
    out_grad = jnp.einsum(
        "td,te->de", attended_low, grad_branch, preferred_element_type=jnp.float32
    )
    grad_attended = jnp.einsum(
        "te,de->td", grad_branch, out_weight, preferred_element_type=jnp.float32
    ).astype(jnp.bfloat16)
    grad_heads = grad_attended.reshape(tok_rows, head_count, HD)
    row_delta = jnp.transpose(jnp.sum(grad_heads.astype(jnp.float32) * attended3, axis=-1))

    def pair_grads(
        query_set, grad_set, total_set, delta_set, query_anchor, key_set, value_set, key_anchor
    ):
        query_pos = query_anchor * tok_rows + row_ids
        key_pos = key_anchor * tok_rows + row_ids
        same_seq = (query_pos // seq_length)[:, None] == (key_pos // seq_length)[None, :]
        scores = (
            jnp.einsum("qhd,khd->hqk", query_set, key_set, preferred_element_type=jnp.float32)
            * score_scale
        )
        prob_rows = jnp.where(same_seq[None], jnp.exp(scores - total_set[..., None]), 0.0)
        value_part = jnp.einsum(
            "hqk,qhd->khd",
            prob_rows.astype(jnp.bfloat16),
            grad_set,
            preferred_element_type=jnp.float32,
        )
        prob_grad = jnp.einsum(
            "qhd,khd->hqk", grad_set, value_set, preferred_element_type=jnp.float32
        )
        score_grad = (prob_rows * (prob_grad - delta_set[..., None])).astype(jnp.bfloat16)
        query_part = (
            jnp.einsum("hqk,khd->qhd", score_grad, key_set, preferred_element_type=jnp.float32)
            * score_scale
        )
        key_part = (
            jnp.einsum("hqk,qhd->khd", score_grad, query_set, preferred_element_type=jnp.float32)
            * score_scale
        )
        return (query_part, key_part, value_part)

    zero_heads = jnp.zeros((tok_rows, head_count, HD), jnp.float32)

    def key_turn(running):
        key_set, value_set, key_acc, value_acc, anchor, query_acc = running
        query_part, key_part, value_part = pair_grads(
            queries, grad_heads, log_total, row_delta, seq_place, key_set, value_set, anchor
        )
        moved_rows = shifted((key_set, value_set), "seq", 1)
        moved_grads = shifted((key_acc + key_part, value_acc + value_part), "seq", 1)
        return (
            moved_rows[0],
            moved_rows[1],
            moved_grads[0],
            moved_grads[1],
            (anchor - 1) % seq_count,
            query_acc + query_part,
        )

    def two_key_turns(turn_index, running):
        return key_turn(key_turn(running))

    finished = lax.fori_loop(
        0,
        seq_count // 2,
        two_key_turns,
        (key_rows, value_rows, zero_heads, zero_heads, seq_place, zero_heads),
    )
    query_grad, key_grad, value_grad = (finished[5], finished[2], finished[3])
    mixed_grad = rotate_back((query_grad, key_grad, value_grad))[0].astype(jnp.bfloat16)
    qkv_grad = jnp.einsum("td,te->de", normed_low, mixed_grad, preferred_element_type=jnp.float32)
    grad_normed = jnp.einsum(
        "te,de->td", mixed_grad, qkv_weight, preferred_element_type=jnp.float32
    )
    input_part, first_gain_grad, shift_one_grad, scale_one_grad = first_back(grad_normed)
    input_grad = (middle_grad + input_part)[None]
    mod_grad = jnp.concatenate(
        [
            shift_one_grad,
            scale_one_grad,
            gate_one_grad,
            shift_two_grad,
            scale_two_grad,
            gate_two_grad,
        ]
    )
    ada_grad = cond_low.astype(jnp.float32)[:, None] * mod_grad[None, :]
    cond_grad = jnp.dot(ada_weight.astype(jnp.float32), mod_grad, precision=highest)
    table_local = table_pick.astype(jnp.float32)[:, None] * silu_back(cond_grad)[0][None, :]
    layer_sums = (
        lax.psum_scatter(table_local, ("seq", "mlp"), scatter_dimension=0, tiled=True),
        lax.psum_scatter(ada_grad, ("seq", "mlp"), scatter_dimension=1, tiled=True),
        lax.psum_scatter(mod_grad, ("seq", "mlp"), scatter_dimension=0, tiled=True),
        lax.psum_scatter(first_gain_grad, ("seq", "mlp"), scatter_dimension=0, tiled=True),
        lax.psum_scatter(qkv_grad, ("seq", "mlp"), scatter_dimension=0, tiled=True),
        lax.psum_scatter(out_grad, ("seq", "mlp"), scatter_dimension=0, tiled=True),
        lax.psum_scatter(second_gain_grad, ("seq", "mlp"), scatter_dimension=0, tiled=True),
        lax.psum_scatter(bias_slot, ("seq", "mlp"), scatter_dimension=0, tiled=True),
        lax.psum_scatter(down_bias_grad, ("seq", "mlp"), scatter_dimension=0, tiled=True),
    )
    feed_summed = (
        lax.psum_scatter(up_grad, "seq", scatter_dimension=0, tiled=True),
        lax.psum_scatter(down_grad, "seq", scatter_dimension=1, tiled=True),
    )
    totals = lax.psum(
        (
            layer_sums[0],
            layer_sums[1],
            layer_sums[2],
            layer_sums[3],
            layer_sums[4],
            layer_sums[5],
            layer_sums[6],
            layer_sums[7],
            layer_sums[8],
            feed_summed[0],
            feed_summed[1],
        ),
        "grp",
    )
    return (
        output,
        input_grad,
        totals[0],
        totals[1],
        totals[2],
        totals[3],
        totals[4],
        totals[5],
        totals[6],
        totals[9],
        totals[7],
        totals[10],
        totals[8],
    )


LOG_SCALE = math.log2(math.e) / math.sqrt(HD)
NT = (((1,), (1,)), ((), ()))
TN = (((0,), (0,)), ((), ()))
F32 = jnp.float32
BF16 = jnp.bfloat16
WHOLE_VMEM = 60 * 1024 * 1024


def params(*semantics):
    return pltpu.CompilerParams(vmem_limit_bytes=WHOLE_VMEM, dimension_semantics=semantics)


def low_lanes(value):
    return lax.broadcasted_iota(jnp.int32, value.shape, 1) < HD


def swap_heads(value):
    return pltpu.roll(value, HD, 1)


def exchange(top, bottom):
    keep = low_lanes(top)
    return (
        jnp.where(keep, top, swap_heads(bottom)),
        jnp.where(keep, swap_heads(top), bottom),
    )


def fold(value):
    half = value.shape[0] // 2
    top = value[:half]
    return jnp.where(low_lanes(top), top, swap_heads(value[half:]))


def unfold_into(target, base, packed, fill):
    half = packed.shape[0]
    value = packed.astype(F32)
    keep = low_lanes(value)
    target[base : base + half, :] = jnp.where(keep, value, fill).astype(BF16)
    target[base + half : base + 2 * half, :] = jnp.where(keep, swap_heads(value), fill).astype(BF16)


def turn(value, cosine, sine):
    lane = lax.broadcasted_iota(jnp.int32, value.shape, 1) % HD
    quarter = HD // 2
    other = jnp.where(
        lane < quarter, pltpu.roll(value, 2 * HD - quarter, 1), pltpu.roll(value, quarter, 1)
    )
    return value * cosine + other * sine


def normalise(values):
    centred = values - jnp.mean(values, axis=-1, keepdims=True)
    spread = jnp.mean(centred * centred, axis=-1, keepdims=True)
    inverse = lax.rsqrt(spread + 1e-05)
    return centred * inverse, inverse


def attend_rows(q, k_ref, v_ref, keys, out_put, log_put, block=512):
    top = None
    for start in range(0, keys, block):
        s = lax.dot_general(q, k_ref[start : start + block, :], NT, preferred_element_type=F32)
        s = s * LOG_SCALE
        peak = jnp.max(s, axis=1, keepdims=True)
        new_top = peak if top is None else jnp.maximum(top, peak)
        p = jnp.exp2(s - new_top).astype(BF16)
        part = jnp.dot(p, v_ref[start : start + block, :], preferred_element_type=F32)
        acc = part if top is None else acc * jnp.exp2(top - new_top) + part
        top = new_top
    out_put(fold(acc / swap_heads(acc)).astype(BF16))
    log_put((top + jnp.log2(acc)).T[HD : HD + 8])


def load_values(source, base, k_s, v_s):
    unfold_into(k_s, base, source[1], 0.0)
    unfold_into(v_s, base, source[2], 1.0)


def packed_queries(packed):
    value = packed.astype(F32)
    return jnp.concatenate([value, swap_heads(value)]).astype(BF16)


def push(src, dst, sems, index, where):
    return pltpu.make_async_remote_copy(
        src_ref=src, dst_ref=dst, send_sem=sems[0].at[index], recv_sem=sems[1].at[index],
        device_id=where, device_id_type=pl.DeviceIdType.MESH,
    )


def reach(src, dst, sems, index, group, place):
    return push(src, dst, sems, index, {"grp": group, "seq": place})


def neighbours(group, place, others):
    found = [
        {"grp": (group + other) % 2, "seq": (place + steps) % 4}
        for other in range(2)
        for steps in range(4)
        if other or steps
    ]
    return found + [{"mlp": other} for other in others]


def greet(devices):
    barrier = pltpu.get_barrier_semaphore()
    for where in devices:
        pl.semaphore_signal(barrier, 1, device_id=where, device_id_type=pl.DeviceIdType.MESH)
    pl.semaphore_wait(barrier, len(devices))


def mlp_place():
    mlp = lax.axis_index("mlp")
    row, core = mlp // 2, mlp % 2
    return row, core, (1 - row) * 2 + core, row * 2 + 1 - core


BLOCKS = 18


def added(left, right):
    return (left.astype(F32) + right.astype(F32)).astype(BF16)


def sum_steps(held, one_p, one_q, two, others, three, out, sems, base, near=None):
    group = lax.axis_index("grp")
    place = lax.axis_index("seq")
    row, _, other_row, _ = mlp_place()
    by_row = {"mlp": other_row}
    by_group = {"grp": 1 - group}
    ahead = lambda s: (place + s) % 4

    def copies(stage):
        if stage == 1:
            return [
                push(held.at[1 - row, :, pl.ds(0, 10)], one_p, sems, base, by_row),
                push(
                    held.at[:, :, pl.ds(10 + 4 * (1 - group), 4)], one_q, sems, base + 1, by_group
                ),
            ]
        if stage == 2:
            return [
                push(
                    one_p.at[:, pl.ds(5 * (1 - group), 5)], two.at[:, pl.ds(0, 5)], sems,
                    base + 2, by_group,
                ),
                push(one_q.at[1 - row], two.at[:, pl.ds(5, 4)], sems, base + 3, by_row),
            ]
        if stage == 3:
            return [
                push(two.at[ahead(s)], others.at[s - 1], sems, base + 3 + s, {"seq": ahead(s)})
                for s in (1, 2, 3)
            ]
        return [
            push(three.at[pl.ds(0, 5)], out.at[pl.ds(5 * group, 5)], sems, base + 7, by_group),
            push(
                three.at[pl.ds(5, 4)], out.at[pl.ds(10 + 4 * group, 4)], sems, base + 8, by_group
            ),
        ]

    def start(stage):
        for copy in copies(stage):
            copy.start()

    def arrive(stage):
        for copy in copies(stage):
            copy.wait()

    def step_one():
        start(1)

    def step_two():
        arrive(1)

        def add(z, carry):
            own = held[row, z, 0:10] if near is None else near[0][z]
            one_p[z] = added(own, one_p[z])
            for y in range(2):
                own = held[y, z, pl.ds(10 + 4 * group, 4)] if near is None else near[1][y, z]
                one_q[y, z] = added(own, one_q[y, z])
            return carry

        lax.fori_loop(0, 4, add, 0)
        start(2)

    def step_three():
        arrive(2)

        def add(z, carry):
            two[z, 0:5] = added(one_p[z, pl.ds(5 * group, 5)], two[z, 0:5])
            two[z, 5:9] = added(one_q[row, z], two[z, 5:9])
            return carry

        lax.fori_loop(0, 4, add, 0)

    def step_over():
        start(3)

    def step_four():
        arrive(3)

        def add(block, carry):
            total = two[place, block].astype(F32)
            for s in range(3):
                total = total + others[s, block].astype(F32)
            three[block] = total.astype(BF16)
            return carry

        lax.fori_loop(0, 9, add, 0)
        start(4)
        out[pl.ds(5 * group, 5)] = three[0:5]
        out[pl.ds(10 + 4 * group, 4)] = three[5:9]

    def step_five():
        arrive(4)

    return step_one, step_two, step_three, step_over, step_four, step_five


def sum_scratch(rows, shapes):
    return [pltpu.VMEM(shape + (rows, 2 * HD), BF16) for shape in shapes]


EARLY = [(4, 10), (2, 4, 4)]
MIDDLE = [(4, 9)]
LATE = [(3, 9), (9,)]


def forward_kernel(
    x_ref, w_ref, near, far, step_ref, table, ada_ref, params_ref,
    packs_out, att, pieces, results, logs, logs_own, cosine, sine, vec_one, vec_two, extra,
    bias_all, blocks_out, packs, blocks, crossed, normed_s, k_s, v_s, send_sems, recv_sems,
    own_sems,
):
    group = lax.axis_index("grp")
    place = lax.axis_index("seq")
    sems = (send_sems, recv_sems)
    heads = packs.shape[0]
    rows = 2 * packs.shape[2]
    ahead = lambda s: (place + s) % 4
    behind = lambda s: (place + 4 - s) % 4

    def first(s):
        return reach(packs.at[2 * ahead(s)], pieces.at[0, s], sems, s - 1, 1, ahead(s))

    def second_values(s):
        source = packs.at[2 * ahead(s) + 1, pl.ds(1, 2)]
        return reach(source, pieces.at[1, s, pl.ds(1, 2)], sems, 2 + s, 1, ahead(s))

    def second_queries(s):
        source = packs.at[2 * ahead(s) + 1, 0]
        return reach(source, pieces.at[1, s, 0], sems, 5 + s, 1, ahead(s))

    def cross(s):
        return reach(packs.at[8 + ahead(s)], crossed.at[s], sems, 9 + s, 0, place)

    def onward(s):
        return reach(crossed.at[s], pieces.at[1, s], sems, 12 + s, 0, ahead(s))

    def home(kind, s, head):
        start = (16, 20, 24)[kind]
        return reach(
            results.at[min(kind, 1), s], att.at[head], sems, start + s, 1, behind(s)
        )

    row, core, _, _ = mlp_place()
    mlp = row * 2 + core
    greet(neighbours(group, place, [(mlp + s) % 4 for s in (1, 2, 3)]))
    width = w_ref.shape[0]
    vectors = params_ref[...].astype(F32)
    vector = lambda index: vectors[:, index * width : (index + 1) * width]
    first_gain, second_gain, down_bias = vector(6), vector(7), vector(8)
    up_bias = vectors[:, 9 * width :]
    bias_all[mlp] = jnp.broadcast_to(up_bias, bias_all.shape[1:])

    def share_bias(s, owner):
        own = bias_all.at[owner]
        return push(own, own, sems, 27 + s, {"mlp": (mlp + s) % 4})

    for s in (1, 2, 3):
        share_bias(s, mlp).start()

    half = packs.shape[2]
    lanes = 2 * HD
    quarters = step_ref[...].astype(F32)
    own_quarter = lax.broadcasted_iota(jnp.int32, quarters.shape, 1) == place
    step = jnp.sum(jnp.where(own_quarter, quarters, 0.0), axis=1, keepdims=True)
    entries = lax.broadcasted_iota(jnp.int32, (16, table.shape[0]), 1).astype(F32)
    chosen = jnp.where(entries == step, 1.0, 0.0).astype(BF16)
    embedded = jnp.dot(chosen, table[...], preferred_element_type=F32)
    gate = 1.0 / (1.0 + jnp.exp(-embedded))
    condition = embedded * gate
    modulation = jnp.dot(condition.astype(BF16), ada_ref[...], preferred_element_type=F32)
    modulation = modulation[0:1] + vectors[:, : 6 * width]
    part = lambda index: modulation[:, index * width : (index + 1) * width]
    for target, values in (
        (vec_one, (first_gain, part(1), part(0))),
        (
            vec_two,
            (part(2), second_gain, part(4), part(3), part(5), down_bias),
        ),
        (
            extra,
            (
                condition[0:1], jnp.broadcast_to(step, (1, condition.shape[1])),
                (gate * (1.0 + embedded * (1.0 - gate)))[0:1],
            ),
        ),
    ):
        target[...] = jnp.zeros_like(target)
        for index, value in enumerate(values):
            target[index : index + 1, :] = value

    near_rows = near.shape[1]
    first_half = lax.broadcasted_iota(jnp.int32, near.shape[1:], 1) % HD < HD // 2
    for index in range(far.shape[1]):
        far_cos, far_sin = far[0, index : index + 1, :], far[1, index : index + 1, :]
        start = index * near_rows
        at = slice(start % half, start % half + near_rows)
        value = far_sin * near[0] + far_cos * near[1]
        cosine[start // half, at, :] = far_cos * near[0] - far_sin * near[1]
        sine[start // half, at, :] = jnp.where(first_half, -value, value)

    tile = half // 2

    def normal(index, carry):
        at = pl.ds(pl.multiple_of(index * tile, tile), tile)
        for side in range(2):
            n, _ = normalise(x_ref[side, at, :].astype(F32))
            value = n * vec_one[0:1, :] * (1.0 + vec_one[1:2, :]) + vec_one[2:3, :]
            normed_s[side, at, :] = value.astype(BF16)
        return carry

    lax.fori_loop(0, 2, normal, 0)

    def project(low_pair, count):
        def tokens(index, carry):
            at = pl.ds(pl.multiple_of(index * tile, tile), tile)
            normed = normed_s[:, at, :].reshape(2 * tile, width)
            turn_cos = cosine[:, at, :].reshape(2 * tile, lanes)
            turn_sin = sine[:, at, :].reshape(2 * tile, lanes)
            for kind in range(3):
                start = kind * width + low_pair * lanes
                mixed = jnp.dot(
                    normed, w_ref[:, start : start + count * lanes], preferred_element_type=F32
                )
                for pair in range(count):
                    value = mixed[:, pair * lanes : (pair + 1) * lanes]
                    if kind < 2:
                        value = turn(value, turn_cos, turn_sin)
                    even, odd = exchange(value[:tile], value[tile:])
                    head = 2 * (low_pair + pair)
                    packs[head, kind, at, :] = even.astype(BF16)
                    packs[head + 1, kind, at, :] = odd.astype(BF16)
            return carry

        lax.fori_loop(0, 2, tokens, 0)

    def full(kind, head, before, after):
        sel = min(kind, 1)
        for s in range(4):
            load_values(pieces.at[sel, s], s * rows, k_s, v_s)

        def step(s, carry):
            before(s)

            def put_out(value):
                results[sel, s] = value

            def put_log(value):
                logs[sel, s] = value

            q = packed_queries(pieces[sel, s, 0])
            attend_rows(q, k_s, v_s, 4 * rows, put_out, put_log)
            after(s)
            return carry

        lax.fori_loop(0, 4, step, 0)

    project(0, 4)

    @pl.when(group == 1)
    def _():
        for s in (1, 2, 3):
            first(s).start()

    project(4, 2)

    @pl.when(group == 1)
    def _():
        for s in (1, 2, 3, 0):
            cross(s).start()

    flipped = normed_s[...].reshape(2 * half, width).T
    part_rows = width // 16
    for which in range(2):
        for y in range(2):
            for z in range(4):
                start = ((z * 2 + y) * 2 + which) * part_rows
                at = (y * 4 + z) * part_rows
                blocks[which, at : at + part_rows, :] = flipped[start : start + part_rows]
    stores = (
        pltpu.make_async_copy(packs, packs_out, own_sems.at[0]),
        pltpu.make_async_copy(blocks, blocks_out, own_sems.at[1]),
    )
    for store in stores:
        store.start()

    @pl.when(group == 1)
    def _():
        pieces[0, 0] = packs[2 * place]
        pieces[1, 0] = packs[2 * place + 1]
        for s in (1, 3, 2):
            first(s).wait_send()
            second_values(s).start()
        for s in (1, 2, 3):
            second_queries(s).start()
        for s in (1, 2, 3):
            first(s).wait_recv()

        def before(s):
            pass

        def after(s):
            @pl.when(s == 0)
            def _():
                att[2 * place] = results[0, 0]

        full(0, 2 * place, before, after)
        for s in (1, 2, 3):
            second_values(s).wait_recv()

    @pl.when(group == 0)
    def _():
        def local(head, carry):
            load_values(packs.at[head], 0, k_s, v_s)

            def put_out(value):
                att[head] = value

            def put_log(value):
                logs_own[head] = value

            attend_rows(packed_queries(packs[head, 0]), k_s, v_s, rows, put_out, put_log)
            for s in (1, 2, 3):

                @pl.when(head == 4 * s - 1)
                def _(s=s):
                    cross(s).wait_recv()
                    onward(s).start()

            return carry

        lax.fori_loop(0, heads, local, 0)
        cross(0).wait_recv()
        pieces[1, 0] = crossed[0]
        for s in (1, 2, 3):
            onward(s).wait_recv()

    def before(s):
        @pl.when((group == 1) & (s > 0))
        def _():
            second_queries(s).wait_recv()

    def after(s):
        @pl.when((group == 1) & (s == 0))
        def _():
            att[2 * place + 1] = results[1, 0]
            for other in (1, 2, 3):
                home(0, other, 2 * place).start()

        @pl.when((group == 1) & (s > 0))
        def _():
            home(1, s, 2 * place + 1).start()

        @pl.when(group == 0)
        def _():
            home(2, s, 8 + place).start()

    full(1, 0, before, after)

    @pl.when(group == 1)
    def _():
        for s in (1, 2, 3):
            second_values(s).wait_send()
            second_queries(s).wait_send()
            for kind in (0, 1):
                home(kind, s, 2 * place + kind).wait_send()
        for s in range(4):
            cross(s).wait_send()
        for s in (1, 2, 3):
            for kind in (0, 1):
                home(kind, s, 2 * ahead(s) + kind).wait_recv()
        for s in range(4):
            home(2, s, 8 + ahead(s)).wait_recv()

    @pl.when(group == 0)
    def _():
        for s in (1, 2, 3):
            onward(s).wait_send()
        for s in range(4):
            home(2, s, 8 + place).wait_send()

    for s in (1, 2, 3):
        share_bias(s, mlp).wait_send()
        share_bias(s, (mlp + 4 - s) % 4).wait_recv()
    for store in stores:
        store.wait()


def in_vmem(count):
    return [pl.BlockSpec(memory_space=pltpu.VMEM)] * count


def forward_attention(x2, weight, *rest):
    _, half, width = x2.shape
    heads, lanes = width // HD, 2 * HD
    shapes = [
        ((heads, 3, half, lanes), BF16),
        ((heads, half, lanes), BF16),
        ((2, 4, 3, half, lanes), BF16),
        ((2, 4, half, lanes), BF16),
        ((2, 4, 8, 2 * half), F32),
        ((heads, 8, 2 * half), F32),
        ((2, half, lanes), F32),
        ((2, half, lanes), F32),
        ((8, width), F32),
        ((8, width), F32),
        ((8, rest[3].shape[1]), F32),
        ((4, 8, rest[-1].shape[1] - 9 * width), F32),
        ((2, width // 2, 2 * half), BF16),
    ]
    return pl.pallas_call(
        forward_kernel,
        in_specs=in_vmem(2 + len(rest)),
        out_specs=[pl.BlockSpec(memory_space=pl.ANY)]
        + in_vmem(len(shapes) - 2)
        + [pl.BlockSpec(memory_space=pl.ANY)],
        out_shape=[jax.ShapeDtypeStruct(shape, kind) for shape, kind in shapes],
        scratch_shapes=[
            pltpu.VMEM(shapes[0][0], BF16),
            pltpu.VMEM(shapes[-1][0], BF16),
            pltpu.VMEM((4, 3, half, lanes), BF16),
            pltpu.VMEM((2, half, width), BF16),
            pltpu.VMEM((8 * half, lanes), BF16),
            pltpu.VMEM((8 * half, lanes), BF16),
            pltpu.SemaphoreType.DMA((31,)),
            pltpu.SemaphoreType.DMA((31,)),
            pltpu.SemaphoreType.DMA((2,)),
        ],
        compiler_params=pltpu.CompilerParams(
            collective_id=1, has_side_effects=True, vmem_limit_bytes=WHOLE_VMEM
        ),
        cost_estimate=pl.CostEstimate(
            flops=100_000_000_000, bytes_accessed=8_000_000, transcendentals=0
        ),
        name="forward_attention",
    )(x2, weight, *rest)


def tile_grads(q, do, k, v, log_row, delta_row):
    s = lax.dot_general(k, q, NT, preferred_element_type=F32)
    p = jnp.exp2(s * LOG_SCALE - log_row)
    dp = lax.dot_general(v, do, NT, preferred_element_type=F32)
    ds = (p * (dp - delta_row)).astype(BF16)
    dv = jnp.dot(p.astype(BF16), do, preferred_element_type=F32)
    dk = jnp.dot(ds, q, preferred_element_type=F32)
    dq = lax.dot_general(k, ds, TN, preferred_element_type=F32)
    return dq, dk, dv


def load_backward(source, do, o, base, q_s, k_s, v_s, do_s, delta_s):
    half = do.shape[0]
    unfold_into(q_s, base, source[0], 0.0)
    unfold_into(k_s, base, source[1], 0.0)
    unfold_into(v_s, base, source[2], 0.0)
    unfold_into(do_s, base, do, 0.0)
    product = (do.astype(F32) * o.astype(F32)).T
    first = jnp.sum(product[:HD], axis=0, keepdims=True)
    second = jnp.sum(product[HD:], axis=0, keepdims=True)
    delta_s[:, base : base + half] = jnp.broadcast_to(first, (8, half))
    delta_s[:, base + half : base + 2 * half] = jnp.broadcast_to(second, (8, half))


def backward_kernel(
    packs_ref, gatt_ref, att_ref, logs_ref, held_ref, pieces, results, logs, dos, back, two,
    packs, gatt, att, logs_own, near_p, near_q, staged, q_s, k_s, v_s, do_s, delta_s, dq_s, one_p, one_q,
    send_sems, recv_sems, own_sems,
):
    group = lax.axis_index("grp")
    place = lax.axis_index("seq")
    sems = (send_sems, recv_sems)
    heads = packs_ref.shape[0]
    rows = 2 * packs.shape[2]
    scale = 1.0 / math.sqrt(HD)
    ahead = lambda s: (place + s) % 4
    behind = lambda s: (place + 4 - s) % 4
    stores = (q_s, k_s, v_s, do_s, delta_s)

    def home_values(kind, s, head):
        source = staged.at[min(kind, 1), s, pl.ds(1, 2)]
        return reach(
            source, back.at[head, pl.ds(1, 2)], sems, (0, 4, 8)[kind] + s, 1, behind(s)
        )

    def home_queries(kind, s, head):
        source = staged.at[min(kind, 1), s, 0]
        return reach(source, back.at[head, 0], sems, (12, 16, 20)[kind] + s, 1, behind(s))

    greet(neighbours(group, place, [mlp_place()[2]]))
    sum_one, sum_two, sum_three, _, _, _ = sum_steps(
        held_ref, one_p, one_q, two, None, None, None, sems, 24, (near_p, near_q)
    )
    sum_one()
    held_loads = (
        pltpu.make_async_copy(
            held_ref.at[mlp_place()[0], :, pl.ds(0, 10)], near_p, own_sems.at[0]
        ),
        pltpu.make_async_copy(
            held_ref.at[:, :, pl.ds(10 + 4 * group, 4)], near_q, own_sems.at[1]
        ),
    )
    for load in held_loads:
        load.start()

    def sum_over_rows():
        for load in held_loads:
            load.wait()
        sum_two()

    def local_loads(head):
        slot = head % 2
        return [
            pltpu.make_async_copy(source.at[head], target.at[slot], own_sems.at[2 + 4 * slot + n])
            for n, (source, target) in enumerate(
                ((packs_ref, packs), (gatt_ref, gatt), (att_ref, att), (logs_ref, logs_own))
            )
        ]

    def full(sel, put_values, put_queries):
        for s in range(4):
            load_backward(
                pieces.at[sel, s], dos[sel, s], results[sel, s], s * rows, *stores
            )

        def step(turn_index, last):
            s = 0 if last else (turn_index + 1) % 4
            block = pl.ds(0 if last else pl.multiple_of(s * rows, rows), rows)
            k = k_s[block, :]
            v = v_s[block, :]
            dk = dv = None
            for index in (1, 2, 3, 0):
                chunk = slice(index * rows, (index + 1) * rows)
                dq, dk_part, dv_part = tile_grads(
                    q_s[chunk, :], do_s[chunk, :], k, v, logs[sel, index, 0:1, :],
                    delta_s[0:1, chunk],
                )
                dk = dk_part if dk is None else dk + dk_part
                dv = dv_part if dv is None else dv + dv_part
                if last:
                    dq = dq_s[:, chunk] + dq
                    staged[sel, index, 0] = fold(dq.T * scale).astype(BF16)
                    put_queries(index)
                else:
                    dq_s[:, chunk] = jnp.where(turn_index == 0, dq, dq_s[:, chunk] + dq)
            staged[sel, s, 1] = fold(dk * scale).astype(BF16)
            staged[sel, s, 2] = fold(dv).astype(BF16)
            put_values(s)

        def one_turn(turn_index, carry):
            step(turn_index, False)
            return carry

        if sel:
            lax.fori_loop(0, 3, one_turn, 0)
            step(3, True)
        else:
            lax.fori_loop(0, 4, one_turn, 0)
            for index in (1, 2, 3, 0):
                chunk = slice(index * rows, (index + 1) * rows)
                staged[sel, index, 0] = fold(dq_s[:, chunk].T * scale).astype(BF16)
                put_queries(index)

    @pl.when(group == 1)
    def _():
        head = 2 * place

        def put_values(s):
            @pl.when(s == 0)
            def _():
                back[head, 1] = staged[0, 0, 1]
                back[head, 2] = staged[0, 0, 2]

            @pl.when(s > 0)
            def _():
                home_values(0, s, head).start()

            @pl.when(s == 0)
            def _():
                sum_over_rows()

        def put_queries(s):
            if s == 0:
                back[head, 0] = staged[0, 0, 0]
            else:
                home_queries(0, s, head).start()

        full(0, put_values, put_queries)

    def put_values(s):
        head = 2 * place + 1

        @pl.when((group == 1) & (s == 0))
        def _():
            back[head, 1] = staged[1, 0, 1]
            back[head, 2] = staged[1, 0, 2]

        @pl.when((group == 1) & (s > 0))
        def _():
            home_values(1, s, head).start()

        @pl.when(group == 0)
        def _():
            home_values(2, s, 8 + place).start()

        @pl.when((group == 0) & (s == 3))
        def _():
            sum_over_rows()

    def put_queries(s):
        if s:
            head = group * (2 * place + 1) + (1 - group) * (8 + place)
            reach(
                staged.at[1, s, 0], back.at[head, 0], sems, 20 - 4 * group + s, 1, behind(s)
            ).start()
            return

        @pl.when(group == 1)
        def _():
            back[2 * place + 1, 0] = staged[1, 0, 0]

        @pl.when(group == 0)
        def _():
            home_queries(2, 0, 8 + place).start()

    full(1, put_values, put_queries)

    @pl.when(group == 0)
    def _():
        for load in local_loads(0):
            load.start()

        def local(head, carry):
            @pl.when(head + 1 < heads)
            def _():
                for load in local_loads(head + 1):
                    load.start()

            for load in local_loads(head):
                load.wait()
            slot = head % 2
            load_backward(packs.at[slot], gatt[slot], att[slot], 0, *stores)
            own = slice(0, rows)
            dq, dk, dv = tile_grads(
                q_s[own, :], do_s[own, :], k_s[own, :], v_s[own, :],
                logs_own[slot, 0:1, :], delta_s[0:1, own],
            )
            back[head, 0] = fold(dq.T * scale).astype(BF16)
            back[head, 1] = fold(dk * scale).astype(BF16)
            back[head, 2] = fold(dv).astype(BF16)
            return carry

        lax.fori_loop(0, heads, local, 0)

    sum_three()

    @pl.when(group == 0)
    def _():
        for s in range(4):
            home_values(2, s, 8 + place).wait_send()
            home_queries(2, s, 8 + place).wait_send()

    @pl.when(group == 1)
    def _():
        for s in (1, 2, 3):
            for kind in (0, 1):
                home_values(kind, s, 2 * place + kind).wait_send()
                home_queries(kind, s, 2 * place + kind).wait_send()
        for s in (1, 2, 3):
            for kind in (0, 1):
                home_values(kind, s, 2 * ahead(s) + kind).wait_recv()
                home_queries(kind, s, 2 * ahead(s) + kind).wait_recv()
        for s in range(4):
            home_values(2, s, 8 + ahead(s)).wait_recv()
            home_queries(2, s, 8 + ahead(s)).wait_recv()


def backward_attention(packs, gatt, att, pieces, results, logs, logs_own, dos, held):
    heads, _, half, lanes = packs.shape
    share = held.shape[2:]
    return pl.pallas_call(
        backward_kernel,
        in_specs=[pl.BlockSpec(memory_space=pl.ANY)] * 5 + in_vmem(4),
        out_specs=in_vmem(2),
        out_shape=[
            jax.ShapeDtypeStruct((heads, 3, half, lanes), BF16),
            jax.ShapeDtypeStruct((4, 9) + share[1:], BF16),
        ],
        scratch_shapes=[
            pltpu.VMEM((2,) + value.shape[1:], value.dtype)
            for value in (packs, gatt, att, logs_own)
        ]
        + sum_scratch(share[1], EARLY)
        + [pltpu.VMEM((2, 4, 3, half, lanes), BF16)]
        + [pltpu.VMEM((8 * half, lanes), BF16)] * 4
        + [pltpu.VMEM((8, 8 * half), F32), pltpu.VMEM((lanes, 8 * half), F32)]
        + sum_scratch(share[1], EARLY)
        + [pltpu.SemaphoreType.DMA((28,))] * 2
        + [pltpu.SemaphoreType.DMA((10,))],
        compiler_params=pltpu.CompilerParams(
            collective_id=2, has_side_effects=True, vmem_limit_bytes=WHOLE_VMEM
        ),
        cost_estimate=pl.CostEstimate(
            flops=120_000_000_000, bytes_accessed=8_000_000, transcendentals=0
        ),
        name="backward_attention",
    )(packs, gatt, att, logs_own, held, pieces, results, logs, dos)


def whole(shape):
    zeros = (0,) * len(shape)
    return pl.BlockSpec(shape, lambda *_: zeros)


def middle_kernel(
    x_ref, cot_ref, att_ref, vec_ref, ow_ref, up_ref, down_ref, bias_ref,
    out_ref, attlow_ref, hidden_ref, act_ref, gfeed_ref, gpre_ref, mgrad_ref, gbranch_ref,
    gatt_ref, sums_ref, upsum_ref, att_s, slope_s,
):
    step = pl.program_id(0)
    rows, width = x_ref.shape[1:]
    both = 2 * rows
    pairs = width // (2 * HD)
    gate_one, gain, scale, shift = (vec_ref[i : i + 1, :] for i in range(4))
    gate_two, down_bias = vec_ref[4:5, :], vec_ref[5:6, :]
    for pair in range(pairs):
        lanes = slice(pair * 2 * HD, (pair + 1) * 2 * HD)
        top, bottom = exchange(
            att_ref[2 * pair].astype(F32), att_ref[2 * pair + 1].astype(F32)
        )
        att_s[:rows, lanes] = top.astype(BF16)
        att_s[rows:, lanes] = bottom.astype(BF16)
    att = att_s[...]
    attlow_ref[...] = att.reshape(2, rows, width)
    branch = jnp.dot(att, ow_ref[...], preferred_element_type=F32)
    middle = x_ref[...].reshape(both, width).astype(F32) + gate_one * branch
    n, inverse = normalise(middle)
    hidden = (n * gain * (1.0 + scale) + shift).astype(BF16)
    hidden_ref[...] = hidden.reshape(2, rows, width)
    shares, _, chunk = up_ref.shape
    feed = None
    following = jnp.dot(hidden, up_ref[0], preferred_element_type=F32)
    for index in range(shares):
        cols = slice(index * chunk, (index + 1) * chunk)
        pre = following + bias_ref[index, 0:1]
        if index + 1 < shares:
            following = jnp.dot(hidden, up_ref[index + 1], preferred_element_type=F32)
        square = pre * pre
        root = math.sqrt(2.0 / math.pi)
        tanh = jnp.tanh(pre * (root + (root * 0.044715) * square))
        half_up = 0.5 + 0.5 * tanh
        act = (pre * half_up).astype(BF16)
        slope_s[:, cols] = half_up + (0.5 * pre) * (1.0 - tanh * tanh) * (
            root + (3.0 * root * 0.044715) * square
        )
        act_ref[:, :, cols] = act.reshape(2, rows, chunk)
        part = jnp.dot(act, down_ref[index], preferred_element_type=F32)
        feed = part if feed is None else feed + part
    feed = feed + down_bias
    out_ref[...] = (middle + gate_two * feed).astype(BF16).reshape(2, rows, width)
    cot = cot_ref[...].reshape(both, width).astype(F32)
    gfeed = (gate_two * cot).astype(BF16)
    gfeed_ref[...] = gfeed.reshape(2, rows, width)
    ghidden = None
    up_sums = []
    for index in range(shares):
        cols = slice(index * chunk, (index + 1) * chunk)
        gact = lax.dot_general(gfeed, down_ref[index], NT, preferred_element_type=F32)
        gpre = (gact * slope_s[:, cols]).astype(BF16)
        gpre_ref[:, :, cols] = gpre.reshape(2, rows, chunk)
        up_sums.append(jnp.sum(gpre.astype(F32), axis=0, keepdims=True))
        part = lax.dot_general(gpre, up_ref[index], NT, preferred_element_type=F32)
        ghidden = part if ghidden is None else ghidden + part
    e = ghidden * ((1.0 + scale) * gain)
    mgrad = cot + inverse * (
        e - jnp.mean(e, axis=-1, keepdims=True) - n * jnp.mean(e * n, axis=-1, keepdims=True)
    )
    mgrad_ref[...] = mgrad.reshape(2, rows, width)
    gbranch = (gate_one * mgrad).astype(BF16)
    gbranch_ref[...] = gbranch.reshape(2, rows, width)
    gatt = lax.dot_general(gbranch, ow_ref[...], NT, preferred_element_type=F32)
    for pair in range(pairs):
        value = gatt[:, pair * 2 * HD : (pair + 1) * 2 * HD]
        even, odd = exchange(value[:rows], value[rows:])
        gatt_ref[2 * pair] = even.astype(BF16)
        gatt_ref[2 * pair + 1] = odd.astype(BF16)
    add = lambda value: jnp.sum(value, axis=0, keepdims=True)

    @pl.when(step == 0)
    def _():
        sums_ref[...] = jnp.zeros_like(sums_ref)
        upsum_ref[...] = jnp.zeros_like(upsum_ref)

    sums_ref[0:1, :] += add(ghidden)
    sums_ref[1:2, :] += add(ghidden * n)
    sums_ref[2:3, :] += add(cot * feed)
    sums_ref[3:4, :] += add(gfeed.astype(F32))
    sums_ref[4:5, :] += add(mgrad * branch)
    for index, value in enumerate(up_sums):
        upsum_ref[0:1, index * chunk : (index + 1) * chunk] += value


def once(shape):
    zeros = (0,) * len(shape)
    return pl.BlockSpec(shape, lambda *_: zeros, pipeline_mode=pl.Buffered(1))


def middle_pass(x2, cot2, att, vecs, out_weight, up_all, down_all, bias_all, rows=128):
    half, width = x2.shape[1:]
    heads = width // HD
    units = up_all.shape[0] * up_all.shape[2]
    tok = lambda last: pl.BlockSpec((2, rows, last), lambda i: (0, i, 0))
    pack = pl.BlockSpec((heads, rows, 2 * HD), lambda i: (0, i, 0))
    token = lambda last, kind: jax.ShapeDtypeStruct((2, half, last), kind)
    return pl.pallas_call(
        middle_kernel,
        grid=(half // rows,),
        in_specs=[
            tok(width), tok(width), pack, whole(vecs.shape), once(out_weight.shape),
            once(up_all.shape), once(down_all.shape), once(bias_all.shape),
        ],
        out_specs=[
            tok(width), tok(width), tok(width), tok(units), tok(width), tok(units), tok(width),
            tok(width), pack, whole((8, width)), whole((8, units)),
        ],
        out_shape=[
            token(width, BF16), token(width, BF16), token(width, BF16), token(units, BF16),
            token(width, BF16), token(units, BF16), token(width, F32), token(width, BF16),
            jax.ShapeDtypeStruct((heads, half, 2 * HD), BF16),
            jax.ShapeDtypeStruct((8, width), F32),
            jax.ShapeDtypeStruct((8, units), F32),
        ],
        scratch_shapes=[pltpu.VMEM((2 * rows, width), BF16), pltpu.VMEM((2 * rows, units), F32)],
        compiler_params=params("arbitrary"),
        name="middle_pass",
    )(x2, cot2, att, vecs, out_weight, up_all, down_all, bias_all)


def feed_grads_kernel(
    hidden_ref, gfeed_ref, att_ref, gbranch_ref, act_ref, gpre_ref, gatt, held, dos,
    hidden_s, gfeed_s, att_s, act_s, gpre_s, sent, got, crossed, send_sems, recv_sems, own_sems,
):
    group = lax.axis_index("grp")
    place = lax.axis_index("seq")
    _, core, _, other_core = mlp_place()
    sems = (send_sems, recv_sems)
    ahead = lambda s: (place + s) % 4

    def first(s):
        return reach(gatt.at[2 * ahead(s)], dos.at[0, s], sems, s - 1, 1, ahead(s))

    def second(s):
        return reach(gatt.at[2 * ahead(s) + 1], dos.at[1, s], sems, 2 + s, 1, ahead(s))

    def cross(s):
        return reach(gatt.at[8 + ahead(s)], crossed.at[s], sems, 6 + s, 0, place)

    def onward(s):
        return reach(crossed.at[s], dos.at[1, s], sems, 9 + s, 0, ahead(s))

    def swap(y):
        return push(sent.at[y], got.at[y], sems, 13 + y, {"mlp": other_core})

    width = hidden_s.shape[0]

    def loads(order, index):
        cols = pl.ds(pl.multiple_of(index * width, width), width)
        return (
            pltpu.make_async_copy(gpre_ref.at[:, cols], gpre_s.at[order], own_sems.at[0, order]),
            pltpu.make_async_copy(act_ref.at[:, cols], act_s.at[order], own_sems.at[1, order]),
        )

    for y in range(2):
        for load in loads(y, 2 * y + 1 - core):
            load.start()
    for y in range(2):
        for load in loads(2 + y, 2 * y + core):
            load.start()
    greet(neighbours(group, place, [other_core]))

    @pl.when(group == 1)
    def _():
        for s in (1, 2, 3):
            cross(s).start()
            first(s).start()
            second(s).start()
        cross(0).start()
        dos[0, 0] = gatt[2 * place]
        dos[1, 0] = gatt[2 * place + 1]

    hidden_s[...] = hidden_ref[...].T
    gfeed_s[...] = gfeed_ref[...].T
    att_s[...] = att_ref[...].T
    split = width // 4
    part = split // 4
    rows = 3 * part

    def blocks(target, y, index, order):
        for load in loads(order, index):
            load.wait()
        up = jnp.dot(hidden_s[...], gpre_s[order], preferred_element_type=F32).astype(BF16)
        down = jnp.dot(gfeed_s[...], act_s[order], preferred_element_type=F32).astype(BF16)
        own = jnp.concatenate(
            [
                att_s[pl.ds(pl.multiple_of(index * part + z * split, 16), part), :]
                for z in range(4)
            ]
        )
        out = jnp.dot(own, gbranch_ref[...], preferred_element_type=F32).astype(BF16)
        for z in range(4):
            start = z * split
            pieces = (
                (up[start : start + rows],),
                (up[start + rows : start + split], down[start : start + split - rows + part]),
                (down[start + 2 * part : start + split], out[z * part : (z + 1) * part]),
            )
            for number, values in enumerate(pieces):
                base = 0
                for value in values:
                    size = value.shape[0]
                    for lane in range(width // (2 * HD)):
                        target[y, z, number * 6 + lane, base : base + size, :] = value[
                            :, lane * 2 * HD : (lane + 1) * 2 * HD
                        ]
                    base += size

    def send_row(y, carry):
        blocks(sent, y, 2 * y + 1 - core, y)
        swap(y).start()
        return carry

    lax.fori_loop(0, 2, send_row, 0)

    @pl.when(group == 0)
    def _():
        for s in (1, 2, 3):
            cross(s).wait_recv()
            onward(s).start()
        cross(0).wait_recv()
        dos[1, 0] = crossed[0]

    def keep_row(y, carry):
        blocks(held, y, 2 * y + core, 2 + y)
        return carry

    lax.fori_loop(0, 2, keep_row, 0)

    def add_row(y, carry):
        swap(y).wait()

        def add(z, inner):
            held[y, z] = added(held[y, z], got[y, z])
            return inner

        return lax.fori_loop(0, 4, add, carry)

    lax.fori_loop(0, 2, add_row, 0)

    @pl.when(group == 1)
    def _():
        for s in (1, 2, 3):
            first(s).wait()
            second(s).wait()
        for s in range(4):
            cross(s).wait_send()

    @pl.when(group == 0)
    def _():
        for s in (1, 2, 3):
            onward(s).wait()


def feed_grads(hidden, gfeed, att, gbranch, act, gpre, gatt):
    tokens, width = hidden.shape
    _, half, lanes = gatt.shape
    rows = 3 * width // 16
    share = (2, 4, BLOCKS, rows, lanes)
    return pl.pallas_call(
        feed_grads_kernel,
        in_specs=in_vmem(4) + [pl.BlockSpec(memory_space=pl.ANY)] * 2 + in_vmem(1),
        out_specs=in_vmem(2),
        out_shape=[
            jax.ShapeDtypeStruct(share, BF16),
            jax.ShapeDtypeStruct((2, 4, half, lanes), BF16),
        ],
        scratch_shapes=[pltpu.VMEM((width, tokens), BF16)] * 3
        + [pltpu.VMEM((4, tokens, width), BF16)] * 2
        + [
            pltpu.VMEM(share, BF16),
            pltpu.VMEM(share, BF16),
            pltpu.VMEM((4, half, lanes), BF16),
            pltpu.SemaphoreType.DMA((15,)),
            pltpu.SemaphoreType.DMA((15,)),
            pltpu.SemaphoreType.DMA((2, 4)),
        ],
        compiler_params=pltpu.CompilerParams(
            collective_id=3, has_side_effects=True, vmem_limit_bytes=WHOLE_VMEM
        ),
        cost_estimate=pl.CostEstimate(
            flops=24_000_000_000, bytes_accessed=20_000_000, transcendentals=0
        ),
        name="feed_grads",
    )(hidden, gfeed, att, gbranch, act, gpre, gatt)


SMALL_ROWS = 40


def finish_kernel(
    packs, cosine, sine, normed_ref, vec_one, vec_two, middle_sums, up_sums, extra, feed_two,
    w_ref, x_ref, mgrad_ref, ada_ref,
    qkv_out, up_out, down_out, out_out, sums_out, ada_out, table_out, grad_ref,
    total, feed_total, rows_all, mixed, w_s, x_s, mgrad_s, ada_s, sums, small, sent, got, held, one_p, one_q, two, others,
    three, feed_others, feed_three, send_sems, recv_sems, own_sems,
):
    group = lax.axis_index("grp")
    place = lax.axis_index("seq")
    row, core, _, other_core = mlp_place()
    mlp = row * 2 + core
    sems = (send_sems, recv_sems)
    ahead = lambda s: (place + s) % 4
    heads = packs.shape[0]
    half = packs.shape[2]
    width = heads * HD
    lanes = 2 * HD
    parts = 3
    each = BLOCKS // parts

    loads = [
        pltpu.make_async_copy(source, target, own_sems.at[index])
        for index, (source, target) in enumerate(
            ((w_ref, w_s), (x_ref, x_s), (mgrad_ref, mgrad_s), (ada_ref, ada_s))
        )
    ]
    for load in loads:
        load.start()
    greet(
        [{"seq": ahead(s)} for s in (1, 2, 3)]
        + [{"mlp": (mlp + s) % 4} for s in (1, 2, 3)]
        + [{"grp": 1 - group}]
    )
    _, _, _, feed_over, feed_four, feed_five = sum_steps(
        None, None, None, feed_two, feed_others, feed_three, feed_total, sems, 0
    )
    sum_one, sum_two, sum_three, sum_over, sum_four, sum_five = sum_steps(
        held, one_p, one_q, two, others, three, total, sems, 9
    )
    feed_over()

    def swap(index):
        own = pl.ds(index * each, each)
        return push(
            sent.at[:, :, own], got.at[:, :, own], sems, 18 + index, {"mlp": other_core}
        )

    def unrotate(part):
        def one_pair(pair, carry):
            top, bottom = exchange(
                packs[2 * pair, part].astype(F32), packs[2 * pair + 1, part].astype(F32)
            )
            if part < 2:
                top = turn(top, cosine[0], -sine[0])
                bottom = turn(bottom, cosine[1], -sine[1])
            cols = pl.ds(pl.multiple_of(part * width + pair * lanes, lanes), lanes)
            mixed[:half, cols] = top.astype(BF16)
            mixed[half:, cols] = bottom.astype(BF16)
            return carry

        lax.fori_loop(0, heads // 2, one_pair, 0)

    def blocks(target, which, index):
        value = jnp.dot(
            normed_ref[which], mixed[:, index * width : (index + 1) * width],
            preferred_element_type=F32,
        ).astype(BF16)
        for lane in range(each):
            target[:, :, index * each + lane] = value[
                :, lane * lanes : (lane + 1) * lanes
            ].reshape(2, 4, width // 16, lanes)

    for index in (2, 0, 1):
        unrotate(index)
        blocks(sent, 1 - core, index)
        swap(index).start()
    for index in range(parts):
        blocks(held, core, index)
    for index in range(parts):
        swap(index).wait()
    for y in range(2):

        def add(z, carry, y=y):
            held[y, z] = added(held[y, z], got[y, z])
            return carry

        lax.fori_loop(0, 4, add, 0)
    sum_one()
    for load in loads:
        load.wait()
    chunk = half // 2
    sums[...] = jnp.zeros_like(sums)

    def store(index):
        own = pl.ds(index * chunk, chunk)
        return pltpu.make_async_copy(mgrad_s.at[own], grad_ref.at[own], own_sems.at[4 + index])

    for index in range(4):
        own = slice(index * chunk, (index + 1) * chunk)
        gnormed = lax.dot_general(mixed[own, :], w_s[...], NT, preferred_element_type=F32)
        n, inverse = normalise(x_s[own, :].astype(F32))
        e = gnormed * ((1.0 + vec_one[1:2, :]) * vec_one[0:1, :])
        mgrad_s[own, :] = mgrad_s[own, :] + inverse * (
            e - jnp.mean(e, axis=-1, keepdims=True) - n * jnp.mean(e * n, axis=-1, keepdims=True)
        )
        store(index).start()
        sums[0:1, :] += jnp.sum(gnormed, axis=0, keepdims=True)
        sums[1:2, :] += jnp.sum(gnormed * n, axis=0, keepdims=True)
        if index == 2:
            sum_two()

    first_sum, second_sum = sums[1:2, :], middle_sums[1:2, :]
    mod = [
        sums[0:1, :], vec_one[0:1, :] * first_sum, middle_sums[4:5, :], middle_sums[0:1, :],
        vec_two[1:2, :] * second_sum, middle_sums[2:3, :],
    ]
    wholes = [
        (1.0 + vec_one[1:2, :]) * first_sum, (1.0 + vec_two[2:3, :]) * second_sum,
        middle_sums[3:4, :],
    ]
    weighted = None
    for index, value in enumerate(mod):
        part = jnp.sum(
            ada_s[:, index * width : (index + 1) * width].astype(F32) * value, axis=1,
            keepdims=True,
        )
        weighted = part if weighted is None else weighted + part
    table_row = jnp.broadcast_to(weighted, (lanes, lanes)).T[0:1] * extra[2:3, :]
    tiles = width // lanes
    for z in range(4):
        for line in range(9):
            tile = 9 * z + line
            value = mod[tile // tiles]
            start = (tile % tiles) * lanes
            small[z, line : line + 1, :] = value[:, start : start + lanes]
        for line in range(tiles):
            start = z * width + line * lanes
            small[z, 9 + line : 10 + line, :] = up_sums[0:1, start : start + lanes]
            for index, value in enumerate(wholes):
                at = 15 + index * tiles + line
                small[z, at : at + 1, :] = value[:, line * lanes : (line + 1) * lanes]
        small[z, 33:34, :] = table_row
        small[z, 34:36, :] = extra[0:2, :]
        small[z, 36:40, :] = jnp.zeros((4, lanes), F32)

    def hop_place(s):
        return push(
            small.at[ahead(s)], rows_all.at[group, mlp, place], sems, 20 + s, {"seq": ahead(s)}
        )

    def hop_place_in(s):
        return push(
            small.at[ahead(s)], rows_all.at[group, mlp, ahead(4 - s)], sems, 20 + s,
            {"seq": ahead(s)},
        )

    def hop_mlp(s, from_place):
        own = rows_all.at[group, from_place]
        return push(own, own, sems, 23 + s, {"mlp": (mlp + s) % 4})

    def hop_group(from_group):
        own = rows_all.at[from_group]
        return push(own, own, sems, 27, {"grp": 1 - group})

    for s in (1, 2, 3):
        hop_place(s).start()
    rows_all[group, mlp, place] = small[place]
    sum_three()
    sum_over()
    feed_four()
    for s in (1, 2, 3):
        hop_place_in(s).wait()
    for s in (1, 2, 3):
        hop_mlp(s, mlp).start()
    sum_four()
    for s in (1, 2, 3):
        hop_mlp(s, mlp).wait_send()
        hop_mlp(s, (mlp + 4 - s) % 4).wait_recv()
    hop_group(group).start()
    feed_five()
    share_rows = feed_total.shape[1]
    part_rows = share_rows // 3
    for lane in range(tiles):
        at = slice(lane * lanes, (lane + 1) * lanes)
        one, two_, three_ = (feed_total[6 * index + lane].astype(F32) for index in range(3))
        up_out[:share_rows, at] = one
        up_out[share_rows:, at] = two_[:part_rows]
        down_out[: 2 * part_rows, at] = two_[part_rows:]
        down_out[2 * part_rows :, at] = three_[: 2 * part_rows]
        out_out[:, at] = three_[2 * part_rows :]
    sum_five()
    for block in range(BLOCKS):
        qkv_out[:, block * lanes : (block + 1) * lanes] = total[block].astype(F32)
    hop_group(group).wait_send()
    hop_group(1 - group).wait_recv()
    every = rows_all[...].reshape(32, SMALL_ROWS, lanes)
    sums_out[...] = jnp.sum(every, axis=0)
    conditions = every[:, 34].astype(BF16).astype(F32)
    for line in range(9):
        ada_out[:, line * lanes : (line + 1) * lanes] = lax.dot_general(
            conditions, every[:, line], TN, precision=highest, preferred_element_type=F32
        )
    table_rows = table_out.shape[0]
    first_row = (place * 4 + mlp) * table_rows
    owned = first_row + lax.broadcasted_iota(jnp.int32, (table_rows, 32), 0)
    steps = every[:, 35].T[:table_rows]
    chosen = jnp.where(owned.astype(F32) == steps, 1.0, 0.0)
    table_out[...] = jnp.dot(chosen, every[:, 33], precision=highest, preferred_element_type=F32)
    for index in range(4):
        store(index).wait()


def finish(
    packs, cosine, sine, normed, vec_one, vec_two, middle_sums, up_sums, extra, feed_two, weight,
    x, mgrad, ada_weight, table_rows,
):
    rows = normed.shape[1] // 8
    lanes = 2 * HD
    share = (2, 4, BLOCKS, rows, lanes)
    feed_rows = feed_two.shape[2]
    tokens, width = x.shape
    like = lambda value: pltpu.VMEM(value.shape, value.dtype)
    apart = pl.BlockSpec(memory_space=pl.ANY)
    return pl.pallas_call(
        finish_kernel,
        in_specs=in_vmem(10) + [apart] * 4,
        out_specs=in_vmem(7) + [apart],
        out_shape=[
            jax.ShapeDtypeStruct(shape, F32)
            for shape in (
                (width // 16, 3 * width), (width // 4, width), (width // 4, width),
                (width // 16, width), (SMALL_ROWS, lanes), (lanes, 9 * lanes),
                (table_rows, lanes), (tokens, width),
            )
        ],
        scratch_shapes=[
            pltpu.VMEM(share[2:], BF16), pltpu.VMEM((BLOCKS, feed_rows, lanes), BF16),
            pltpu.VMEM((2, 4, 4, SMALL_ROWS, lanes), F32),
            pltpu.VMEM((tokens, 3 * width), BF16), like(weight), like(x), like(mgrad),
            like(ada_weight), pltpu.VMEM((8, width), F32), pltpu.VMEM((4, SMALL_ROWS, lanes), F32),
        ]
        + [pltpu.VMEM(share, BF16)] * 3
        + sum_scratch(rows, EARLY + MIDDLE + LATE)
        + sum_scratch(feed_rows, LATE)
        + [pltpu.SemaphoreType.DMA((28,))] * 2
        + [pltpu.SemaphoreType.DMA((8,))],
        compiler_params=pltpu.CompilerParams(
            collective_id=4, has_side_effects=True, vmem_limit_bytes=WHOLE_VMEM
        ),
        cost_estimate=pl.CostEstimate(
            flops=60_000_000_000, bytes_accessed=20_000_000, transcendentals=0
        ),
        name="finish",
    )(
        packs, cosine, sine, normed, vec_one, vec_two, middle_sums, up_sums, extra, feed_two,
        weight, x, mgrad, ada_weight,
    )


def four_shards(
    tokens, step_index, time_table, ada_weight, ada_bias, first_gain, qkv_weight, out_weight,
    second_gain, up_weight, up_bias, down_weight, down_bias, cotangent,
):
    place = lax.axis_index("seq")
    group = lax.axis_index("grp")
    mlp_count = lax.axis_size("mlp")
    token_rows, width = tokens.shape[1:]
    half = token_rows // 2
    lanes = 2 * HD
    up_all = lax.all_gather(up_weight, "mlp", axis=0)
    down_all = lax.all_gather(down_weight, "mlp", axis=0)

    frequency = jnp.exp(jnp.arange(HD // 2, dtype=F32) * (-2.0 * math.log(10000.0) / HD))
    frequency = jnp.concatenate([frequency] * 4)[None, :]
    near_rows = 32
    offset = jnp.where(group == 1, place * token_rows, 0)
    far_rows = offset + near_rows * jnp.arange(token_rows // near_rows, dtype=jnp.int32)

    def circle(positions):
        angles = positions.astype(F32)[:, None] * frequency
        return jnp.stack([jnp.cos(angles), jnp.sin(angles)])

    x2 = tokens.reshape(2, half, width)
    parameters = jnp.concatenate([ada_bias, first_gain, second_gain, down_bias, up_bias])[None, :]
    (
        packs, att, pieces, results, logs, logs_own, cosine, sine, vec_one, vec_two, extra,
        bias_all, blocks,
    ) = forward_attention(
        x2, qkv_weight, circle(jnp.arange(near_rows, dtype=jnp.int32)), circle(far_rows),
        step_index, time_table, ada_weight, parameters,
    )

    (
        output, att_low, hidden, act, grad_feed, grad_pre, middle_grad, grad_branch, grad_att,
        middle_sums, up_sums,
    ) = middle_pass(
        x2, cotangent.reshape(2, half, width), att, vec_two, out_weight, up_all, down_all,
        bias_all,
    )
    flat = lambda value: value.reshape(token_rows, value.shape[2])
    feed_held, att_grads = feed_grads(
        *(flat(value) for value in (hidden, grad_feed, att_low, grad_branch, act, grad_pre)),
        grad_att,
    )
    grads, feed_two = backward_attention(
        packs, grad_att, att, pieces, results, logs, logs_own, att_grads, feed_held
    )
    ranks = 4 * mlp_count
    (
        qkv_total, up_total, down_total, out_total, row_sums, ada_rows, table_share, input_grad,
    ) = finish(
        grads, cosine, sine, blocks, vec_one, vec_two, middle_sums, up_sums, extra, feed_two,
        qkv_weight, flat(x2), flat(middle_grad), ada_weight, time_table.shape[0] // ranks,
    )
    mlp = lax.axis_index("mlp")
    rank = place * mlp_count + mlp

    def share(value, index, count):
        each = value.shape[-1] // count
        return lax.dynamic_slice_in_dim(value, index * each, each, value.ndim - 1)

    mod_sums, up_bias_sums, first_sums, second_sums, down_bias_sums = (
        row_sums[start:end].reshape(-1)
        for start, end in ((0, 9), (9, 15), (15, 21), (21, 27), (27, 33))
    )
    return (
        output.reshape(1, token_rows, width),
        input_grad.reshape(1, token_rows, width),
        table_share,
        share(ada_rows, mlp, mlp_count),
        share(mod_sums, mlp, mlp_count),
        share(first_sums, rank, ranks),
        qkv_total,
        out_total,
        share(second_sums, rank, ranks),
        up_total,
        share(up_bias_sums, mlp, mlp_count),
        down_total.T,
        share(down_bias_sums, rank, ranks),
    )


def solution(mesh):
    in_specs = (
        P(("grp", "mlp"), "seq", None),
        P(("grp", "mlp"), None),
        P(),
        P(),
        P(),
        P(),
        P(),
        P(),
        P(),
        P(None, "mlp"),
        P("mlp"),
        P("mlp", None),
        P(),
        P(("grp", "mlp"), "seq", None),
    )
    out_specs = (
        P(("grp", "mlp"), "seq", None),
        P(("grp", "mlp"), "seq", None),
        P(("seq", "mlp"), None),
        P(None, ("seq", "mlp")),
        P(("seq", "mlp")),
        P(("seq", "mlp")),
        P(("seq", "mlp"), None),
        P(("seq", "mlp"), None),
        P(("seq", "mlp")),
        P("seq", "mlp"),
        P(("seq", "mlp")),
        P("mlp", "seq"),
        P(("seq", "mlp")),
    )
    body = four_shards if mesh.shape["seq"] == 4 and mesh.shape["grp"] == 2 else shards
    return jax.shard_map(body, mesh=mesh, in_specs=in_specs, out_specs=out_specs, check_vma=False)
```
